128 devices in a mesh: pre: 8 (over y, core), dec: 16 (over x, z).
Axes of the slice: x: 4, y: 4, z: 4, core: 2. Of those that a mesh axis runs over, the one named last changes fastest.
Arguments:
- latent_cache: bfloat16 [64, 8192, 576], P(None, ('dec', 'pre')), may hold values from -29 to 29
- query: bfloat16 [64, 128, 576], P(None, 'dec'), may hold values from -4.5 to 4.5
- new_latent: bfloat16 [64, 576], replicated, may hold values from -9 to 9
- lengths: int32 [64], replicated, may hold values from 1 to 8192, 262144 in all
- slot_of: int32 [64], replicated, may hold values from 0 to 63, each once
- token_ids: int32 [64], replicated, may hold values from 0 to 129279
- latent_value_weight: bfloat16 [128, 512, 128], P('dec'), may hold values from -2 to 2
- out_weight: bfloat16 [16384, 7168], P('dec', 'pre'), may hold values from -0.046875 to 0.046875
- residual: bfloat16 [64, 7168], P(None, 'pre'), may hold values from -24 to 24
- norm_gain: bfloat16 [7168], P('pre'), may hold values from 0.5 to 1.5
- lm_weight: bfloat16 [7168, 129280], P('pre', 'dec'), may hold values from -6 to 6
Outputs:
- logprobs: float32 [64, 129280], P('pre', 'dec')
- target_logprob: float32 [64], P('pre')
The draws below stay inside these ranges and needn't reach their ends.
Inputs may be any that keep to these rules, and one draw needn't show every extreme that they name: `slot_of`: each slot holds exactly one request.
All inputs are finite; a program needn't handle non-finite values.
Results may differ from the reference program's by a relative error of at most 0.0075.
Values may be sent and summed in bfloat16 or wider, within the bound.
A program may use at most 128 MiB of HBM per device.

```python
import math
import jax
import jax.numpy as jnp
import numpy as np
from jax import lax

H = 128
KV_RANK = 512
ROPE = 64
VHEAD = 128
D = 7168
VOCAB = 129280
CTX = 8192
REQUESTS = 64


def query_base(key):
    return jnp.clip(jax.random.normal(jax.random.fold_in(key, 11), (REQUESTS, H, KV_RANK + ROPE), jnp.float32), -4.5, 4.5)


def draw_query(key, part):
    base = query_base(key)
    return base.astype(jnp.bfloat16)


def draw_latent_cache(key, part):
    key = jax.random.fold_in(key, 5)
    cache = jnp.clip(jax.random.normal(key, (REQUESTS, CTX, KV_RANK + ROPE), jnp.float32), -4.5, 4.5)
    return cache.astype(jnp.bfloat16)


def draw_residual(key, part):
    key = jax.random.fold_in(key, 7)
    first_key, second_key, third_key = jax.random.split(key, 3)
    row_scale = jnp.exp(jax.random.uniform(second_key, (REQUESTS, 1), jnp.float32, math.log(0.5), math.log(2.0)))
    ramp = jnp.arange(D, dtype=jnp.float32) / (D - 1)
    col_scale = jnp.exp(ramp * math.log(3.0))[None, :] / math.sqrt(3.0)
    col_scale = col_scale * jnp.exp(jax.random.uniform(third_key, (1, D), jnp.float32, math.log(0.7), math.log(1.4)))
    values = jnp.clip(jax.random.normal(first_key, (REQUESTS, D), jnp.float32), -4.0, 4.0)
    return (values * row_scale * col_scale).astype(jnp.bfloat16)


def draw_lm_weight(key, part):
    key = jax.random.fold_in(key, 9)
    first_key = jax.random.fold_in(key, 0)
    spread = 3.0 / math.sqrt(D)
    values = jnp.clip(jax.random.normal(first_key, (D, VOCAB), jnp.float32), -4.0, 4.0) * spread
    return jnp.clip(values, -6.0, 6.0).astype(jnp.bfloat16)


def place_ends(array, key, least, largest):
    shape = array.shape
    spot = [jax.random.randint(jax.random.fold_in(key, axis), (), 0, shape[axis]) for axis in range(len(shape))]
    array = array.at[tuple(spot)].set(least)
    longest = shape.index(max(shape))
    spot[longest] = (spot[longest] + 1) % shape[longest]
    return array.at[tuple(spot)].set(largest)


def levels(own_key, extent, pieces, smallest, high):
    level, own = 1.0, jax.random.fold_in(own_key, 6)
    for axis_at, shards_of in pieces:
        heights = jnp.exp(jax.random.uniform(jax.random.fold_in(own, axis_at), (shards_of,), jnp.float32, smallest / len(pieces), high / len(pieces)))
        level = level * jnp.repeat(heights, extent[axis_at] // shards_of).reshape([-1 if axis == axis_at else 1 for axis in range(len(extent))])
    return level


def split_up(count, total, reach, slope):
    portions = [(1 << 20) // math.isqrt(rank ** slope) + 1 for rank in range(2, count + 1)]
    surplus, counts = total - reach - (count - 1), [1] * (count - 1)
    while surplus > 0:
        candidates = [i for i in range(count - 1) if counts[i] < reach]
        mass, budget = sum([portions[i] for i in candidates]), surplus
        for i in candidates:
            addition = min(reach - counts[i], max(1, budget * portions[i] // mass), surplus)
            counts[i] = counts[i] + addition
            surplus = surplus - addition
    return np.array([reach] + counts)


def uneven_parts(key, number_of, total, most, slope):
    if number_of == 2:
        one = jax.random.randint(key, (), max(1, total - most), min(most, total - 1) + 1)
        return jnp.stack([one, total - one])
    sizes = jnp.asarray(split_up(number_of, total, most, slope), jnp.int32)
    twos = (number_of - 1) // 2
    donor, taker = sizes[1:1 + 2 * twos:2], sizes[2:2 + 2 * twos:2]
    margin = jnp.minimum(donor - 1, most - taker)
    moved = jax.random.randint(jax.random.fold_in(key, 1), (twos,), 0, 1 << 20) % (margin + 1)
    sizes = sizes.at[1:1 + 2 * twos:2].set(donor - moved).at[2:2 + 2 * twos:2].set(taker + moved)
    return sizes[jax.random.permutation(jax.random.fold_in(key, 2), number_of)]


def noise(key, dims, scale, reach, cuts=(), kind=jnp.bfloat16):
    drawn = scale * jax.random.normal(key, dims, jnp.float32)
    if cuts:
        drawn = drawn * levels(key, dims, cuts, -0.22, 0.18)
    return jnp.clip(drawn, -reach, reach).astype(kind)


def setup_inputs(seed: int = 0) -> dict:
    arg_keys = jax.random.split(jax.random.key(seed), 12)
    latent_cache = draw_latent_cache(jax.random.fold_in(arg_keys[11], 71), 0)
    query = draw_query(jax.random.fold_in(arg_keys[11], 71), 0)
    new_latent = noise(arg_keys[2], (REQUESTS, KV_RANK + ROPE), 2.0, 9.0)
    lengths = uneven_parts(arg_keys[3], REQUESTS, REQUESTS * CTX // 2, CTX, 2).astype(jnp.int32)
    slot_of = jax.random.permutation(arg_keys[4], REQUESTS).astype(jnp.int32)
    token_ids = place_ends(jax.random.randint(arg_keys[5], (REQUESTS,), 0, VOCAB), jax.random.fold_in(arg_keys[5], 1), 0, VOCAB - 1).astype(jnp.int32)
    latent_value_weight = noise(arg_keys[6], (H, KV_RANK, VHEAD), (max(1, KV_RANK // 64)) ** -0.5, 2.0, ((0, 16),))
    out_weight = noise(arg_keys[7], (H * VHEAD, D), (H * VHEAD) ** -0.5, 0.046875, ((0, 16), (1, 8)))
    residual = draw_residual(jax.random.fold_in(arg_keys[11], 71), 0)
    norm_gain = jnp.clip(1.0 + 0.1 * jax.random.normal(arg_keys[9], (D,), jnp.float32), 0.5, 1.5).astype(jnp.bfloat16)
    lm_weight = draw_lm_weight(jax.random.fold_in(arg_keys[11], 71), 0)
    return {"latent_cache": latent_cache, "query": query, "new_latent": new_latent, "lengths": lengths, "slot_of": slot_of, "token_ids": token_ids, "latent_value_weight": latent_value_weight, "out_weight": out_weight, "residual": residual, "norm_gain": norm_gain, "lm_weight": lm_weight}


def reference(latent_cache, query, new_latent, lengths, slot_of, token_ids, latent_value_weight, out_weight, residual, norm_gain, lm_weight):
    sm_scale = (VHEAD + ROPE) ** (-0.5)
    holder = jnp.zeros((REQUESTS,), jnp.int32).at[slot_of].set(jnp.arange(REQUESTS, dtype=jnp.int32))
    positions = jnp.arange(CTX, dtype=jnp.int32)

    def attend(operands):
        cache_one, query_one, new_one, length_one = operands
        scores = jnp.dot(query_one, cache_one.T, preferred_element_type=jnp.float32) * sm_scale
        scores = jnp.where(positions[None, :] < length_one, scores, -jnp.inf)
        own_score = jnp.dot(query_one, new_one, preferred_element_type=jnp.float32) * sm_scale
        highest = jnp.maximum(lax.optimization_barrier(jnp.max(scores, axis=1)), own_score)
        probs = jnp.exp(scores - highest[:, None])
        own_prob = jnp.exp(own_score - highest)
        total = lax.optimization_barrier(jnp.sum(probs, axis=1)) + own_prob
        accum = jnp.dot(probs.astype(jnp.bfloat16), cache_one[:, :KV_RANK], preferred_element_type=jnp.float32)
        accum = accum + own_prob.astype(jnp.bfloat16).astype(jnp.float32)[:, None] * new_one[:KV_RANK].astype(jnp.float32)[None, :]
        return (accum / total[:, None]).astype(jnp.bfloat16)
    latent_output = lax.map(attend, (latent_cache, query, new_latent, lengths))
    per_head_values = jnp.einsum('yfg,fgu->yfu', latent_output.astype(jnp.float32), latent_value_weight.astype(jnp.float32)).astype(jnp.bfloat16)
    attention_result = jnp.dot(per_head_values.reshape(REQUESTS, H * VHEAD), out_weight, preferred_element_type=jnp.float32)
    hidden = residual.astype(jnp.float32) + attention_result
    squares = lax.optimization_barrier(jnp.sum(hidden * hidden, axis=1))
    scaled = (hidden * norm_gain.astype(jnp.float32)[None, :]).astype(jnp.bfloat16)
    logits = jnp.dot(scaled, lm_weight, preferred_element_type=jnp.float32) * lax.rsqrt(squares / D + 1e-06)[:, None]
    highest = lax.optimization_barrier(jnp.max(logits, axis=1))
    log_normalizer = highest + jnp.log(lax.optimization_barrier(jnp.sum(jnp.exp(logits - highest[:, None]), axis=1)))
    logp = logits - log_normalizer[:, None]
    target_all = jnp.take_along_axis(logp, token_ids[:, None], axis=1)[:, 0]
    logprobs = jnp.take(logp, holder, axis=0)
    target_logprob = jnp.take(target_all, holder, axis=0)
    return (logprobs, target_logprob)
```

```python
import functools

import jax
import jax.numpy as jnp
from jax import lax
from jax.experimental import pallas as pl
from jax.experimental.pallas import tpu as pltpu
from jax.sharding import PartitionSpec as P

KV_RANK = 512
ROPE = 64
VHEAD = 128
D = 7168
WIDTH = KV_RANK + ROPE
MESH = pl.DeviceIdType.MESH
FILL = -(2.0**100)
SCALE = (VHEAD + ROPE) ** (-0.5)
EXTRA = 128
HALF = 4096
CHUNKS = 4

PAIRS = ("x", "y", "y", "z")


def drain(ref, sem):
    pltpu.make_async_copy(ref, ref, sem).wait()


def kernel(
    lens, cache, query, newl, slots, toks, resid, gain, vw, ow, lm,
    out, tgt,
    kbuf, qbuf, pout, pin, vwv, owv, lmv, qown, lat, hv, rss, rsr, hsl, hid,
    sqs, sqr, ls, lr, lb, sms, smr,
    s_k, r_k, s_q, r_q, s_p, r_p, l_w, s_h, r_h, s_r, r_r, s_a, r_a, s_s, r_s,
    s_c, r_c, s_y, r_y, s_m, r_m,
):
    p, d = lax.axis_index("pre"), lax.axis_index("dec")
    y, c = lax.div(p, 2), lax.rem(p, 2)
    x, z = lax.div(d, 4), lax.rem(d, 4)
    vocab = lm.shape[1]

    def at(xx, yy, zz, cc):
        return (2 * yy + cc, 4 * xx + zz)

    def turn(value, step):
        return lax.rem(value + step, 4)

    def send(src, dst, ssem, rsem, device):
        pltpu.make_async_remote_copy(
            src_ref=src, dst_ref=dst, send_sem=ssem, recv_sem=rsem,
            device_id=device, device_id_type=MESH,
        ).start()

    def signal(device):
        pl.semaphore_signal(barrier, inc=1, device_id=device, device_id_type=MESH)

    DEC = [(i, j) for i in range(4) for j in range(4) if (i, j) != (0, 0)]
    PRE = [(i, j) for i in range(4) for j in range(2) if (i, j) != (0, 0)]

    barrier = pltpu.get_barrier_semaphore()
    for i, j in DEC:
        signal(at(turn(x, i), y, turn(z, j), c))
    for i, j in PRE:
        signal(at(x, turn(y, i), z, lax.rem(c + j, 2)))
    for i in (1, 2, 3):
        signal(at(turn(x, i), y, z, 1 - c))
        signal(at(x, y, turn(z, i), 1 - c))
    for i, j in DEC:
        signal(at(y, turn(y, i), turn(z, j), c))
        signal(at(turn(x, i), turn(y, j), y, c))

    @pl.when(x != y)
    def _():
        signal(at(y, y, z, c))

    @pl.when(z != y)
    def _():
        signal(at(x, y, y, c))

    pl.semaphore_wait(
        barrier,
        15 + 7 + 6 + 30 + (x != y).astype(jnp.int32) + (z != y).astype(jnp.int32),
    )

    def group_of(axis, xx, yy, zz, cc):
        return 2 * {"x": xx, "y": yy, "z": zz}[axis] + cc

    def send_cache(k):
        axis = PAIRS[k]
        mine = group_of(axis, x, y, z, c)
        for i, j in PRE:
            xx = turn(x, i) if axis == "x" else x
            yy = turn(y, i) if axis == "y" else y
            zz = turn(z, i) if axis == "z" else z
            cc = lax.rem(c + j, 2)
            send(
                cache.at[pl.ds(8 * group_of(axis, xx, yy, zz, cc) + 2 * k, 2)],
                kbuf.at[k, :, pl.ds(64 * mine, 64), :],
                s_k.at[k], r_k.at[k], at(xx, yy, zz, cc),
            )
        pltpu.make_async_copy(
            cache.at[pl.ds(8 * mine + 2 * k, 2)],
            kbuf.at[k, :, pl.ds(64 * mine, 64), :],
            r_k.at[k],
        ).start()

    QROWS = {"x": (0, 16), "y": (16, 32), "z": (48, 16)}
    QSEM = {"x": 0, "y": 1, "z": 2}

    def send_query(axis):
        first, rows = QROWS[axis]
        sem = QSEM[axis]
        for i, j in DEC:
            xx, zz = turn(x, i), turn(z, j)
            send(
                query.at[pl.ds(64 * group_of(axis, xx, y, zz, c) + first, rows)],
                qbuf.at[d, pl.ds(first, rows), :],
                s_q.at[sem], r_q.at[sem], at(xx, y, zz, c),
            )
        pltpu.make_async_copy(
            query.at[pl.ds(64 * group_of(axis, x, y, z, c) + first, rows)],
            qbuf.at[d, pl.ds(first, rows), :],
            r_q.at[sem],
        ).start()

    send_cache(1)
    send_query("y")
    send_query("x")
    send_query("z")
    send_cache(0)
    send_cache(3)
    send_cache(2)
    loads = [
        pltpu.make_async_copy(query.at[pl.ds(64 * p, 64)], qown, l_w.at[0]),
        pltpu.make_async_copy(vw, vwv, l_w.at[1]),
        pltpu.make_async_copy(ow, owv, l_w.at[2]),
        pltpu.make_async_copy(lm, lmv, l_w.at[3]),
    ]
    for load in loads:
        load.start()

    loads[0].wait()
    row = lax.broadcasted_iota(jnp.int32, (64, 64), 0)
    col = lax.broadcasted_iota(jnp.int32, (64, 64), 1)
    pick = (col == 8 * p + (row >> 3)).astype(jnp.float32).astype(jnp.bfloat16)
    new_rows = jnp.dot(pick, newl[...], preferred_element_type=jnp.float32)
    own = jnp.sum(qown[...].astype(jnp.float32) * new_rows, axis=1, keepdims=True) * SCALE
    to_slot = (slots[...] == row).astype(jnp.float32).astype(jnp.bfloat16)
    resid_slot = jnp.dot(to_slot, resid[...], preferred_element_type=jnp.float32)
    ls[:, :, :, pl.ds(HALF - 128, 128)] = jnp.zeros((2, 4, 16, 128), jnp.bfloat16)

    spot = lax.broadcasted_iota(jnp.int32, (1, 512), 1)
    lane = lax.broadcasted_iota(jnp.int32, (128, EXTRA), 1)

    def position(axis):
        slot, core, inner = spot >> 7, (spot >> 6) & 1, spot & 63
        xx = slot if axis == "x" else x
        yy = slot if axis == "y" else y
        zz = slot if axis == "z" else z
        return 64 * ((4 * xx + zz) * 8 + 2 * yy + core) + inner

    def attend(k):
        axis = PAIRS[k]
        drain(kbuf.at[k], r_k.at[k])
        spots = position(axis)
        group = group_of(axis, x, y, z, c)
        both = qbuf[:, pl.ds(16 * k, 16), :].astype(jnp.float32).reshape(16, 2, 8, WIDTH)
        sums, extras = [], []
        for j in range(2):
            rows = both[:, j].reshape(128, WIDTH).astype(jnp.bfloat16)
            keys = kbuf[k, j]
            scores = lax.dot_general(
                rows, keys, (((1,), (1,)), ((), ())), preferred_element_type=jnp.float32
            ) * SCALE
            scores = jnp.where(spots < lens[8 * group + 2 * k + j], scores, FILL)
            top = jnp.max(scores, axis=1, keepdims=True)
            top = top.astype(jnp.bfloat16).astype(jnp.float32)
            weights = jnp.exp(scores - top)
            total = jnp.sum(weights, axis=1, keepdims=True)
            sums.append(
                jnp.dot(
                    weights.astype(jnp.bfloat16), keys[:, :KV_RANK],
                    preferred_element_type=jnp.float32,
                ).reshape(16, 8, KV_RANK)
            )
            high = total.astype(jnp.bfloat16).astype(jnp.float32)
            extra = jnp.where(lane == 0, top, jnp.where(lane == 1, high, total - high))
            extras.append(extra.reshape(16, 8, EXTRA))
        pout[k, :, :, pl.ds(0, KV_RANK)] = jnp.concatenate(sums, axis=1).astype(jnp.bfloat16)
        pout[k, :, :, pl.ds(KV_RANK, EXTRA)] = jnp.concatenate(extras, axis=1).astype(jnp.bfloat16)
        yy = {"x": x, "y": y, "z": z}[axis]
        place = {"x": 4 * y + z, "y": d, "z": 4 * x + y}[axis]
        for i, j in DEC:
            xx, zz = turn(x, i), turn(z, j)
            send(
                pout.at[k, 4 * xx + zz], pin.at[k, place],
                s_p.at[k], r_p.at[k], at(xx, yy, zz, c),
            )

        def keep():
            pltpu.make_async_copy(pout.at[k, d], pin.at[k, place], r_p.at[k]).start()

        if axis == "y":
            keep()
        else:
            pl.when(yy == y)(keep)

            @pl.when(yy != y)
            def _():
                send(
                    pout.at[k, d], pin.at[k, place],
                    s_p.at[k], r_p.at[k], at(x, yy, z, c),
                )

    drain(qbuf.at[:, pl.ds(16, 32), :], r_q.at[1])
    attend(1)
    drain(qbuf.at[:, pl.ds(0, 16), :], r_q.at[0])
    attend(0)
    drain(qbuf.at[:, pl.ds(48, 16), :], r_q.at[2])
    attend(3)
    attend(2)

    for k in (1, 0, 3, 2):
        drain(pin.at[k], r_p.at[k])
        extra = pin[k, :, :, pl.ds(KV_RANK, EXTRA)].astype(jnp.float32)
        tops = extra[:, :, 0:1]
        totals = extra[:, :, 1:2] + extra[:, :, 2:3]
        own_k = own[16 * k:16 * k + 16]
        top = jnp.maximum(jnp.max(tops, axis=0), own_k)
        shrink = jnp.exp(tops - top[None])
        own_weight = jnp.exp(own_k - top)
        total = jnp.sum(totals * shrink, axis=0) + own_weight
        summed = (
            own_weight.astype(jnp.bfloat16).astype(jnp.float32)
            * new_rows[16 * k:16 * k + 16, :KV_RANK]
        )
        for s in range(16):
            summed = summed + shrink[s] * pin[k, s, :, pl.ds(0, KV_RANK)].astype(jnp.float32)
        summed = summed / total
        for b in range(KV_RANK // 128):
            lat[b, pl.ds(16 * k, 16), :] = summed[:, 128 * b:128 * b + 128]

    loads[1].wait()
    values = []
    for f in range(8):
        rows = jnp.concatenate(
            [lat[b, pl.ds(f, 8, stride=8), :] for b in range(KV_RANK // 128)], axis=1
        ).astype(jnp.bfloat16)
        values.append(jnp.dot(rows, vwv[f], preferred_element_type=jnp.float32))
    packed = jnp.concatenate(
        [jnp.concatenate(values[:4], axis=1), jnp.concatenate(values[4:], axis=1)], axis=0
    )
    hv[p] = packed.astype(jnp.bfloat16)
    for n, (i, j) in enumerate(PRE):
        send(hv.at[p], hv.at[p], s_h.at[n], r_h.at[n], at(x, turn(y, i), z, lax.rem(c + j, 2)))
    loads[2].wait()
    for n in range(7):
        drain(hv.at[0], r_h.at[n])

    heads = hv[...].astype(jnp.float32).reshape(8, 2, 8, KV_RANK)
    part = resid_slot * jnp.where(d == 0, 1.0, 0.0)
    for half in range(2):
        rows = heads[:, half].reshape(64, KV_RANK).astype(jnp.bfloat16)
        rows = jnp.dot(to_slot, rows, preferred_element_type=jnp.float32).astype(jnp.bfloat16)
        part = part + jnp.dot(
            rows, owv[pl.ds(KV_RANK * half, KV_RANK), :], preferred_element_type=jnp.float32
        )
    for s in range(16):
        rss[s] = part[4 * s:4 * s + 4]
    for n, (i, j) in enumerate(DEC):
        xx, zz = turn(x, i), turn(z, j)
        send(rss.at[4 * xx + zz], rsr.at[n], s_r.at[0], r_r.at[0], at(xx, y, zz, c))
    drain(rsr, r_r.at[0])
    hidden4 = rss[d]
    for n in range(15):
        hidden4 = hidden4 + rsr[n]
    hsl[d] = hidden4
    for n, (i, j) in enumerate(DEC):
        send(hsl.at[d], hsl.at[d], s_a.at[n], r_a.at[n], at(turn(x, i), y, turn(z, j), c))
    for n in range(15):
        drain(hsl.at[0], r_a.at[n])
    for s in range(16):
        hid[pl.ds(4 * s, 4), :] = hsl[s]
    hidden = hid[...]
    squares = jnp.sum(hidden * hidden, axis=1, keepdims=True)
    sqs[...] = jnp.broadcast_to(squares, (64, 128)).reshape(8, 8, 128)
    for n, (i, j) in enumerate(PRE):
        yy, cc = turn(y, i), lax.rem(c + j, 2)
        send(sqs.at[2 * yy + cc], sqr.at[n], s_s.at[0], r_s.at[0], at(x, yy, z, cc))
    scaled = (hidden * gain[...].astype(jnp.float32)).astype(jnp.bfloat16)

    wide = HALF // CHUNKS

    def join_cores(i):
        lanes = pl.ds(wide * i, wide)
        drain(lr.at[:, :, lanes], r_c.at[i])
        ls[c, :, :, lanes] = (
            ls[c, :, :, lanes].astype(jnp.float32) + lr[:, :, lanes].astype(jnp.float32)
        ).astype(jnp.bfloat16)
        for step in (1, 2, 3):
            yy = turn(y, step)
            send(
                ls.at[c, yy, :, lanes], lb.at[step - 1, :, lanes],
                s_y.at[i], r_y.at[i], at(x, yy, z, c),
            )

    loads[3].wait()
    for i in range(CHUNKS):
        for half in range(2):
            start = HALF * half + wide * i
            count = min(wide, vocab - start)
            product = jnp.dot(
                scaled, lmv[:, pl.ds(start, count)], preferred_element_type=jnp.float32
            ).reshape(8, 8, count).astype(jnp.bfloat16)
            for q in range(8):
                ls[q % 2, q // 2, pl.ds(8 * half, 8), pl.ds(wide * i, count)] = product[q]
        lanes = pl.ds(wide * i, wide)
        send(
            ls.at[1 - c, :, :, lanes], lr.at[:, :, lanes],
            s_c.at[i], r_c.at[i], at(x, y, z, 1 - c),
        )
        if i > 0:
            join_cores(i - 1)
    join_cores(CHUNKS - 1)

    drain(sqr, r_s.at[0])
    norm = sqs[p]
    for n in range(7):
        norm = norm + sqr[n]
    norm = lax.rsqrt(norm[:, 0:1] / D + 1e-06)
    for i in range(CHUNKS):
        drain(lb.at[:, :, pl.ds(wide * i, wide)], r_y.at[i])
    logits = ls[c, y].astype(jnp.float32)
    for n in range(3):
        logits = logits + lb[n].astype(jnp.float32)
    low, high = logits[:8] * norm, logits[8:] * norm

    column = lax.broadcasted_iota(jnp.int32, (8, HALF), 1)
    high = jnp.where(column < vocab - HALF, high, FILL)
    slot_rows = lax.broadcasted_iota(jnp.int32, (8, 64), 0) + 8 * p
    token = jnp.sum(jnp.where(slots[...] == slot_rows, toks[...], 0), axis=1, keepdims=True)
    token = token - d * vocab
    picked = jnp.sum(jnp.where(column == token, low, 0.0), axis=1, keepdims=True) + jnp.sum(
        jnp.where((column + HALF == token) & (column < vocab - HALF), high, 0.0),
        axis=1, keepdims=True,
    )
    top = jnp.maximum(
        jnp.max(low, axis=1, keepdims=True), jnp.max(high, axis=1, keepdims=True)
    )
    total = jnp.sum(jnp.exp(low - top), axis=1, keepdims=True) + jnp.sum(
        jnp.exp(high - top), axis=1, keepdims=True
    )
    lane8 = lax.broadcasted_iota(jnp.int32, (8, 128), 1)
    mine = jnp.where(lane8 == 0, top, jnp.where(lane8 == 1, total, picked))
    sms[...] = mine
    for n, (i, j) in enumerate(DEC):
        send(sms, smr.at[n], s_m.at[0], r_m.at[0], at(turn(x, i), y, turn(z, j), c))
    drain(smr, r_m.at[0])
    others = smr[...]
    best = jnp.maximum(jnp.max(others[:, :, 0:1], axis=0), top)
    total = total * jnp.exp(top - best) + jnp.sum(
        others[:, :, 1:2] * jnp.exp(others[:, :, 0:1] - best[None]), axis=0
    )
    picked = picked + jnp.sum(others[:, :, 2:3], axis=0)
    normalizer = best + jnp.log(total)
    out[:, pl.ds(0, HALF)] = low - normalizer
    out[:, pl.ds(HALF, vocab - HALF)] = (high - normalizer)[:, : vocab - HALF]
    tgt[...] = jnp.broadcast_to(picked - normalizer, (8, 128))

    for k in range(4):
        drain(kbuf.at[k, :, pl.ds(0, 448), :], s_k.at[k])
        drain(pin.at[k, pl.ds(0, 15)], s_p.at[k])
        if PAIRS[k] != "y":

            @pl.when({"x": x, "z": z}[PAIRS[k]] != y)
            def _():
                drain(pin.at[k, 0], s_p.at[k])

    for axis in "xyz":
        first, rows = QROWS[axis]
        drain(qbuf.at[pl.ds(0, 15), pl.ds(first, rows), :], s_q.at[QSEM[axis]])
    for n in range(7):
        drain(hv.at[0], s_h.at[n])
    drain(rsr, s_r.at[0])
    for n in range(15):
        drain(hsl.at[0], s_a.at[n])
    drain(sqr, s_s.at[0])
    for i in range(CHUNKS):
        drain(lr.at[:, :, pl.ds(wide * i, wide)], s_c.at[i])
        drain(lb.at[:, :, pl.ds(wide * i, wide)], s_y.at[i])
    drain(smr, s_m.at[0])


def body(
    latent_cache, query, new_latent, lengths, slot_of, token_ids,
    latent_value_weight, out_weight, residual, norm_gain, lm_weight,
):
    columns, vocab = lm_weight.shape
    bf16, f32 = jnp.bfloat16, jnp.float32
    vmem = pl.BlockSpec(memory_space=pltpu.VMEM)
    anywhere = pl.BlockSpec(memory_space=pl.ANY)
    smem = pl.BlockSpec(memory_space=pltpu.SMEM)
    dma = pltpu.SemaphoreType.DMA
    logprobs, target = pl.pallas_call(
        kernel,
        out_shape=(
            jax.ShapeDtypeStruct((8, vocab), f32),
            jax.ShapeDtypeStruct((8, 128), f32),
        ),
        in_specs=[smem, anywhere, anywhere, vmem, vmem, vmem, vmem, vmem,
                  anywhere, anywhere, anywhere],
        out_specs=(vmem, vmem),
        scratch_shapes=[
            pltpu.VMEM((4, 2, 512, WIDTH), bf16),
            pltpu.VMEM((16, 64, WIDTH), bf16),
            pltpu.VMEM((4, 16, 16, KV_RANK + EXTRA), bf16),
            pltpu.VMEM((4, 16, 16, KV_RANK + EXTRA), bf16),
            pltpu.VMEM((8, KV_RANK, VHEAD), bf16),
            pltpu.VMEM((1024, columns), bf16),
            pltpu.VMEM((columns, vocab), bf16),
            pltpu.VMEM((64, WIDTH), bf16),
            pltpu.VMEM((KV_RANK // 128, 64, 128), f32),
            pltpu.VMEM((8, 16, 512), bf16),
            pltpu.VMEM((16, 4, columns), f32),
            pltpu.VMEM((15, 4, columns), f32),
            pltpu.VMEM((16, 4, columns), f32),
            pltpu.VMEM((64, columns), f32),
            pltpu.VMEM((8, 8, 128), f32),
            pltpu.VMEM((7, 8, 128), f32),
            pltpu.VMEM((2, 4, 16, HALF), bf16),
            pltpu.VMEM((4, 16, HALF), bf16),
            pltpu.VMEM((3, 16, HALF), bf16),
            pltpu.VMEM((8, 128), f32),
            pltpu.VMEM((15, 8, 128), f32),
            dma((4,)), dma((4,)), dma((3,)), dma((3,)), dma((4,)), dma((4,)), dma((4,)),
            dma((7,)), dma((7,)), dma((1,)), dma((1,)), dma((15,)), dma((15,)),
            dma((1,)), dma((1,)), dma((CHUNKS,)), dma((CHUNKS,)), dma((CHUNKS,)),
            dma((CHUNKS,)), dma((1,)), dma((1,)),
        ],
        name="decode_step",
        compiler_params=pltpu.CompilerParams(
            collective_id=0, has_side_effects=True, vmem_limit_bytes=56 << 20
        ),
    )(
        lengths,
        latent_cache,
        query.reshape(-1, WIDTH),
        new_latent,
        slot_of.reshape(1, -1),
        token_ids.reshape(1, -1),
        residual,
        norm_gain.reshape(1, -1),
        latent_value_weight,
        out_weight,
        lm_weight,
    )
    return logprobs, target[:, 0]


def solution(mesh):
    return jax.shard_map(
        body,
        mesh=mesh,
        in_specs=(
            P(None, ("dec", "pre"), None),
            P(None, "dec", None),
            P(),
            P(),
            P(),
            P(),
            P("dec", None, None),
            P("dec", "pre"),
            P(None, "pre"),
            P("pre"),
            P("pre", "dec"),
        ),
        out_specs=(P("pre", "dec"), P("pre")),
        check_vma=False,
    )
```

```python
import functools

import jax
import jax.numpy as jnp
from jax import lax
from jax.experimental import pallas as pl
from jax.experimental.pallas import tpu as pltpu
from jax.sharding import PartitionSpec as P

KV_RANK = 512
ROPE = 64
VHEAD = 128
D = 7168
WIDTH = KV_RANK + ROPE
MESH = pl.DeviceIdType.MESH
FILL = -(2.0**100)
SCALE = (VHEAD + ROPE) ** (-0.5)
EXTRA = 128
HALF = 4096
CHUNKS = 4

PAIRS = ("x", "y", "y", "z")
EARLY = ("x", "z", "x", "z")
FIRST = ("z", "x", "z", "x")


def drain(ref, sem):
    pltpu.make_async_copy(ref, ref, sem).wait()


def kernel(
    lens, cache, query, newl, slots, toks, resid, gain, vw, ow, lm,
    out, tgt,
    kbuf, qbuf, pout, pjoin, pmid, pin, vwv, owv, lmv, qown, lat, hv, resw, rss, rsr, agb,
    sqs, sqr, ls, lr, lb, sms, smr,
    s_k, r_k, s_q, r_q, s_v, r_v, s_p, r_p, s_j, r_j, l_w, s_h, r_h, s_r, r_r, s_a, r_a, s_s, r_s,
    s_c, r_c, s_y, r_y, s_m, r_m,
):
    p, d = lax.axis_index("pre"), lax.axis_index("dec")
    y, c = lax.div(p, 2), lax.rem(p, 2)
    x, z = lax.div(d, 4), lax.rem(d, 4)
    vocab = lm.shape[0]

    def at(xx, yy, zz, cc):
        return (2 * yy + cc, 4 * xx + zz)

    def turn(value, step):
        return lax.rem(value + step, 4)

    def send(src, dst, ssem, rsem, device):
        pltpu.make_async_remote_copy(
            src_ref=src, dst_ref=dst, send_sem=ssem, recv_sem=rsem,
            device_id=device, device_id_type=MESH,
        ).start()

    pending = []

    def later(ref, sem):
        pending.append(lambda: drain(ref, sem))

    def finish():
        for wait in pending:
            wait()

    def signal(device):
        pl.semaphore_signal(barrier, inc=1, device_id=device, device_id_type=MESH)

    DEC = [(i, j) for i in range(4) for j in range(4) if (i, j) != (0, 0)]
    PRE = [(i, j) for i in range(4) for j in range(2) if (i, j) != (0, 0)]

    barrier = pltpu.get_barrier_semaphore()
    for i, j in DEC:
        signal(at(turn(x, i), y, turn(z, j), c))
    for i, j in PRE:
        signal(at(x, turn(y, i), z, lax.rem(c + j, 2)))
    for i in (1, 2, 3):
        signal(at(turn(x, i), y, z, 1 - c))
        signal(at(x, y, turn(z, i), 1 - c))
    for i in (1, 2, 3):
        signal(at(y, turn(y, i), z, c))
        signal(at(x, turn(y, i), y, c))

    @pl.when(x != y)
    def _():
        signal(at(y, y, z, c))

    @pl.when(z != y)
    def _():
        signal(at(x, y, y, c))

    pl.semaphore_wait(
        barrier,
        15 + 7 + 6 + 6 + (x != y).astype(jnp.int32) + (z != y).astype(jnp.int32),
    )

    def group_of(axis, xx, yy, zz, cc):
        return 2 * {"x": xx, "y": yy, "z": zz}[axis] + cc

    def send_cache(k):
        axis = PAIRS[k]
        mine = group_of(axis, x, y, z, c)
        for i, j in PRE:
            xx = turn(x, i) if axis == "x" else x
            yy = turn(y, i) if axis == "y" else y
            zz = turn(z, i) if axis == "z" else z
            cc = lax.rem(c + j, 2)
            send(
                cache.at[pl.ds(8 * group_of(axis, xx, yy, zz, cc) + 2 * k, 2)],
                kbuf.at[k, :, pl.ds(64 * mine, 64), :],
                s_k.at[k], r_k.at[k], at(xx, yy, zz, cc),
            )
        pltpu.make_async_copy(
            cache.at[pl.ds(8 * mine + 2 * k, 2)],
            kbuf.at[k, :, pl.ds(64 * mine, 64), :],
            r_k.at[k],
        ).start()
        later(kbuf.at[k, :, pl.ds(0, 448), :], s_k.at[k])

    def along(axis, step):
        return (turn(x, step), z) if axis == "x" else (x, turn(z, step))

    def coordinate(axis):
        return x if axis == "x" else z

    def send_query(k):
        axis = PAIRS[k]
        block = qbuf.at[k, coordinate(FIRST[k]), coordinate(EARLY[k])]
        for i in (1, 2, 3):
            xx, zz = along(EARLY[k], i)
            send(
                query.at[pl.ds(64 * group_of(axis, xx, y, zz, c) + 16 * k, 16)], block,
                s_q.at[k], r_q.at[k], at(xx, y, zz, c),
            )
        pltpu.make_async_copy(
            query.at[pl.ds(64 * group_of(axis, x, y, z, c) + 16 * k, 16)], block, r_q.at[k]
        ).start()
        later(qbuf.at[k, 0, pl.ds(0, 3)], s_q.at[k])

    def pass_query(k):
        met = qbuf.at[k, coordinate(FIRST[k])]
        drain(met, r_q.at[k])
        for i in (1, 2, 3):
            xx, zz = along(FIRST[k], i)
            send(met, met, s_v.at[k], r_v.at[k], at(xx, y, zz, c))
        later(qbuf.at[k, pl.ds(0, 3)], s_v.at[k])

    for k in range(4):
        send_query(k)
    for k in (1, 0, 3, 2):
        send_cache(k)
    loads = [
        pltpu.make_async_copy(query.at[pl.ds(64 * p, 64)], qown, l_w.at[0]),
        pltpu.make_async_copy(vw, vwv, l_w.at[1]),
        pltpu.make_async_copy(ow, owv, l_w.at[2]),
        pltpu.make_async_copy(lm, lmv, l_w.at[3]),
    ]
    for load in loads:
        load.start()

    def window(rows, n):
        left = 384 * (n % 2)
        block = rows[8 * (n // 2):8 * (n // 2) + 8]
        return jnp.concatenate([block[:, left:left + 256], block[:, left + 256:left + 512]], axis=0)

    for k in (1, 0, 3, 2):
        pass_query(k)

    loads[0].wait()
    row = lax.broadcasted_iota(jnp.int32, (64, 64), 0)
    col = lax.broadcasted_iota(jnp.int32, (64, 64), 1)
    pick = (col == 8 * p + (row >> 3)).astype(jnp.float32).astype(jnp.bfloat16)
    new_rows = jnp.dot(pick, newl[...], preferred_element_type=jnp.float32)
    own = jnp.sum(qown[...].astype(jnp.float32) * new_rows, axis=1, keepdims=True) * SCALE
    to_slot = (slots[...] == row).astype(jnp.float32).astype(jnp.bfloat16)
    resid_slot = jnp.dot(to_slot, resid[...], preferred_element_type=jnp.float32)
    for n in range(16):
        resw[n] = window(resid_slot, n)
    ls[:, :, :, pl.ds(HALF - 128, 128)] = jnp.zeros((2, 4, 16, 128), jnp.bfloat16)

    spot = lax.broadcasted_iota(jnp.int32, (1, 512), 1)
    lane = lax.broadcasted_iota(jnp.int32, (128, EXTRA), 1)
    lane16 = lax.broadcasted_iota(jnp.int32, (16, EXTRA), 1)

    def position(axis):
        slot, core, inner = spot >> 7, (spot >> 6) & 1, spot & 63
        xx = slot if axis == "x" else x
        yy = slot if axis == "y" else y
        zz = slot if axis == "z" else z
        return 64 * ((4 * xx + zz) * 8 + 2 * yy + core) + inner

    def attend(k):
        axis = PAIRS[k]
        drain(qbuf.at[k, pl.ds(0, 3)], r_v.at[k])
        drain(kbuf.at[k], r_k.at[k])
        spots = position(axis)
        group = group_of(axis, x, y, z, c)
        both = qbuf[k].astype(jnp.float32).reshape(16, 2, 8, WIDTH)
        sums, extras = [], []
        for j in range(2):
            rows = both[:, j].reshape(128, WIDTH).astype(jnp.bfloat16)
            keys = kbuf[k, j]
            scores = lax.dot_general(
                rows, keys, (((1,), (1,)), ((), ())), preferred_element_type=jnp.float32
            ) * SCALE
            scores = jnp.where(spots < lens[8 * group + 2 * k + j], scores, FILL)
            top = jnp.max(scores, axis=1, keepdims=True)
            top = top.astype(jnp.bfloat16).astype(jnp.float32)
            weights = jnp.exp(scores - top)
            total = jnp.sum(weights, axis=1, keepdims=True)
            sums.append(
                jnp.dot(
                    weights.astype(jnp.bfloat16), keys[:, :KV_RANK],
                    preferred_element_type=jnp.float32,
                ).reshape(16, 8, KV_RANK)
            )
            high = total.astype(jnp.bfloat16).astype(jnp.float32)
            extra = jnp.where(lane == 0, top, jnp.where(lane == 1, high, total - high))
            extras.append(extra.reshape(16, 8, EXTRA))
        sums = jnp.concatenate(sums, axis=1).astype(jnp.bfloat16).reshape(4, 4, 16, KV_RANK)
        extras = jnp.concatenate(extras, axis=1).astype(jnp.bfloat16).reshape(4, 4, 16, EXTRA)
        for n in range(4):
            pout[k, n, :, :, pl.ds(0, KV_RANK)] = sums[n]
            pout[k, n, :, :, pl.ds(KV_RANK, EXTRA)] = extras[n]
        for i in (1, 2, 3):
            xx, zz = along(FIRST[k], i)
            send(
                pout.at[k, xx if FIRST[k] == "x" else zz], pmid.at[k, i - 1],
                s_p.at[k], r_p.at[k], at(xx, y, zz, c),
            )
        later(pmid.at[k], s_p.at[k])

    def joined(blocks, own=None):
        extra = [block[..., KV_RANK:].astype(jnp.float32) for block in blocks]
        tops = [part[..., 0:1] for part in extra]
        top = functools.reduce(jnp.maximum, tops)
        if own is not None:
            top = jnp.maximum(top, own)
        shrink = [jnp.exp(part - top) for part in tops]
        total = sum((part[..., 1:2] + part[..., 2:3]) * by for part, by in zip(extra, shrink))
        summed = sum(
            block[..., :KV_RANK].astype(jnp.float32) * by for block, by in zip(blocks, shrink)
        )
        return top, total, summed

    def join_first(k):
        axis, first = PAIRS[k], FIRST[k]
        drain(pmid.at[k], r_p.at[k])
        for n in range(4):
            blocks = [pout[k, coordinate(first), n]] + [pmid[k, i, n] for i in range(3)]
            top, total, summed = joined(blocks)
            high = total.astype(jnp.bfloat16).astype(jnp.float32)
            extra = jnp.where(lane16 == 0, top, jnp.where(lane16 == 1, high, total - high))
            pjoin[k, n, :, pl.ds(0, KV_RANK)] = summed.astype(jnp.bfloat16)
            pjoin[k, n, :, pl.ds(KV_RANK, EXTRA)] = extra.astype(jnp.bfloat16)
        yy = {"x": x, "y": y, "z": z}[axis]
        place = y if axis != "y" else (z if first == "x" else x)
        here = z if first == "x" else x
        for i in (1, 2, 3):
            other = turn(here, i)
            xx, zz = (x, other) if first == "x" else (other, z)
            send(
                pjoin.at[k, other], pin.at[k, place],
                s_j.at[k], r_j.at[k], at(xx, yy, zz, c),
            )
        later(pin.at[k, pl.ds(0, 3)], s_j.at[k])

        def keep():
            pltpu.make_async_copy(pjoin.at[k, here], pin.at[k, place], r_j.at[k]).start()

        if axis == "y":
            keep()
        else:
            pl.when(yy == y)(keep)

            @pl.when(yy != y)
            def _():
                send(
                    pjoin.at[k, here], pin.at[k, place],
                    s_j.at[k], r_j.at[k], at(x, yy, z, c),
                )

            def left():
                pl.when(yy != y)(lambda: drain(pin.at[k, 0], s_j.at[k]))

            pending.append(left)

    attend(1)
    attend(0)
    join_first(1)
    attend(3)
    join_first(0)
    attend(2)
    join_first(3)
    join_first(2)

    for k in (1, 0, 3, 2):
        drain(pin.at[k], r_j.at[k])
        own_k = own[16 * k:16 * k + 16]
        top, total, summed = joined([pin[k, n] for n in range(4)], own_k)
        own_weight = jnp.exp(own_k - top)
        summed = summed + (
            own_weight.astype(jnp.bfloat16).astype(jnp.float32)
            * new_rows[16 * k:16 * k + 16, :KV_RANK]
        )
        summed = summed / (total + own_weight)
        for b in range(KV_RANK // 128):
            lat[b, pl.ds(16 * k, 16), :] = summed[:, 128 * b:128 * b + 128]

    loads[1].wait()
    values = []
    for f in range(8):
        rows = jnp.concatenate(
            [lat[b, pl.ds(f, 8, stride=8), :] for b in range(KV_RANK // 128)], axis=1
        ).astype(jnp.bfloat16)
        values.append(jnp.dot(rows, vwv[f], preferred_element_type=jnp.float32))
    packed = jnp.concatenate(
        [jnp.concatenate(values[:4], axis=1), jnp.concatenate(values[4:], axis=1)], axis=0
    )
    hv[p] = packed.astype(jnp.bfloat16)
    for n, (i, j) in enumerate(PRE):
        send(hv.at[p], hv.at[p], s_h.at[n], r_h.at[n], at(x, turn(y, i), z, lax.rem(c + j, 2)))
        later(hv.at[0], s_h.at[n])
    loads[2].wait()
    for n in range(7):
        drain(hv.at[0], r_h.at[n])

    heads = hv[...].astype(jnp.float32).reshape(8, 2, 8, KV_RANK)
    part = jnp.zeros((64, owv.shape[1]), jnp.float32)
    for half in range(2):
        rows = heads[:, half].reshape(64, KV_RANK).astype(jnp.bfloat16)
        rows = jnp.dot(to_slot, rows, preferred_element_type=jnp.float32).astype(jnp.bfloat16)
        part = part + jnp.dot(
            rows, owv[pl.ds(KV_RANK * half, KV_RANK), :], preferred_element_type=jnp.float32
        )
    for s in range(16):
        rss[s] = window(part, s).astype(jnp.bfloat16)
    for n, (i, j) in enumerate(DEC):
        xx, zz = turn(x, i), turn(z, j)
        send(rss.at[4 * xx + zz], rsr.at[n], s_r.at[0], r_r.at[0], at(xx, y, zz, c))
    later(rsr, s_r.at[0])
    drain(rsr, r_r.at[0])
    hidden = resw[d] + rss[d].astype(jnp.float32)
    for n in range(15):
        hidden = hidden + rsr[n].astype(jnp.float32)
    odd = lax.rem(d, 2) == 1
    gains = jnp.broadcast_to(gain[...].astype(jnp.float32).reshape(1, -1), (8, owv.shape[1]))
    scaled = hidden * jnp.where(odd, window(gains, 1), window(gains, 0))
    twice = (
        (lax.broadcasted_iota(jnp.int32, (16, 256), 0) < 8)
        & (lax.broadcasted_iota(jnp.int32, (16, 256), 1) < 128)
        & odd
    )
    squares = jnp.sum(jnp.where(twice, 0.0, hidden * hidden), axis=1, keepdims=True)
    squares = squares + jnp.concatenate([squares[8:], squares[:8]], axis=0)
    first = squares.astype(jnp.bfloat16).astype(jnp.float32)
    second = (squares - first).astype(jnp.bfloat16).astype(jnp.float32)
    third = squares - first - second
    agb[d, :, pl.ds(0, 256)] = scaled.astype(jnp.bfloat16)
    agb[d, :, pl.ds(256, 128)] = jnp.where(
        lane16 == 0, first, jnp.where(lane16 == 1, second, third)
    ).astype(jnp.bfloat16)
    for n, (i, j) in enumerate(DEC):
        send(agb.at[d], agb.at[d], s_a.at[n], r_a.at[n], at(turn(x, i), y, turn(z, j), c))
        later(agb.at[0], s_a.at[n])
    for n in range(15):
        drain(agb.at[0], r_a.at[n])
    gathered = agb[...].astype(jnp.float32).reshape(8, 2, 2, 8, 384)
    squares = sum(
        gathered[:, h, 0, :, 256 + n:257 + n] for h in range(2) for n in range(3)
    )
    sqs[...] = jnp.broadcast_to(squares, (8, 8, 128))
    for n, (i, j) in enumerate(PRE):
        yy, cc = turn(y, i), lax.rem(c + j, 2)
        send(sqs.at[2 * yy + cc], sqr.at[n], s_s.at[0], r_s.at[0], at(x, yy, z, cc))
    later(sqr, s_s.at[0])
    scaled = jnp.concatenate(
        [
            gathered[:, 0, 0, :, 0:256].reshape(64, 256),
            gathered[:, 0, 1, :, 0:256].reshape(64, 256),
            gathered[:, 1, 0, :, 128:256].reshape(64, 128),
            gathered[:, 1, 1, :, 0:256].reshape(64, 256),
        ],
        axis=1,
    ).astype(jnp.bfloat16)

    wide = HALF // CHUNKS

    def join_cores(i):
        lanes = pl.ds(wide * i, wide)
        drain(lr.at[:, :, lanes], r_c.at[i])
        ls[c, :, :, lanes] = (
            ls[c, :, :, lanes].astype(jnp.float32) + lr[:, :, lanes].astype(jnp.float32)
        ).astype(jnp.bfloat16)
        for step in (1, 2, 3):
            yy = turn(y, step)
            send(
                ls.at[c, yy, :, lanes], lb.at[step - 1, :, lanes],
                s_y.at[i], r_y.at[i], at(x, yy, z, c),
            )
        later(lb.at[:, :, lanes], s_y.at[i])

    loads[3].wait()
    for i in range(CHUNKS):
        for half in range(2):
            start = HALF * half + wide * i
            count = min(wide, vocab - start)
            product = lax.dot_general(
                scaled, lmv[pl.ds(start, count), :], (((1,), (1,)), ((), ())),
                preferred_element_type=jnp.float32,
            ).reshape(8, 8, count).astype(jnp.bfloat16)
            for q in range(8):
                ls[q % 2, q // 2, pl.ds(8 * half, 8), pl.ds(wide * i, count)] = product[q]
        lanes = pl.ds(wide * i, wide)
        send(
            ls.at[1 - c, :, :, lanes], lr.at[:, :, lanes],
            s_c.at[i], r_c.at[i], at(x, y, z, 1 - c),
        )
        later(lr.at[:, :, lanes], s_c.at[i])
        if i > 0:
            join_cores(i - 1)
    join_cores(CHUNKS - 1)

    drain(sqr, r_s.at[0])
    norm = sqs[p]
    for n in range(7):
        norm = norm + sqr[n]
    norm = lax.rsqrt(norm[:, 0:1] / D + 1e-06)
    for i in range(CHUNKS):
        drain(lb.at[:, :, pl.ds(wide * i, wide)], r_y.at[i])
    logits = ls[c, y].astype(jnp.float32)
    for n in range(3):
        logits = logits + lb[n].astype(jnp.float32)
    low, high = logits[:8] * norm, logits[8:] * norm

    column = lax.broadcasted_iota(jnp.int32, (8, HALF), 1)
    high = jnp.where(column < vocab - HALF, high, FILL)
    slot_rows = lax.broadcasted_iota(jnp.int32, (8, 64), 0) + 8 * p
    token = jnp.sum(jnp.where(slots[...] == slot_rows, toks[...], 0), axis=1, keepdims=True)
    token = token - d * vocab
    picked = jnp.sum(jnp.where(column == token, low, 0.0), axis=1, keepdims=True) + jnp.sum(
        jnp.where((column + HALF == token) & (column < vocab - HALF), high, 0.0),
        axis=1, keepdims=True,
    )
    top = jnp.maximum(
        jnp.max(low, axis=1, keepdims=True), jnp.max(high, axis=1, keepdims=True)
    )
    total = jnp.sum(jnp.exp(low - top), axis=1, keepdims=True) + jnp.sum(
        jnp.exp(high - top), axis=1, keepdims=True
    )
    lane8 = lax.broadcasted_iota(jnp.int32, (8, 128), 1)
    mine = jnp.where(lane8 == 0, top, jnp.where(lane8 == 1, total, picked))
    sms[...] = mine
    for n, (i, j) in enumerate(DEC):
        send(sms, smr.at[n], s_m.at[0], r_m.at[0], at(turn(x, i), y, turn(z, j), c))
    later(smr, s_m.at[0])
    drain(smr, r_m.at[0])
    others = smr[...]
    best = jnp.maximum(jnp.max(others[:, :, 0:1], axis=0), top)
    total = total * jnp.exp(top - best) + jnp.sum(
        others[:, :, 1:2] * jnp.exp(others[:, :, 0:1] - best[None]), axis=0
    )
    picked = picked + jnp.sum(others[:, :, 2:3], axis=0)
    normalizer = best + jnp.log(total)
    out[:, pl.ds(0, HALF)] = low - normalizer
    out[:, pl.ds(HALF, vocab - HALF)] = (high - normalizer)[:, : vocab - HALF]
    square = lax.broadcasted_iota(jnp.int32, (8, 8), 0) == lax.broadcasted_iota(
        jnp.int32, (8, 8), 1
    )
    tgt[...] = jnp.sum(jnp.where(square, picked - normalizer, 0.0), axis=0, keepdims=True)

    finish()


def body(
    latent_cache, query, new_latent, lengths, slot_of, token_ids,
    latent_value_weight, out_weight, residual, norm_gain, lm_weight,
):
    columns, vocab = lm_weight.shape
    bf16, f32 = jnp.bfloat16, jnp.float32
    vmem = pl.BlockSpec(memory_space=pltpu.VMEM)
    anywhere = pl.BlockSpec(memory_space=pl.ANY)
    smem = pl.BlockSpec(memory_space=pltpu.SMEM)
    dma = pltpu.SemaphoreType.DMA
    logprobs, target = pl.pallas_call(
        kernel,
        out_shape=(
            jax.ShapeDtypeStruct((8, vocab), f32),
            jax.ShapeDtypeStruct((1, 8), f32),
        ),
        in_specs=[smem, anywhere, anywhere, vmem, vmem, vmem, vmem, vmem,
                  anywhere, anywhere, anywhere],
        out_specs=(vmem, vmem),
        scratch_shapes=[
            pltpu.VMEM((4, 2, 512, WIDTH), bf16),
            pltpu.VMEM((4, 4, 4, 16, WIDTH), bf16),
            pltpu.VMEM((4, 4, 4, 16, KV_RANK + EXTRA), bf16),
            pltpu.VMEM((4, 4, 16, KV_RANK + EXTRA), bf16),
            pltpu.VMEM((4, 3, 4, 16, KV_RANK + EXTRA), bf16),
            pltpu.VMEM((4, 4, 16, KV_RANK + EXTRA), bf16),
            pltpu.VMEM((8, KV_RANK, VHEAD), bf16),
            pltpu.VMEM((1024, columns), bf16),
            pltpu.VMEM((vocab, columns), bf16),
            pltpu.VMEM((64, WIDTH), bf16),
            pltpu.VMEM((KV_RANK // 128, 64, 128), f32),
            pltpu.VMEM((8, 16, 512), bf16),
            pltpu.VMEM((16, 16, 256), f32),
            pltpu.VMEM((16, 16, 256), bf16),
            pltpu.VMEM((15, 16, 256), bf16),
            pltpu.VMEM((16, 16, 384), bf16),
            pltpu.VMEM((8, 8, 128), f32),
            pltpu.VMEM((7, 8, 128), f32),
            pltpu.VMEM((2, 4, 16, HALF), bf16),
            pltpu.VMEM((4, 16, HALF), bf16),
            pltpu.VMEM((3, 16, HALF), bf16),
            pltpu.VMEM((8, 128), f32),
            pltpu.VMEM((15, 8, 128), f32),
            dma((4,)), dma((4,)), dma((4,)), dma((4,)), dma((4,)), dma((4,)), dma((4,)), dma((4,)), dma((4,)), dma((4,)),
            dma((4,)),
            dma((7,)), dma((7,)), dma((1,)), dma((1,)), dma((15,)), dma((15,)),
            dma((1,)), dma((1,)), dma((CHUNKS,)), dma((CHUNKS,)), dma((CHUNKS,)),
            dma((CHUNKS,)), dma((1,)), dma((1,)),
        ],
        name="decode_step",
        compiler_params=pltpu.CompilerParams(
            collective_id=0, has_side_effects=True, vmem_limit_bytes=56 << 20
        ),
    )(
        lengths,
        latent_cache,
        query.reshape(-1, WIDTH),
        new_latent,
        slot_of.reshape(1, -1),
        token_ids.reshape(1, -1),
        residual,
        norm_gain,
        latent_value_weight,
        out_weight,
        lm_weight.T,
    )
    return logprobs, target.reshape(8)


def solution(mesh):
    return jax.shard_map(
        body,
        mesh=mesh,
        in_specs=(
            P(None, ("dec", "pre"), None),
            P(None, "dec", None),
            P(),
            P(),
            P(),
            P(),
            P("dec", None, None),
            P("dec", "pre"),
            P(None, "pre"),
            P("pre"),
            P("pre", "dec"),
        ),
        out_specs=(P("pre", "dec"), P("pre")),
        check_vma=False,
    )
```

```python
import functools

import jax
import jax.numpy as jnp
from jax import lax
from jax.experimental import pallas as pl
from jax.experimental.pallas import tpu as pltpu
from jax.sharding import PartitionSpec as P

KV_RANK = 512
ROPE = 64
VHEAD = 128
D = 7168
WIDTH = KV_RANK + ROPE
MESH = pl.DeviceIdType.MESH
FILL = -(2.0**100)
SCALE = (VHEAD + ROPE) ** (-0.5)
EXTRA = 128
HALF = 4096
CHUNKS = 4

PAIRS = ("x", "y", "y", "z")
EARLY = ("x", "z", "x", "z")
FIRST = ("z", "x", "z", "x")


def drain(ref, sem):
    pltpu.make_async_copy(ref, ref, sem).wait()


def kernel(
    lens, cache, query, newl, slots, toks, resid, gain, vw, ow, lm,
    out, tgt,
    kbuf, raw, rope, krope, qbuf, pout, pjoin, pmid, pin, vwv, owv, lmv, qown, lat, hv, resw, rss, rsr, agb,
    sqs, sqr, ls, lr, lb, sms, smr,
    s_k, r_k, s_o, r_o, s_q, r_q, s_v, r_v, s_p, r_p, s_j, r_j, l_w, s_h, r_h, s_r, r_r, s_a, r_a, s_s, r_s,
    s_c, r_c, s_y, r_y, s_m, r_m,
):
    p, d = lax.axis_index("pre"), lax.axis_index("dec")
    y, c = lax.div(p, 2), lax.rem(p, 2)
    x, z = lax.div(d, 4), lax.rem(d, 4)
    vocab = lm.shape[0]

    def at(xx, yy, zz, cc):
        return (2 * yy + cc, 4 * xx + zz)

    def turn(value, step):
        return lax.rem(value + step, 4)

    def send(src, dst, ssem, rsem, device):
        pltpu.make_async_remote_copy(
            src_ref=src, dst_ref=dst, send_sem=ssem, recv_sem=rsem,
            device_id=device, device_id_type=MESH,
        ).start()

    pending = []

    def later(ref, sem):
        pending.append(lambda: drain(ref, sem))

    def finish():
        for wait in pending:
            wait()

    def signal(device):
        pl.semaphore_signal(barrier, inc=1, device_id=device, device_id_type=MESH)

    DEC = [(i, j) for i in range(4) for j in range(4) if (i, j) != (0, 0)]
    PRE = [(i, j) for i in range(4) for j in range(2) if (i, j) != (0, 0)]

    barrier = pltpu.get_barrier_semaphore()
    for i, j in DEC:
        signal(at(turn(x, i), y, turn(z, j), c))
    for i, j in PRE:
        signal(at(x, turn(y, i), z, lax.rem(c + j, 2)))
    for i in (1, 2, 3):
        signal(at(turn(x, i), y, z, 1 - c))
        signal(at(x, y, turn(z, i), 1 - c))
    for i in (1, 2, 3):
        signal(at(y, turn(y, i), z, c))
        signal(at(x, turn(y, i), y, c))

    @pl.when(x != y)
    def _():
        signal(at(y, y, z, c))

    @pl.when(z != y)
    def _():
        signal(at(x, y, y, c))

    loads = [
        pltpu.make_async_copy(query.at[pl.ds(64 * p, 64)], qown, l_w.at[0]),
        pltpu.make_async_copy(vw, vwv, l_w.at[1]),
        pltpu.make_async_copy(ow, owv, l_w.at[2]),
        pltpu.make_async_copy(lm, lmv, l_w.at[3]),
        pltpu.make_async_copy(cache.at[:, :, pl.ds(KV_RANK, ROPE)], raw, l_w.at[4]),
    ]
    for n in (4, 0, 1, 2):
        loads[n].start()
    def half(j):
        down = lax.broadcasted_iota(jnp.int32, (ROPE, 2 * ROPE), 0) + ROPE * j
        right = lax.broadcasted_iota(jnp.int32, (ROPE, 2 * ROPE), 1)
        return (down == right).astype(jnp.float32).astype(jnp.bfloat16)

    halves = [half(0), half(1)]
    loads[4].wait()
    for n in range(4):
        keys = raw[pl.ds(16 * n, 16)].reshape(8, 2, 64, ROPE)
        both = sum(
            jnp.dot(
                keys[:, j].reshape(512, ROPE), halves[j], preferred_element_type=jnp.float32
            )
            for j in range(2)
        )
        rope[pl.ds(8 * n, 8)] = both.astype(jnp.bfloat16).reshape(8, 64, 2 * ROPE)

    pl.semaphore_wait(
        barrier,
        15 + 7 + 6 + 6 + (x != y).astype(jnp.int32) + (z != y).astype(jnp.int32),
    )

    def group_of(axis, xx, yy, zz, cc):
        return 2 * {"x": xx, "y": yy, "z": zz}[axis] + cc

    def send_cache(k, source, target, ssem, rsem):
        axis = PAIRS[k]
        mine = group_of(axis, x, y, z, c)
        for i, j in PRE:
            xx = turn(x, i) if axis == "x" else x
            yy = turn(y, i) if axis == "y" else y
            zz = turn(z, i) if axis == "z" else z
            cc = lax.rem(c + j, 2)
            send(
                source(group_of(axis, xx, yy, zz, cc)), target(mine),
                ssem.at[k], rsem.at[k], at(xx, yy, zz, cc),
            )
        pltpu.make_async_copy(source(mine), target(mine), rsem.at[k]).start()

    def send_latents(k):
        send_cache(
            k,
            lambda group: cache.at[pl.ds(8 * group + 2 * k, 2), :, pl.ds(0, KV_RANK)],
            lambda mine: kbuf.at[k, :, pl.ds(64 * mine, 64), :],
            s_k, r_k,
        )
        later(kbuf.at[k, :, pl.ds(0, 448), :], s_k.at[k])

    def send_ropes(k):
        send_cache(
            k,
            lambda group: rope.at[4 * group + k],
            lambda mine: krope.at[k, pl.ds(64 * mine, 64), :],
            s_o, r_o,
        )
        later(krope.at[k, pl.ds(0, 448), :], s_o.at[k])

    def along(axis, step):
        return (turn(x, step), z) if axis == "x" else (x, turn(z, step))

    def coordinate(axis):
        return x if axis == "x" else z

    def send_query(k):
        axis = PAIRS[k]
        block = qbuf.at[k, coordinate(FIRST[k]), coordinate(EARLY[k])]
        for i in (1, 2, 3):
            xx, zz = along(EARLY[k], i)
            send(
                query.at[pl.ds(64 * group_of(axis, xx, y, zz, c) + 16 * k, 16)], block,
                s_q.at[k], r_q.at[k], at(xx, y, zz, c),
            )
        pltpu.make_async_copy(
            query.at[pl.ds(64 * group_of(axis, x, y, z, c) + 16 * k, 16)], block, r_q.at[k]
        ).start()
        later(qbuf.at[k, 0, pl.ds(0, 3)], s_q.at[k])

    def pass_query(k):
        met = qbuf.at[k, coordinate(FIRST[k])]
        drain(met, r_q.at[k])
        for i in (1, 2, 3):
            xx, zz = along(FIRST[k], i)
            send(met, met, s_v.at[k], r_v.at[k], at(xx, y, zz, c))
        later(qbuf.at[k, pl.ds(0, 3)], s_v.at[k])

    send_latents(1)
    for k in range(4):
        send_query(k)
    send_ropes(1)
    for k in (0, 3, 2):
        send_latents(k)
        send_ropes(k)
    loads[3].start()

    for k in (1, 0, 3, 2):
        pass_query(k)

    def window(rows, n):
        left = 384 * (n % 2)
        block = rows[8 * (n // 2):8 * (n // 2) + 8]
        return jnp.concatenate([block[:, left:left + 256], block[:, left + 256:left + 512]], axis=0)

    loads[0].wait()
    row = lax.broadcasted_iota(jnp.int32, (64, 64), 0)
    col = lax.broadcasted_iota(jnp.int32, (64, 64), 1)
    pick = (col == 8 * p + (row >> 3)).astype(jnp.float32).astype(jnp.bfloat16)
    new_rows = jnp.dot(pick, newl[...], preferred_element_type=jnp.float32)
    own = jnp.sum(qown[...].astype(jnp.float32) * new_rows, axis=1, keepdims=True) * SCALE
    to_slot = (slots[...] == row).astype(jnp.float32).astype(jnp.bfloat16)
    resid_slot = jnp.dot(to_slot, resid[...], preferred_element_type=jnp.float32)
    for n in range(16):
        resw[n] = window(resid_slot, n)
    ls[:, :, :, pl.ds(HALF - 128, 128)] = jnp.zeros((2, 4, 16, 128), jnp.bfloat16)

    spot = lax.broadcasted_iota(jnp.int32, (1, 512), 1)
    lane = lax.broadcasted_iota(jnp.int32, (128, EXTRA), 1)
    lane16 = lax.broadcasted_iota(jnp.int32, (16, EXTRA), 1)

    def position(axis):
        slot, core, inner = spot >> 7, (spot >> 6) & 1, spot & 63
        xx = slot if axis == "x" else x
        yy = slot if axis == "y" else y
        zz = slot if axis == "z" else z
        return 64 * ((4 * xx + zz) * 8 + 2 * yy + core) + inner

    def attend(k):
        axis = PAIRS[k]
        drain(qbuf.at[k, pl.ds(0, 3)], r_v.at[k])
        spots = position(axis)
        group = group_of(axis, x, y, z, c)
        both = qbuf[k].astype(jnp.float32).reshape(16, 2, 8, WIDTH)
        queries = []
        for j in range(2):
            rows = both[:, j].reshape(128, WIDTH)
            turned = jnp.dot(
                rows[:, KV_RANK:].astype(jnp.bfloat16), halves[j],
                preferred_element_type=jnp.float32,
            )
            queries.append((rows[:, :KV_RANK].astype(jnp.bfloat16), turned.astype(jnp.bfloat16)))
        drain(krope.at[k], r_o.at[k])
        drain(kbuf.at[k], r_k.at[k])
        sums, extras = [], []
        for j in range(2):
            keys = kbuf[k, j]
            scores = (
                lax.dot_general(
                    queries[j][0], keys, (((1,), (1,)), ((), ())),
                    preferred_element_type=jnp.float32,
                )
                + lax.dot_general(
                    queries[j][1], krope[k], (((1,), (1,)), ((), ())),
                    preferred_element_type=jnp.float32,
                )
            ) * SCALE
            scores = jnp.where(spots < lens[8 * group + 2 * k + j], scores, FILL)
            top = jnp.max(scores, axis=1, keepdims=True)
            top = top.astype(jnp.bfloat16).astype(jnp.float32)
            weights = jnp.exp(scores - top)
            total = jnp.sum(weights, axis=1, keepdims=True)
            sums.append(
                jnp.dot(
                    weights.astype(jnp.bfloat16), keys,
                    preferred_element_type=jnp.float32,
                ).reshape(16, 8, KV_RANK)
            )
            high = total.astype(jnp.bfloat16).astype(jnp.float32)
            extra = jnp.where(lane == 0, top, jnp.where(lane == 1, high, total - high))
            extras.append(extra.reshape(16, 8, EXTRA))
        sums = jnp.concatenate(sums, axis=1).astype(jnp.bfloat16).reshape(4, 4, 16, KV_RANK)
        extras = jnp.concatenate(extras, axis=1).astype(jnp.bfloat16).reshape(4, 4, 16, EXTRA)
        for n in range(4):
            pout[k, n, :, :, pl.ds(0, KV_RANK)] = sums[n]
            pout[k, n, :, :, pl.ds(KV_RANK, EXTRA)] = extras[n]
        for i in (1, 2, 3):
            xx, zz = along(FIRST[k], i)
            send(
                pout.at[k, xx if FIRST[k] == "x" else zz], pmid.at[k, i - 1],
                s_p.at[k], r_p.at[k], at(xx, y, zz, c),
            )
        later(pmid.at[k], s_p.at[k])

    def joined(blocks, own=None):
        extra = [block[..., KV_RANK:].astype(jnp.float32) for block in blocks]
        tops = [part[..., 0:1] for part in extra]
        top = functools.reduce(jnp.maximum, tops)
        if own is not None:
            top = jnp.maximum(top, own)
        shrink = [jnp.exp(part - top) for part in tops]
        total = sum((part[..., 1:2] + part[..., 2:3]) * by for part, by in zip(extra, shrink))
        summed = sum(
            block[..., :KV_RANK].astype(jnp.float32) * by for block, by in zip(blocks, shrink)
        )
        return top, total, summed

    def join_first(k):
        axis, first = PAIRS[k], FIRST[k]
        drain(pmid.at[k], r_p.at[k])
        for n in range(4):
            blocks = [pout[k, coordinate(first), n]] + [pmid[k, i, n] for i in range(3)]
            top, total, summed = joined(blocks)
            high = total.astype(jnp.bfloat16).astype(jnp.float32)
            extra = jnp.where(lane16 == 0, top, jnp.where(lane16 == 1, high, total - high))
            pjoin[k, n, :, pl.ds(0, KV_RANK)] = summed.astype(jnp.bfloat16)
            pjoin[k, n, :, pl.ds(KV_RANK, EXTRA)] = extra.astype(jnp.bfloat16)
        yy = {"x": x, "y": y, "z": z}[axis]
        place = y if axis != "y" else (z if first == "x" else x)
        here = z if first == "x" else x
        for i in (1, 2, 3):
            other = turn(here, i)
            xx, zz = (x, other) if first == "x" else (other, z)
            send(
                pjoin.at[k, other], pin.at[k, place],
                s_j.at[k], r_j.at[k], at(xx, yy, zz, c),
            )
        later(pin.at[k, pl.ds(0, 3)], s_j.at[k])

        def keep():
            pltpu.make_async_copy(pjoin.at[k, here], pin.at[k, place], r_j.at[k]).start()

        if axis == "y":
            keep()
        else:
            pl.when(yy == y)(keep)

            @pl.when(yy != y)
            def _():
                send(
                    pjoin.at[k, here], pin.at[k, place],
                    s_j.at[k], r_j.at[k], at(x, yy, z, c),
                )

            def left():
                pl.when(yy != y)(lambda: drain(pin.at[k, 0], s_j.at[k]))

            pending.append(left)

    def join_last(k):
        drain(pin.at[k], r_j.at[k])
        blocks = [pin[k, n] for n in range(4)]
        own_k = own[16 * k:16 * k + 16]
        top, total, summed = joined(blocks, own_k)
        own_weight = jnp.exp(own_k - top)
        summed = summed + (
            own_weight.astype(jnp.bfloat16).astype(jnp.float32)
            * new_rows[16 * k:16 * k + 16, :KV_RANK]
        )
        summed = summed / (total + own_weight)
        for b in range(KV_RANK // 128):
            lat[b, pl.ds(16 * k, 16), :] = summed[:, 128 * b:128 * b + 128]

    attend(1)
    attend(0)
    join_first(1)
    attend(3)
    join_first(0)
    attend(2)
    join_first(3)
    for k in (1, 0):
        join_last(k)
    join_first(2)
    for k in (3, 2):
        join_last(k)

    loads[1].wait()
    values = []
    for f in range(8):
        rows = jnp.concatenate(
            [lat[b, pl.ds(f, 8, stride=8), :] for b in range(KV_RANK // 128)], axis=1
        ).astype(jnp.bfloat16)
        values.append(jnp.dot(rows, vwv[f], preferred_element_type=jnp.float32))
    packed = jnp.concatenate(
        [jnp.concatenate(values[:4], axis=1), jnp.concatenate(values[4:], axis=1)], axis=0
    )
    hv[p] = packed.astype(jnp.bfloat16)
    for n, (i, j) in enumerate(PRE):
        send(hv.at[p], hv.at[p], s_h.at[n], r_h.at[n], at(x, turn(y, i), z, lax.rem(c + j, 2)))
        later(hv.at[0], s_h.at[n])
    loads[2].wait()
    for n in range(7):
        drain(hv.at[0], r_h.at[n])

    heads = hv[...].astype(jnp.float32).reshape(8, 2, 8, KV_RANK)
    part = jnp.zeros((64, owv.shape[1]), jnp.float32)
    for half in range(2):
        rows = heads[:, half].reshape(64, KV_RANK).astype(jnp.bfloat16)
        rows = jnp.dot(to_slot, rows, preferred_element_type=jnp.float32).astype(jnp.bfloat16)
        part = part + jnp.dot(
            rows, owv[pl.ds(KV_RANK * half, KV_RANK), :], preferred_element_type=jnp.float32
        )
    for s in range(16):
        rss[s] = window(part, s).astype(jnp.bfloat16)
    for n, (i, j) in enumerate(DEC):
        xx, zz = turn(x, i), turn(z, j)
        send(rss.at[4 * xx + zz], rsr.at[n], s_r.at[0], r_r.at[0], at(xx, y, zz, c))
    later(rsr, s_r.at[0])
    drain(rsr, r_r.at[0])
    hidden = resw[d] + rss[d].astype(jnp.float32)
    for n in range(15):
        hidden = hidden + rsr[n].astype(jnp.float32)
    odd = lax.rem(d, 2) == 1
    gains = jnp.broadcast_to(gain[...].astype(jnp.float32).reshape(1, -1), (8, owv.shape[1]))
    scaled = hidden * jnp.where(odd, window(gains, 1), window(gains, 0))
    twice = (
        (lax.broadcasted_iota(jnp.int32, (16, 256), 0) < 8)
        & (lax.broadcasted_iota(jnp.int32, (16, 256), 1) < 128)
        & odd
    )
    squares = jnp.sum(jnp.where(twice, 0.0, hidden * hidden), axis=1, keepdims=True)
    squares = squares + jnp.concatenate([squares[8:], squares[:8]], axis=0)
    first = squares.astype(jnp.bfloat16).astype(jnp.float32)
    second = (squares - first).astype(jnp.bfloat16).astype(jnp.float32)
    third = squares - first - second
    agb[d, :, pl.ds(0, 256)] = scaled.astype(jnp.bfloat16)
    agb[d, :, pl.ds(256, 128)] = jnp.where(
        lane16 == 0, first, jnp.where(lane16 == 1, second, third)
    ).astype(jnp.bfloat16)
    for n, (i, j) in enumerate(DEC):
        send(agb.at[d], agb.at[d], s_a.at[n], r_a.at[n], at(turn(x, i), y, turn(z, j), c))
        later(agb.at[0], s_a.at[n])
    for n in range(15):
        drain(agb.at[0], r_a.at[n])
    gathered = agb[...].astype(jnp.float32).reshape(8, 2, 2, 8, 384)
    squares = sum(
        gathered[:, h, 0, :, 256 + n:257 + n] for h in range(2) for n in range(3)
    )
    sqs[...] = jnp.broadcast_to(squares, (8, 8, 128))
    for n, (i, j) in enumerate(PRE):
        yy, cc = turn(y, i), lax.rem(c + j, 2)
        send(sqs.at[2 * yy + cc], sqr.at[n], s_s.at[0], r_s.at[0], at(x, yy, z, cc))
    later(sqr, s_s.at[0])
    scaled = jnp.concatenate(
        [
            gathered[:, 0, 0, :, 0:256].reshape(64, 256),
            gathered[:, 0, 1, :, 0:256].reshape(64, 256),
            gathered[:, 1, 0, :, 128:256].reshape(64, 128),
            gathered[:, 1, 1, :, 0:256].reshape(64, 256),
        ],
        axis=1,
    ).astype(jnp.bfloat16)

    wide = HALF // CHUNKS

    def join_cores(i):
        lanes = pl.ds(wide * i, wide)
        drain(lr.at[:, :, lanes], r_c.at[i])
        ls[c, :, :, lanes] = (
            ls[c, :, :, lanes].astype(jnp.float32) + lr[:, :, lanes].astype(jnp.float32)
        ).astype(jnp.bfloat16)
        for step in (1, 2, 3):
            yy = turn(y, step)
            send(
                ls.at[c, yy, :, lanes], lb.at[step - 1, :, lanes],
                s_y.at[i], r_y.at[i], at(x, yy, z, c),
            )
        later(lb.at[:, :, lanes], s_y.at[i])

    loads[3].wait()
    for i in range(CHUNKS):
        for half in range(2):
            start = HALF * half + wide * i
            count = min(wide, vocab - start)
            product = lax.dot_general(
                scaled, lmv[pl.ds(start, count), :], (((1,), (1,)), ((), ())),
                preferred_element_type=jnp.float32,
            ).reshape(8, 8, count).astype(jnp.bfloat16)
            for q in range(8):
                ls[q % 2, q // 2, pl.ds(8 * half, 8), pl.ds(wide * i, count)] = product[q]
        lanes = pl.ds(wide * i, wide)
        send(
            ls.at[1 - c, :, :, lanes], lr.at[:, :, lanes],
            s_c.at[i], r_c.at[i], at(x, y, z, 1 - c),
        )
        later(lr.at[:, :, lanes], s_c.at[i])
        if i > 0:
            join_cores(i - 1)
    join_cores(CHUNKS - 1)

    drain(sqr, r_s.at[0])
    norm = sqs[p]
    for n in range(7):
        norm = norm + sqr[n]
    norm = lax.rsqrt(norm[:, 0:1] / D + 1e-06)
    for i in range(CHUNKS):
        drain(lb.at[:, :, pl.ds(wide * i, wide)], r_y.at[i])
    logits = ls[c, y].astype(jnp.float32)
    for n in range(3):
        logits = logits + lb[n].astype(jnp.float32)
    low, high = logits[:8] * norm, logits[8:] * norm

    column = lax.broadcasted_iota(jnp.int32, (8, HALF), 1)
    high = jnp.where(column < vocab - HALF, high, FILL)
    slot_rows = lax.broadcasted_iota(jnp.int32, (8, 64), 0) + 8 * p
    token = jnp.sum(jnp.where(slots[...] == slot_rows, toks[...], 0), axis=1, keepdims=True)
    token = token - d * vocab
    picked = jnp.sum(jnp.where(column == token, low, 0.0), axis=1, keepdims=True) + jnp.sum(
        jnp.where((column + HALF == token) & (column < vocab - HALF), high, 0.0),
        axis=1, keepdims=True,
    )
    top = jnp.maximum(
        jnp.max(low, axis=1, keepdims=True), jnp.max(high, axis=1, keepdims=True)
    )
    total = jnp.sum(jnp.exp(low - top), axis=1, keepdims=True) + jnp.sum(
        jnp.exp(high - top), axis=1, keepdims=True
    )
    lane8 = lax.broadcasted_iota(jnp.int32, (8, 128), 1)
    mine = jnp.where(lane8 == 0, top, jnp.where(lane8 == 1, total, picked))
    sms[...] = mine
    for n, (i, j) in enumerate(DEC):
        send(sms, smr.at[n], s_m.at[0], r_m.at[0], at(turn(x, i), y, turn(z, j), c))
    later(smr, s_m.at[0])
    drain(smr, r_m.at[0])
    others = smr[...]
    best = jnp.maximum(jnp.max(others[:, :, 0:1], axis=0), top)
    total = total * jnp.exp(top - best) + jnp.sum(
        others[:, :, 1:2] * jnp.exp(others[:, :, 0:1] - best[None]), axis=0
    )
    picked = picked + jnp.sum(others[:, :, 2:3], axis=0)
    normalizer = best + jnp.log(total)
    out[:, pl.ds(0, HALF)] = low - normalizer
    out[:, pl.ds(HALF, vocab - HALF)] = (high - normalizer)[:, : vocab - HALF]
    square = lax.broadcasted_iota(jnp.int32, (8, 8), 0) == lax.broadcasted_iota(
        jnp.int32, (8, 8), 1
    )
    tgt[...] = jnp.sum(jnp.where(square, picked - normalizer, 0.0), axis=0, keepdims=True)

    finish()


def body(
    latent_cache, query, new_latent, lengths, slot_of, token_ids,
    latent_value_weight, out_weight, residual, norm_gain, lm_weight,
):
    columns, vocab = lm_weight.shape
    bf16, f32 = jnp.bfloat16, jnp.float32
    vmem = pl.BlockSpec(memory_space=pltpu.VMEM)
    anywhere = pl.BlockSpec(memory_space=pl.ANY)
    smem = pl.BlockSpec(memory_space=pltpu.SMEM)
    dma = pltpu.SemaphoreType.DMA
    logprobs, target = pl.pallas_call(
        kernel,
        out_shape=(
            jax.ShapeDtypeStruct((8, vocab), f32),
            jax.ShapeDtypeStruct((1, 8), f32),
        ),
        in_specs=[smem, anywhere, anywhere, vmem, vmem, vmem, vmem, vmem,
                  anywhere, anywhere, anywhere],
        out_specs=(vmem, vmem),
        scratch_shapes=[
            pltpu.VMEM((4, 2, 512, KV_RANK), bf16),
            pltpu.VMEM((64, 64, ROPE), bf16),
            pltpu.VMEM((32, 64, 2 * ROPE), bf16),
            pltpu.VMEM((4, 512, 2 * ROPE), bf16),
            pltpu.VMEM((4, 4, 4, 16, WIDTH), bf16),
            pltpu.VMEM((4, 4, 4, 16, KV_RANK + EXTRA), bf16),
            pltpu.VMEM((4, 4, 16, KV_RANK + EXTRA), bf16),
            pltpu.VMEM((4, 3, 4, 16, KV_RANK + EXTRA), bf16),
            pltpu.VMEM((4, 4, 16, KV_RANK + EXTRA), bf16),
            pltpu.VMEM((8, KV_RANK, VHEAD), bf16),
            pltpu.VMEM((1024, columns), bf16),
            pltpu.VMEM((vocab, columns), bf16),
            pltpu.VMEM((64, WIDTH), bf16),
            pltpu.VMEM((KV_RANK // 128, 64, 128), f32),
            pltpu.VMEM((8, 16, 512), bf16),
            pltpu.VMEM((16, 16, 256), f32),
            pltpu.VMEM((16, 16, 256), bf16),
            pltpu.VMEM((15, 16, 256), bf16),
            pltpu.VMEM((16, 16, 384), bf16),
            pltpu.VMEM((8, 8, 128), f32),
            pltpu.VMEM((7, 8, 128), f32),
            pltpu.VMEM((2, 4, 16, HALF), bf16),
            pltpu.VMEM((4, 16, HALF), bf16),
            pltpu.VMEM((3, 16, HALF), bf16),
            pltpu.VMEM((8, 128), f32),
            pltpu.VMEM((15, 8, 128), f32),
            dma((4,)), dma((4,)), dma((4,)), dma((4,)), dma((4,)), dma((4,)), dma((4,)), dma((4,)), dma((4,)), dma((4,)), dma((4,)), dma((4,)),
            dma((5,)),
            dma((7,)), dma((7,)), dma((1,)), dma((1,)), dma((15,)), dma((15,)),
            dma((1,)), dma((1,)), dma((CHUNKS,)), dma((CHUNKS,)), dma((CHUNKS,)),
            dma((CHUNKS,)), dma((1,)), dma((1,)),
        ],
        name="decode_step",
        compiler_params=pltpu.CompilerParams(
            collective_id=0, has_side_effects=True, vmem_limit_bytes=56 << 20
        ),
    )(
        lengths,
        latent_cache,
        query.reshape(-1, WIDTH),
        new_latent,
        slot_of.reshape(1, -1),
        token_ids.reshape(1, -1),
        residual,
        norm_gain,
        latent_value_weight,
        out_weight,
        lm_weight.T,
    )
    return logprobs, target.reshape(8)


def solution(mesh):
    return jax.shard_map(
        body,
        mesh=mesh,
        in_specs=(
            P(None, ("dec", "pre"), None),
            P(None, "dec", None),
            P(),
            P(),
            P(),
            P(),
            P("dec", None, None),
            P("dec", "pre"),
            P(None, "pre"),
            P("pre"),
            P("pre", "dec"),
        ),
        out_specs=(P("pre", "dec"), P("pre")),
        check_vma=False,
    )
```

```python
import functools

import jax
import jax.numpy as jnp
from jax import lax
from jax.experimental import pallas as pl
from jax.experimental.pallas import tpu as pltpu
from jax.sharding import PartitionSpec as P

KV_RANK = 512
ROPE = 64
VHEAD = 128
D = 7168
WIDTH = KV_RANK + ROPE
MESH = pl.DeviceIdType.MESH
FILL = -(2.0**100)
SCALE = (VHEAD + ROPE) ** (-0.5)
EXTRA = 128
HALF = 4096
CHUNKS = 4

PAIRS = ("x", "y", "y", "z")
FIRST_PAIR = 1
LAST = 2
EARLY = ("x", "z", "x", "z")
FIRST = ("z", "x", "z", "x")


def drain(ref, sem):
    pltpu.make_async_copy(ref, ref, sem).wait()


def kernel(
    lens_in, cache, query, newl_in, slots_in, toks_in, resid_in, gain_in, vw, ow, lm,
    out, tail,
    lens, newl, slots, toks, resid, gain, raws, kbuf, raw, rope, krope, qbuf, pout, pjoin, pmid, pin, vwv, owv, lmv, qown, lat, hv, resw, rss, rsr, agb,
    sqs, sqr, ls, lr, lb, sms, smr,
    s_k, r_k, s_o, r_o, s_q, r_q, s_v, r_v, s_p, r_p, s_j, r_j, l_w, s_h, r_h, s_r, r_r, s_a, r_a, s_s, r_s,
    s_c, r_c, s_y, r_y, s_m, r_m,
):
    p, d = lax.axis_index("pre"), lax.axis_index("dec")
    y, c = lax.div(p, 2), lax.rem(p, 2)
    x, z = lax.div(d, 4), lax.rem(d, 4)
    vocab = lm.shape[0]

    def at(xx, yy, zz, cc):
        return (2 * yy + cc, 4 * xx + zz)

    def turn(value, step):
        return lax.rem(value + step, 4)

    def send(src, dst, ssem, rsem, device):
        pltpu.make_async_remote_copy(
            src_ref=src, dst_ref=dst, send_sem=ssem, recv_sem=rsem,
            device_id=device, device_id_type=MESH,
        ).start()

    pending, known = [], set()

    def later(ref, sem):
        pending.append(lambda: drain(ref, sem))

    def once(key, wait):
        if key not in known:
            known.add(key)
            pending.append(wait)

    def finish():
        for wait in pending:
            wait()

    def signal(device):
        pl.semaphore_signal(barrier, inc=1, device_id=device, device_id_type=MESH)

    DEC = [(i, j) for i in range(4) for j in range(4) if (i, j) != (0, 0)]
    PRE = [(i, j) for i in range(4) for j in range(2) if (i, j) != (0, 0)]

    loads = [
        pltpu.make_async_copy(query.at[pl.ds(64 * p, 64)], qown, l_w.at[0]),
        pltpu.make_async_copy(vw, vwv, l_w.at[1]),
        pltpu.make_async_copy(ow, owv, l_w.at[2]),
        pltpu.make_async_copy(lm, lmv, l_w.at[3]),
        pltpu.make_async_copy(cache.at[:, :, pl.ds(KV_RANK, ROPE)], raw, l_w.at[4]),
    ]
    barrier = pltpu.get_barrier_semaphore()
    for i, j in DEC:
        signal(at(turn(x, i), y, turn(z, j), c))
    for i, j in PRE:
        signal(at(x, turn(y, i), z, lax.rem(c + j, 2)))
    for i in (1, 2, 3):
        signal(at(turn(x, i), y, z, 1 - c))
        signal(at(x, y, turn(z, i), 1 - c))
    for i in (1, 2, 3):
        signal(at(y, turn(y, i), z, c))
        signal(at(x, turn(y, i), y, c))

    @pl.when(x != y)
    def _():
        signal(at(y, y, z, c))

    @pl.when(z != y)
    def _():
        signal(at(x, y, y, c))

    small = [
        pltpu.make_async_copy(src, dst, l_w.at[5 + n])
        for n, (src, dst) in enumerate([
            (newl_in, newl), (slots_in, slots), (toks_in, toks), (resid_in, resid),
            (gain_in, gain), (lens_in, lens),
        ])
    ]
    loads[4].start()
    loads[0].start()
    for load in small:
        load.start()
    loads[1].start()
    loads[2].start()

    pl.semaphore_wait(
        barrier,
        15 + 7 + 6 + 6 + (x != y).astype(jnp.int32) + (z != y).astype(jnp.int32),
    )

    def group_of(axis, xx, yy, zz, cc):
        return 2 * {"x": xx, "y": yy, "z": zz}[axis] + cc

    def send_cache(k, source, target, ssem, rsem):
        axis = PAIRS[k]
        mine = group_of(axis, x, y, z, c)
        for i, j in PRE:
            xx = turn(x, i) if axis == "x" else x
            yy = turn(y, i) if axis == "y" else y
            zz = turn(z, i) if axis == "z" else z
            cc = lax.rem(c + j, 2)
            send(
                source(group_of(axis, xx, yy, zz, cc)), target(mine),
                ssem.at[k], rsem.at[k], at(xx, yy, zz, cc),
            )
        pltpu.make_async_copy(source(mine), target(mine), rsem.at[k]).start()

    def send_latents(k, core):
        axis = PAIRS[k]
        target = kbuf.at[k, :, pl.ds(64 * group_of(axis, x, y, z, c), 64), :]

        def source(xx, yy, zz, cc):
            first = 8 * group_of(axis, xx, yy, zz, cc) + 2 * k
            return cache.at[pl.ds(first, 2), :, pl.ds(0, KV_RANK)]

        for i in (1, 2, 3):
            xx = turn(x, i) if axis == "x" else x
            yy = turn(y, i) if axis == "y" else y
            zz = turn(z, i) if axis == "z" else z
            send(
                source(xx, yy, zz, core), target, s_k.at[k + 4 * core], r_k.at[k],
                at(xx, yy, zz, core),
            )
        if core == 0:
            send(source(x, y, z, 1 - c), target, s_k.at[k], r_k.at[k], at(x, y, z, 1 - c))
            pltpu.make_async_copy(source(x, y, z, c), target, r_k.at[k]).start()

    def latents_left(k, core):
        drain(kbuf.at[k, :, pl.ds(0, 192 if core else 256), :], s_k.at[k + 4 * core])

    def send_ropes(k):
        send_cache(
            k,
            lambda group: rope.at[4 * group + k],
            lambda mine: krope.at[k, pl.ds(64 * mine, 64), :],
            s_o, r_o,
        )
        later(krope.at[k, pl.ds(0, 448), :], s_o.at[k])

    def along(axis, step):
        return (turn(x, step), z) if axis == "x" else (x, turn(z, step))

    def coordinate(axis):
        return x if axis == "x" else z

    def send_query(k):
        axis = PAIRS[k]
        met = qbuf.at[k, coordinate(FIRST[k])]
        rows = query.at[pl.ds(64 * group_of(axis, x, y, z, c) + 16 * k, 16)]
        for i in (1, 2, 3):
            xx, zz = along(EARLY[k], i)
            send(
                query.at[pl.ds(64 * group_of(axis, xx, y, zz, c) + 16 * k, 16)], met.at[4 - i],
                s_q.at[k], r_q.at[k], at(xx, y, zz, c),
            )
        for i in (1, 2, 3):
            xx, zz = along(FIRST[k], i)
            send(rows, met.at[0], s_v.at[k], r_v.at[k], at(xx, y, zz, c))
        pltpu.make_async_copy(rows, met.at[0], r_q.at[k]).start()
        later(qbuf.at[k, 0, pl.ds(0, 3)], s_q.at[k])

    def pass_query(k):
        met = qbuf.at[k, coordinate(FIRST[k])]
        drain(met, r_q.at[k])
        for i in (1, 2, 3):
            xx, zz = along(FIRST[k], i)
            send(
                met.at[pl.ds(1, 3)], met.at[pl.ds(1, 3)], s_v.at[k], r_v.at[k],
                at(xx, y, zz, c),
            )
        later(qbuf.at[k, pl.ds(0, 3)], s_v.at[k])

    for k in (1, 0, 3, 2):
        send_query(k)
    for core in range(2):
        send_latents(FIRST_PAIR, core)
    def half(j):
        down = lax.broadcasted_iota(jnp.int32, (ROPE, 2 * ROPE), 0) + ROPE * j
        right = lax.broadcasted_iota(jnp.int32, (ROPE, 2 * ROPE), 1)
        return (down == right).astype(jnp.float32).astype(jnp.bfloat16)

    halves = [half(0), half(1)]
    loads[4].wait()
    for n in range(4):
        keys = raw[pl.ds(16 * n, 16)].reshape(8, 2, 64, ROPE)
        both = sum(
            jnp.dot(
                keys[:, j].reshape(512, ROPE), halves[j], preferred_element_type=jnp.float32
            )
            for j in range(2)
        )
        rope[pl.ds(8 * n, 8)] = both.astype(jnp.bfloat16).reshape(8, 64, 2 * ROPE)
    for k in (1, 0, 3, 2):
        send_ropes(k)
    loads[3].start()

    for k in (1, 0, 3, 2):
        pass_query(k)
    for k in (0, 3):
        send_latents(k, 0)

    def window(rows, n):
        left = 384 * (n % 2)
        block = rows[8 * (n // 2):8 * (n // 2) + 8]
        return jnp.concatenate([block[:, left:left + 256], block[:, left + 256:left + 512]], axis=0)

    loads[0].wait()
    for load in small:
        load.wait()
    row = lax.broadcasted_iota(jnp.int32, (64, 64), 0)
    col = lax.broadcasted_iota(jnp.int32, (64, 64), 1)
    pick = (col == 8 * p + (row >> 3)).astype(jnp.float32).astype(jnp.bfloat16)
    new_rows = jnp.dot(pick, newl[...], preferred_element_type=jnp.float32)
    own = jnp.sum(qown[...].astype(jnp.float32) * new_rows, axis=1, keepdims=True) * SCALE
    to_slot = (slots[...] == row).astype(jnp.float32).astype(jnp.bfloat16)
    resid_slot = jnp.dot(to_slot, resid[...], preferred_element_type=jnp.float32)
    for n in range(16):
        resw[n] = window(resid_slot, n)
    ls[:, :, :, pl.ds(HALF - 128, 128)] = jnp.zeros((2, 4, 16, 128), jnp.bfloat16)

    spot = lax.broadcasted_iota(jnp.int32, (1, 512), 1)
    lane = lax.broadcasted_iota(jnp.int32, (128, EXTRA), 1)
    lane16 = lax.broadcasted_iota(jnp.int32, (16, EXTRA), 1)

    def position(axis):
        slot, core, inner = spot >> 7, (spot >> 6) & 1, spot & 63
        xx = slot if axis == "x" else x
        yy = slot if axis == "y" else y
        zz = slot if axis == "z" else z
        return 64 * ((4 * xx + zz) * 8 + 2 * yy + core) + inner

    def queries_of(k):
        drain(qbuf.at[k, pl.ds(0, 3)], r_v.at[k])
        both = qbuf[k].astype(jnp.float32).reshape(16, 2, 8, WIDTH)
        queries = []
        for j in range(2):
            rows = both[:, j].reshape(128, WIDTH)
            turned = jnp.dot(
                rows[:, KV_RANK:].astype(jnp.bfloat16), halves[j],
                preferred_element_type=jnp.float32,
            )
            queries.append((rows[:, :KV_RANK].astype(jnp.bfloat16), turned.astype(jnp.bfloat16)))
        return queries

    def attend(k, queries=None):
        queries = queries or queries_of(k)
        axis = PAIRS[k]
        spots = position(axis)
        group = group_of(axis, x, y, z, c)
        drain(krope.at[k], r_o.at[k])
        drain(kbuf.at[k], r_k.at[k])
        sums, extras = [], []
        for j in range(2):
            keys = kbuf[k, j]
            scores = (
                lax.dot_general(
                    queries[j][0], keys, (((1,), (1,)), ((), ())),
                    preferred_element_type=jnp.float32,
                )
                + lax.dot_general(
                    queries[j][1], krope[k], (((1,), (1,)), ((), ())),
                    preferred_element_type=jnp.float32,
                )
            ) * SCALE
            scores = jnp.where(spots < lens[8 * group + 2 * k + j], scores, FILL)
            top = jnp.max(scores, axis=1, keepdims=True)
            top = top.astype(jnp.bfloat16).astype(jnp.float32)
            weights = jnp.exp(scores - top)
            total = jnp.sum(weights, axis=1, keepdims=True)
            sums.append(
                jnp.dot(
                    weights.astype(jnp.bfloat16), keys,
                    preferred_element_type=jnp.float32,
                ).reshape(16, 8, KV_RANK)
            )
            high = total.astype(jnp.bfloat16).astype(jnp.float32)
            extra = jnp.where(lane == 0, top, jnp.where(lane == 1, high, total - high))
            extras.append(extra.reshape(16, 8, EXTRA))
        sums = jnp.concatenate(sums, axis=1).astype(jnp.bfloat16).reshape(4, 4, 16, KV_RANK)
        extras = jnp.concatenate(extras, axis=1).astype(jnp.bfloat16).reshape(4, 4, 16, EXTRA)
        for n in range(4):
            pout[k, n, :, :, pl.ds(0, KV_RANK)] = sums[n]
            pout[k, n, :, :, pl.ds(KV_RANK, EXTRA)] = extras[n]
        for i in (1, 2, 3):
            xx, zz = along(FIRST[k], i)
            send(
                pout.at[k, xx if FIRST[k] == "x" else zz], pmid.at[k, i - 1],
                s_p.at[k], r_p.at[k], at(xx, y, zz, c),
            )
        once((0, k), lambda: drain(pmid.at[k], s_p.at[k]))

    def joined(blocks, own=None):
        extra = [block[..., KV_RANK:].astype(jnp.float32) for block in blocks]
        tops = [part[..., 0:1] for part in extra]
        top = functools.reduce(jnp.maximum, tops)
        if own is not None:
            top = jnp.maximum(top, own)
        shrink = [jnp.exp(part - top) for part in tops]
        total = sum((part[..., 1:2] + part[..., 2:3]) * by for part, by in zip(extra, shrink))
        summed = sum(
            block[..., :KV_RANK].astype(jnp.float32) * by for block, by in zip(blocks, shrink)
        )
        return top, total, summed

    def join_first(k):
        axis, first = PAIRS[k], FIRST[k]
        drain(pmid.at[k], r_p.at[k])
        for n in range(4):
            blocks = [pout[k, coordinate(first), n]] + [pmid[k, i, n] for i in range(3)]
            top, total, summed = joined(blocks)
            high = total.astype(jnp.bfloat16).astype(jnp.float32)
            extra = jnp.where(lane16 == 0, top, jnp.where(lane16 == 1, high, total - high))
            pjoin[k, n, :, pl.ds(0, KV_RANK)] = summed.astype(jnp.bfloat16)
            pjoin[k, n, :, pl.ds(KV_RANK, EXTRA)] = extra.astype(jnp.bfloat16)
        yy = {"x": x, "y": y, "z": z}[axis]
        place = y if axis != "y" else (z if first == "x" else x)
        here = z if first == "x" else x
        for i in (1, 2, 3):
            other = turn(here, i)
            xx, zz = (x, other) if first == "x" else (other, z)
            send(
                pjoin.at[k, i], pin.at[k, place],
                s_j.at[k], r_j.at[k], at(xx, yy, zz, c),
            )
        once((1, k), lambda: drain(pin.at[k, pl.ds(0, 3)], s_j.at[k]))

        def keep():
            pltpu.make_async_copy(pjoin.at[k, 0], pin.at[k, place], r_j.at[k]).start()

        if axis == "y":
            keep()
        else:
            pl.when(yy == y)(keep)

            @pl.when(yy != y)
            def _():
                send(
                    pjoin.at[k, 0], pin.at[k, place],
                    s_j.at[k], r_j.at[k], at(x, yy, z, c),
                )

            def left():
                pl.when(yy != y)(lambda: drain(pin.at[k, 0], s_j.at[k]))

            once((2, k), left)

    def join_last(k):
        drain(pin.at[k], r_j.at[k])
        blocks = [pin[k, n] for n in range(4)]
        own_k = own[16 * k:16 * k + 16]
        top, total, summed = joined(blocks, own_k)
        own_weight = jnp.exp(own_k - top)
        summed = summed + (
            own_weight.astype(jnp.bfloat16).astype(jnp.float32)
            * new_rows[16 * k:16 * k + 16, :KV_RANK]
        )
        summed = summed / (total + own_weight)
        for b in range(KV_RANK // 128):
            lat[b, pl.ds(16 * k, 16), :] = summed[:, 128 * b:128 * b + 128]

    queries = queries_of(FIRST_PAIR)
    send_latents(LAST, 0)
    for core in range(2):
        latents_left(FIRST_PAIR, core)
    send_latents(LAST, 1)
    attend(FIRST_PAIR, queries)
    for k in (0, 3):
        latents_left(k, 0)
        send_latents(k, 1)

    @pl.when(c == 0)
    def _():
        attend(0)
        attend(3)
        join_first(1)
        attend(2)

    @pl.when(c == 1)
    def _():
        join_first(1)
        attend(0)
        attend(3)
        attend(2)

    for k in (0, 3, 2):
        join_first(k)
    latents_left(LAST, 0)
    for k in (0, 3, 2):
        latents_left(k, 1)
    for k in (1, 0, 3, 2):
        join_last(k)

    loads[1].wait()
    values = []
    for f in range(8):
        rows = jnp.concatenate(
            [lat[b, pl.ds(f, 8, stride=8), :] for b in range(KV_RANK // 128)], axis=1
        ).astype(jnp.bfloat16)
        values.append(jnp.dot(rows, vwv[f], preferred_element_type=jnp.float32))
    packed = jnp.concatenate(
        [jnp.concatenate(values[:4], axis=1), jnp.concatenate(values[4:], axis=1)], axis=0
    )
    hv[p] = packed.astype(jnp.bfloat16)
    for n, (i, j) in enumerate(PRE):
        send(hv.at[p], hv.at[p], s_h.at[n], r_h.at[n], at(x, turn(y, i), z, lax.rem(c + j, 2)))
        later(hv.at[0], s_h.at[n])
    loads[2].wait()
    for n in range(7):
        drain(hv.at[0], r_h.at[n])

    heads = hv[...].astype(jnp.float32).reshape(8, 2, 8, KV_RANK)
    part = jnp.zeros((64, owv.shape[1]), jnp.float32)
    for half in range(2):
        rows = heads[:, half].reshape(64, KV_RANK).astype(jnp.bfloat16)
        rows = jnp.dot(to_slot, rows, preferred_element_type=jnp.float32).astype(jnp.bfloat16)
        part = part + jnp.dot(
            rows, owv[pl.ds(KV_RANK * half, KV_RANK), :], preferred_element_type=jnp.float32
        )
    for s in range(16):
        rss[s] = window(part, s).astype(jnp.bfloat16)
    for n, (i, j) in enumerate(DEC):
        xx, zz = turn(x, i), turn(z, j)
        send(rss.at[4 * xx + zz], rsr.at[n], s_r.at[0], r_r.at[0], at(xx, y, zz, c))
    later(rsr, s_r.at[0])
    drain(rsr, r_r.at[0])
    hidden = resw[d] + rss[d].astype(jnp.float32)
    for n in range(15):
        hidden = hidden + rsr[n].astype(jnp.float32)
    odd = lax.rem(d, 2) == 1
    gains = jnp.broadcast_to(gain[...].astype(jnp.float32).reshape(1, -1), (8, owv.shape[1]))
    scaled = hidden * jnp.where(odd, window(gains, 1), window(gains, 0))
    twice = (
        (lax.broadcasted_iota(jnp.int32, (16, 256), 0) < 8)
        & (lax.broadcasted_iota(jnp.int32, (16, 256), 1) < 128)
        & odd
    )
    squares = jnp.sum(jnp.where(twice, 0.0, hidden * hidden), axis=1, keepdims=True)
    squares = squares + jnp.concatenate([squares[8:], squares[:8]], axis=0)
    first = squares.astype(jnp.bfloat16).astype(jnp.float32)
    second = (squares - first).astype(jnp.bfloat16).astype(jnp.float32)
    third = squares - first - second
    agb[d, :, pl.ds(0, 256)] = scaled.astype(jnp.bfloat16)
    agb[d, :, pl.ds(256, 128)] = jnp.where(
        lane16 == 0, first, jnp.where(lane16 == 1, second, third)
    ).astype(jnp.bfloat16)
    for n, (i, j) in enumerate(DEC):
        send(agb.at[d], agb.at[d], s_a.at[n], r_a.at[n], at(turn(x, i), y, turn(z, j), c))
        later(agb.at[0], s_a.at[n])
    for n in range(15):
        drain(agb.at[0], r_a.at[n])
    gathered = agb[...].astype(jnp.float32).reshape(8, 2, 2, 8, 384)
    squares = sum(
        gathered[:, h, 0, :, 256 + n:257 + n] for h in range(2) for n in range(3)
    )
    sqs[...] = jnp.broadcast_to(squares, (8, 8, 128))
    for n, (i, j) in enumerate(PRE):
        yy, cc = turn(y, i), lax.rem(c + j, 2)
        send(sqs.at[2 * yy + cc], sqr.at[n], s_s.at[0], r_s.at[0], at(x, yy, z, cc))
    later(sqr, s_s.at[0])
    scaled = jnp.concatenate(
        [
            gathered[:, 0, 0, :, 0:256].reshape(64, 256),
            gathered[:, 0, 1, :, 0:256].reshape(64, 256),
            gathered[:, 1, 0, :, 128:256].reshape(64, 128),
            gathered[:, 1, 1, :, 0:256].reshape(64, 256),
        ],
        axis=1,
    ).astype(jnp.bfloat16)

    wide = HALF // CHUNKS

    def join_cores(i):
        lanes = pl.ds(wide * i, wide)
        drain(lr.at[:, :, lanes], r_c.at[i])
        ls[c, :, :, lanes] = (
            ls[c, :, :, lanes].astype(jnp.float32) + lr[:, :, lanes].astype(jnp.float32)
        ).astype(jnp.bfloat16)
        for step in (1, 2, 3):
            yy = turn(y, step)
            send(
                ls.at[c, yy, :, lanes], lb.at[step - 1, :, lanes],
                s_y.at[i], r_y.at[i], at(x, yy, z, c),
            )
        later(lb.at[:, :, lanes], s_y.at[i])

    loads[3].wait()
    for i in range(CHUNKS):
        for half in range(2):
            start = HALF * half + wide * i
            count = min(wide, vocab - start)
            product = lax.dot_general(
                scaled, lmv[pl.ds(start, count), :], (((1,), (1,)), ((), ())),
                preferred_element_type=jnp.float32,
            ).reshape(8, 8, count).astype(jnp.bfloat16)
            for q in range(8):
                ls[q % 2, q // 2, pl.ds(8 * half, 8), pl.ds(wide * i, count)] = product[q]
        lanes = pl.ds(wide * i, wide)
        send(
            ls.at[1 - c, :, :, lanes], lr.at[:, :, lanes],
            s_c.at[i], r_c.at[i], at(x, y, z, 1 - c),
        )
        later(lr.at[:, :, lanes], s_c.at[i])
        if i > 0:
            join_cores(i - 1)
    join_cores(CHUNKS - 1)

    drain(sqr, r_s.at[0])
    norm = sqs[p]
    for n in range(7):
        norm = norm + sqr[n]
    norm = lax.rsqrt(norm[:, 0:1] / D + 1e-06)
    for i in range(CHUNKS):
        drain(lb.at[:, :, pl.ds(wide * i, wide)], r_y.at[i])
    logits = ls[c, y].astype(jnp.float32)
    for n in range(3):
        logits = logits + lb[n].astype(jnp.float32)
    low, high = logits[:8] * norm, logits[8:] * norm

    raws[:, pl.ds(0, HALF)] = low
    raws[:, pl.ds(HALF, vocab - HALF)] = high[:, : vocab - HALF]
    write = pltpu.make_async_copy(raws, out, l_w.at[0])
    write.start()

    column = lax.broadcasted_iota(jnp.int32, (8, HALF), 1)
    high = jnp.where(column < vocab - HALF, high, FILL)
    slot_rows = lax.broadcasted_iota(jnp.int32, (8, 64), 0) + 8 * p
    token = jnp.sum(jnp.where(slots[...] == slot_rows, toks[...], 0), axis=1, keepdims=True)
    token = token - d * vocab
    picked = jnp.sum(jnp.where(column == token, low, 0.0), axis=1, keepdims=True) + jnp.sum(
        jnp.where((column + HALF == token) & (column < vocab - HALF), high, 0.0),
        axis=1, keepdims=True,
    )
    top = jnp.maximum(
        jnp.max(low, axis=1, keepdims=True), jnp.max(high, axis=1, keepdims=True)
    )
    total = jnp.sum(jnp.exp(low - top), axis=1, keepdims=True) + jnp.sum(
        jnp.exp(high - top), axis=1, keepdims=True
    )
    lane8 = lax.broadcasted_iota(jnp.int32, (8, 128), 1)
    mine = jnp.where(lane8 == 0, top, jnp.where(lane8 == 1, total, picked))
    sms[...] = mine
    for n, (i, j) in enumerate(DEC):
        send(sms, smr.at[n], s_m.at[0], r_m.at[0], at(turn(x, i), y, turn(z, j), c))
    later(smr, s_m.at[0])
    drain(smr, r_m.at[0])
    others = smr[...]
    best = jnp.maximum(jnp.max(others[:, :, 0:1], axis=0), top)
    total = total * jnp.exp(top - best) + jnp.sum(
        others[:, :, 1:2] * jnp.exp(others[:, :, 0:1] - best[None]), axis=0
    )
    picked = picked + jnp.sum(others[:, :, 2:3], axis=0)
    normalizer = best + jnp.log(total)
    tail[...] = jnp.where(lane8 == 0, normalizer, picked - normalizer)
    write.wait()
    finish()


def finish_kernel(logits, tail, out, tgt):
    out[...] = logits[...] - tail[:, 0:1]
    square = lax.broadcasted_iota(jnp.int32, (8, 8), 0) == lax.broadcasted_iota(
        jnp.int32, (8, 8), 1
    )
    tgt[...] = jnp.sum(jnp.where(square, tail[:, 1:2], 0.0), axis=0, keepdims=True)


def body(
    latent_cache, query, new_latent, lengths, slot_of, token_ids,
    latent_value_weight, out_weight, residual, norm_gain, lm_weight,
):
    columns, vocab = lm_weight.shape
    bf16, f32 = jnp.bfloat16, jnp.float32
    vmem = pl.BlockSpec(memory_space=pltpu.VMEM)
    anywhere = pl.BlockSpec(memory_space=pl.ANY)
    dma = pltpu.SemaphoreType.DMA
    logits, tail = pl.pallas_call(
        kernel,
        out_shape=(
            jax.ShapeDtypeStruct((8, vocab), f32),
            jax.ShapeDtypeStruct((8, 128), f32),
        ),
        in_specs=[anywhere] * 11,
        out_specs=(anywhere, vmem),
        scratch_shapes=[
            pltpu.SMEM((64,), jnp.int32),
            pltpu.VMEM((64, WIDTH), bf16),
            pltpu.VMEM((1, 64), jnp.int32),
            pltpu.VMEM((1, 64), jnp.int32),
            pltpu.VMEM((64, columns), bf16),
            pltpu.VMEM((columns,), bf16),
            pltpu.VMEM((8, vocab), f32),
            pltpu.VMEM((4, 2, 512, KV_RANK), bf16),
            pltpu.VMEM((64, 64, ROPE), bf16),
            pltpu.VMEM((32, 64, 2 * ROPE), bf16),
            pltpu.VMEM((4, 512, 2 * ROPE), bf16),
            pltpu.VMEM((4, 4, 4, 16, WIDTH), bf16),
            pltpu.VMEM((4, 4, 4, 16, KV_RANK + EXTRA), bf16),
            pltpu.VMEM((4, 4, 16, KV_RANK + EXTRA), bf16),
            pltpu.VMEM((4, 3, 4, 16, KV_RANK + EXTRA), bf16),
            pltpu.VMEM((4, 4, 16, KV_RANK + EXTRA), bf16),
            pltpu.VMEM((8, KV_RANK, VHEAD), bf16),
            pltpu.VMEM((1024, columns), bf16),
            pltpu.VMEM((vocab, columns), bf16),
            pltpu.VMEM((64, WIDTH), bf16),
            pltpu.VMEM((KV_RANK // 128, 64, 128), f32),
            pltpu.VMEM((8, 16, 512), bf16),
            pltpu.VMEM((16, 16, 256), f32),
            pltpu.VMEM((16, 16, 256), bf16),
            pltpu.VMEM((15, 16, 256), bf16),
            pltpu.VMEM((16, 16, 384), bf16),
            pltpu.VMEM((8, 8, 128), f32),
            pltpu.VMEM((7, 8, 128), f32),
            pltpu.VMEM((2, 4, 16, HALF), bf16),
            pltpu.VMEM((4, 16, HALF), bf16),
            pltpu.VMEM((3, 16, HALF), bf16),
            pltpu.VMEM((8, 128), f32),
            pltpu.VMEM((15, 8, 128), f32),
            dma((8,)), dma((4,)), dma((4,)), dma((4,)), dma((4,)), dma((4,)), dma((4,)), dma((4,)),
            dma((4,)), dma((4,)), dma((4,)), dma((4,)),
            dma((11,)),
            dma((7,)), dma((7,)), dma((1,)), dma((1,)), dma((15,)), dma((15,)),
            dma((1,)), dma((1,)), dma((CHUNKS,)), dma((CHUNKS,)), dma((CHUNKS,)),
            dma((CHUNKS,)), dma((1,)), dma((1,)),
        ],
        name="decode_step",
        compiler_params=pltpu.CompilerParams(
            collective_id=0, has_side_effects=True, vmem_limit_bytes=56 << 20
        ),
    )(
        lengths,
        latent_cache,
        query.reshape(-1, WIDTH),
        new_latent,
        slot_of.reshape(1, -1),
        token_ids.reshape(1, -1),
        residual,
        norm_gain,
        latent_value_weight,
        out_weight,
        lm_weight.T,
    )
    logprobs, target = pl.pallas_call(
        finish_kernel,
        out_shape=(
            jax.ShapeDtypeStruct((8, vocab), f32),
            jax.ShapeDtypeStruct((1, 8), f32),
        ),
        name="log_probabilities",
    )(logits, tail)
    return logprobs, target.reshape(8)


def solution(mesh):
    return jax.shard_map(
        body,
        mesh=mesh,
        in_specs=(
            P(None, ("dec", "pre"), None),
            P(None, "dec", None),
            P(),
            P(),
            P(),
            P(),
            P("dec", None, None),
            P("dec", "pre"),
            P(None, "pre"),
            P("pre"),
            P("pre", "dec"),
        ),
        out_specs=(P("pre", "dec"), P("pre")),
        check_vma=False,
    )
```

```python
import functools

import jax
import jax.numpy as jnp
from jax import lax
from jax.experimental import pallas as pl
from jax.experimental.pallas import tpu as pltpu
from jax.sharding import PartitionSpec as P

KV_RANK = 512
ROPE = 64
VHEAD = 128
D = 7168
WIDTH = KV_RANK + ROPE
MESH = pl.DeviceIdType.MESH
FILL = -(2.0**100)
SCALE = (VHEAD + ROPE) ** (-0.5)
EXTRA = 128
HALF = 4096
CHUNKS = 4

PAIRS = ("x", "y", "y", "z")
FIRST_PAIR = 1
LAST = 2
EARLY = ("x", "z", "x", "z")
FIRST = ("z", "x", "z", "x")


def drain(ref, sem):
    pltpu.make_async_copy(ref, ref, sem).wait()


def kernel(
    lens_in, cache, query, newl_in, slots_in, toks_in, resid_in, gain_in, vw, ow, lm,
    out, tail,
    lens, newl, slots, toks, resid, gain, raws, kbuf, raw, rope, krope, qbuf, pout, pjoin, pmid, pin, vwv, owv, lmv, qown, lat, hv, resw, rss, rsr, agb,
    sqs, sqr, ls, lr, lb, sms, smr,
    s_k, r_k, s_o, r_o, s_q, r_q, s_v, r_v, s_p, r_p, s_j, r_j, l_w, s_h, r_h, s_r, r_r, s_a, r_a, s_s, r_s,
    s_c, r_c, s_y, r_y, s_m, r_m,
):
    p, d = lax.axis_index("pre"), lax.axis_index("dec")
    y, c = lax.div(p, 2), lax.rem(p, 2)
    x, z = lax.div(d, 4), lax.rem(d, 4)
    vocab = lm.shape[0]

    def at(xx, yy, zz, cc):
        return (2 * yy + cc, 4 * xx + zz)

    def turn(value, step):
        return lax.rem(value + step, 4)

    def send(src, dst, ssem, rsem, device):
        pltpu.make_async_remote_copy(
            src_ref=src, dst_ref=dst, send_sem=ssem, recv_sem=rsem,
            device_id=device, device_id_type=MESH,
        ).start()

    pending, known = [], set()

    def later(ref, sem):
        pending.append(lambda: drain(ref, sem))

    def once(key, wait):
        if key not in known:
            known.add(key)
            pending.append(wait)

    def finish():
        for wait in pending:
            wait()

    def signal(device):
        pl.semaphore_signal(barrier, inc=1, device_id=device, device_id_type=MESH)

    hops = (0, 1, 2, 1)
    DEC = [(i, j) for i in range(4) for j in range(4) if (i, j) != (0, 0)]
    DEC.sort(key=lambda ij: -hops[ij[0]] - hops[ij[1]])
    PRE = [(i, j) for i in range(4) for j in range(2) if (i, j) != (0, 0)]
    PRE.sort(key=lambda ij: -hops[ij[0]] - ij[1])

    loads = [
        pltpu.make_async_copy(query.at[pl.ds(64 * p, 64)], qown, l_w.at[0]),
        pltpu.make_async_copy(vw, vwv, l_w.at[1]),
        pltpu.make_async_copy(ow, owv, l_w.at[2]),
        pltpu.make_async_copy(lm, lmv, l_w.at[3]),
        pltpu.make_async_copy(cache.at[:, :, pl.ds(KV_RANK, ROPE)], raw, l_w.at[4]),
    ]
    barrier = pltpu.get_barrier_semaphore()
    for i, j in DEC:
        signal(at(turn(x, i), y, turn(z, j), c))
    for i, j in PRE:
        signal(at(x, turn(y, i), z, lax.rem(c + j, 2)))
    for i in (2, 1, 3):
        signal(at(turn(x, i), y, z, 1 - c))
        signal(at(x, y, turn(z, i), 1 - c))
    for i in (2, 1, 3):
        signal(at(y, turn(y, i), z, c))
        signal(at(x, turn(y, i), y, c))

    @pl.when(x != y)
    def _():
        signal(at(y, y, z, c))

    @pl.when(z != y)
    def _():
        signal(at(x, y, y, c))

    small = [
        pltpu.make_async_copy(src, dst, l_w.at[5 + n])
        for n, (src, dst) in enumerate([
            (newl_in, newl), (slots_in, slots), (toks_in, toks), (resid_in, resid),
            (gain_in, gain), (lens_in, lens),
        ])
    ]
    loads[4].start()
    loads[0].start()
    for load in small:
        load.start()
    loads[1].start()
    loads[2].start()

    pl.semaphore_wait(
        barrier,
        15 + 7 + 6 + 6 + (x != y).astype(jnp.int32) + (z != y).astype(jnp.int32),
    )

    def group_of(axis, xx, yy, zz, cc):
        return 2 * {"x": xx, "y": yy, "z": zz}[axis] + cc

    def send_cache(k, source, target, ssem, rsem):
        axis = PAIRS[k]
        mine = group_of(axis, x, y, z, c)
        for i, j in PRE:
            xx = turn(x, i) if axis == "x" else x
            yy = turn(y, i) if axis == "y" else y
            zz = turn(z, i) if axis == "z" else z
            cc = lax.rem(c + j, 2)
            send(
                source(group_of(axis, xx, yy, zz, cc)), target(mine),
                ssem.at[k], rsem.at[k], at(xx, yy, zz, cc),
            )
        pltpu.make_async_copy(source(mine), target(mine), rsem.at[k]).start()

    def send_latents(k, core):
        axis = PAIRS[k]
        target = kbuf.at[k, :, pl.ds(64 * group_of(axis, x, y, z, c), 64), :]

        def source(xx, yy, zz, cc):
            first = 8 * group_of(axis, xx, yy, zz, cc) + 2 * k
            return cache.at[pl.ds(first, 2), :, pl.ds(0, KV_RANK)]

        for i in (2, 1, 3):
            xx = turn(x, i) if axis == "x" else x
            yy = turn(y, i) if axis == "y" else y
            zz = turn(z, i) if axis == "z" else z
            send(
                source(xx, yy, zz, core), target, s_k.at[k + 4 * core], r_k.at[k],
                at(xx, yy, zz, core),
            )
        if core == 0:
            send(source(x, y, z, 1 - c), target, s_k.at[k], r_k.at[k], at(x, y, z, 1 - c))
            pltpu.make_async_copy(source(x, y, z, c), target, r_k.at[k]).start()

    def latents_left(k, core):
        drain(kbuf.at[k, :, pl.ds(0, 192 if core else 256), :], s_k.at[k + 4 * core])

    def send_ropes(k):
        send_cache(
            k,
            lambda group: rope.at[4 * group + k],
            lambda mine: krope.at[k, pl.ds(64 * mine, 64), :],
            s_o, r_o,
        )
        later(krope.at[k, pl.ds(0, 448), :], s_o.at[k])

    def along(axis, step):
        return (turn(x, step), z) if axis == "x" else (x, turn(z, step))

    def coordinate(axis):
        return x if axis == "x" else z

    def send_query(k):
        axis = PAIRS[k]
        met = qbuf.at[k, coordinate(FIRST[k])]
        rows = query.at[pl.ds(64 * group_of(axis, x, y, z, c) + 16 * k, 16)]
        for i in (2, 1, 3):
            xx, zz = along(EARLY[k], i)
            send(
                query.at[pl.ds(64 * group_of(axis, xx, y, zz, c) + 16 * k, 16)], met.at[4 - i],
                s_q.at[k], r_q.at[k], at(xx, y, zz, c),
            )
        for i in (2, 1, 3):
            xx, zz = along(FIRST[k], i)
            send(rows, met.at[0], s_v.at[k], r_v.at[k], at(xx, y, zz, c))
        pltpu.make_async_copy(rows, met.at[0], r_q.at[k]).start()
        later(qbuf.at[k, 0, pl.ds(0, 3)], s_q.at[k])

    def pass_query(k):
        met = qbuf.at[k, coordinate(FIRST[k])]
        drain(met, r_q.at[k])
        for i in (2, 1, 3):
            xx, zz = along(FIRST[k], i)
            send(
                met.at[pl.ds(1, 3)], met.at[pl.ds(1, 3)], s_v.at[k], r_v.at[k],
                at(xx, y, zz, c),
            )
        later(qbuf.at[k, pl.ds(0, 3)], s_v.at[k])

    for k in (1, 0, 3, 2):
        send_query(k)
    for core in range(2):
        send_latents(FIRST_PAIR, core)
    def half(j):
        down = lax.broadcasted_iota(jnp.int32, (ROPE, 2 * ROPE), 0) + ROPE * j
        right = lax.broadcasted_iota(jnp.int32, (ROPE, 2 * ROPE), 1)
        return (down == right).astype(jnp.float32).astype(jnp.bfloat16)

    halves = [half(0), half(1)]
    loads[4].wait()
    for n in range(4):
        keys = raw[pl.ds(16 * n, 16)].reshape(8, 2, 64, ROPE)
        both = sum(
            jnp.dot(
                keys[:, j].reshape(512, ROPE), halves[j], preferred_element_type=jnp.float32
            )
            for j in range(2)
        )
        rope[pl.ds(8 * n, 8)] = both.astype(jnp.bfloat16).reshape(8, 64, 2 * ROPE)
    for k in (1, 0, 3, 2):
        send_ropes(k)
    loads[3].start()

    for k in (1, 0, 3, 2):
        pass_query(k)
    for k in (0, 3):
        send_latents(k, 0)

    def window(rows, n):
        left = 384 * (n % 2)
        block = rows[8 * (n // 2):8 * (n // 2) + 8]
        return jnp.concatenate([block[:, left:left + 256], block[:, left + 256:left + 512]], axis=0)

    loads[0].wait()
    for load in small:
        load.wait()
    row = lax.broadcasted_iota(jnp.int32, (64, 64), 0)
    col = lax.broadcasted_iota(jnp.int32, (64, 64), 1)
    pick = (col == 8 * p + (row >> 3)).astype(jnp.float32).astype(jnp.bfloat16)
    new_rows = jnp.dot(pick, newl[...], preferred_element_type=jnp.float32)
    own = jnp.sum(qown[...].astype(jnp.float32) * new_rows, axis=1, keepdims=True) * SCALE
    to_slot = (slots[...] == row).astype(jnp.float32).astype(jnp.bfloat16)
    resid_slot = jnp.dot(to_slot, resid[...], preferred_element_type=jnp.float32)
    for n in range(16):
        resw[n] = window(resid_slot, n)
    ls[:, :, :, pl.ds(HALF - 128, 128)] = jnp.zeros((2, 4, 16, 128), jnp.bfloat16)

    spot = lax.broadcasted_iota(jnp.int32, (1, 512), 1)
    lane = lax.broadcasted_iota(jnp.int32, (128, EXTRA), 1)
    lane16 = lax.broadcasted_iota(jnp.int32, (16, EXTRA), 1)

    def position(axis):
        slot, core, inner = spot >> 7, (spot >> 6) & 1, spot & 63
        xx = slot if axis == "x" else x
        yy = slot if axis == "y" else y
        zz = slot if axis == "z" else z
        return 64 * ((4 * xx + zz) * 8 + 2 * yy + core) + inner

    def queries_of(k):
        drain(qbuf.at[k, pl.ds(0, 3)], r_v.at[k])
        both = qbuf[k].astype(jnp.float32).reshape(16, 2, 8, WIDTH)
        queries = []
        for j in range(2):
            rows = both[:, j].reshape(128, WIDTH)
            turned = jnp.dot(
                rows[:, KV_RANK:].astype(jnp.bfloat16), halves[j],
                preferred_element_type=jnp.float32,
            )
            queries.append((rows[:, :KV_RANK].astype(jnp.bfloat16), turned.astype(jnp.bfloat16)))
        return queries

    def attend(k, queries=None):
        queries = queries or queries_of(k)
        axis = PAIRS[k]
        spots = position(axis)
        group = group_of(axis, x, y, z, c)
        drain(krope.at[k], r_o.at[k])
        drain(kbuf.at[k], r_k.at[k])
        sums, extras = [], []
        for j in range(2):
            keys = kbuf[k, j]
            scores = (
                lax.dot_general(
                    queries[j][0], keys, (((1,), (1,)), ((), ())),
                    preferred_element_type=jnp.float32,
                )
                + lax.dot_general(
                    queries[j][1], krope[k], (((1,), (1,)), ((), ())),
                    preferred_element_type=jnp.float32,
                )
            ) * SCALE
            scores = jnp.where(spots < lens[8 * group + 2 * k + j], scores, FILL)
            top = jnp.max(scores, axis=1, keepdims=True)
            top = top.astype(jnp.bfloat16).astype(jnp.float32)
            weights = jnp.exp(scores - top)
            total = jnp.sum(weights, axis=1, keepdims=True)
            sums.append(
                jnp.dot(
                    weights.astype(jnp.bfloat16), keys,
                    preferred_element_type=jnp.float32,
                ).reshape(16, 8, KV_RANK)
            )
            high = total.astype(jnp.bfloat16).astype(jnp.float32)
            extra = jnp.where(lane == 0, top, jnp.where(lane == 1, high, total - high))
            extras.append(extra.reshape(16, 8, EXTRA))
        sums = jnp.concatenate(sums, axis=1).astype(jnp.bfloat16).reshape(4, 4, 16, KV_RANK)
        extras = jnp.concatenate(extras, axis=1).astype(jnp.bfloat16).reshape(4, 4, 16, EXTRA)
        for n in range(4):
            pout[k, n, :, :, pl.ds(0, KV_RANK)] = sums[n]
            pout[k, n, :, :, pl.ds(KV_RANK, EXTRA)] = extras[n]
        for i in (2, 1, 3):
            xx, zz = along(FIRST[k], i)
            send(
                pout.at[k, xx if FIRST[k] == "x" else zz], pmid.at[k, i - 1],
                s_p.at[k], r_p.at[k], at(xx, y, zz, c),
            )
        once((0, k), lambda: drain(pmid.at[k], s_p.at[k]))

    def joined(blocks, own=None):
        extra = [block[..., KV_RANK:].astype(jnp.float32) for block in blocks]
        tops = [part[..., 0:1] for part in extra]
        top = functools.reduce(jnp.maximum, tops)
        if own is not None:
            top = jnp.maximum(top, own)
        shrink = [jnp.exp(part - top) for part in tops]
        total = sum((part[..., 1:2] + part[..., 2:3]) * by for part, by in zip(extra, shrink))
        summed = sum(
            block[..., :KV_RANK].astype(jnp.float32) * by for block, by in zip(blocks, shrink)
        )
        return top, total, summed

    def join_first(k):
        axis, first = PAIRS[k], FIRST[k]
        drain(pmid.at[k], r_p.at[k])
        for n in range(4):
            blocks = [pout[k, coordinate(first), n]] + [pmid[k, i, n] for i in range(3)]
            top, total, summed = joined(blocks)
            high = total.astype(jnp.bfloat16).astype(jnp.float32)
            extra = jnp.where(lane16 == 0, top, jnp.where(lane16 == 1, high, total - high))
            pjoin[k, n, :, pl.ds(0, KV_RANK)] = summed.astype(jnp.bfloat16)
            pjoin[k, n, :, pl.ds(KV_RANK, EXTRA)] = extra.astype(jnp.bfloat16)
        yy = {"x": x, "y": y, "z": z}[axis]
        place = y if axis != "y" else (z if first == "x" else x)
        here = z if first == "x" else x
        for i in (2, 1, 3):
            other = turn(here, i)
            xx, zz = (x, other) if first == "x" else (other, z)
            send(
                pjoin.at[k, i], pin.at[k, place],
                s_j.at[k], r_j.at[k], at(xx, yy, zz, c),
            )
        once((1, k), lambda: drain(pin.at[k, pl.ds(0, 3)], s_j.at[k]))

        def keep():
            pltpu.make_async_copy(pjoin.at[k, 0], pin.at[k, place], r_j.at[k]).start()

        if axis == "y":
            keep()
        else:
            pl.when(yy == y)(keep)

            @pl.when(yy != y)
            def _():
                send(
                    pjoin.at[k, 0], pin.at[k, place],
                    s_j.at[k], r_j.at[k], at(x, yy, z, c),
                )

            def left():
                pl.when(yy != y)(lambda: drain(pin.at[k, 0], s_j.at[k]))

            once((2, k), left)

    def join_last(k):
        drain(pin.at[k], r_j.at[k])
        blocks = [pin[k, n] for n in range(4)]
        own_k = own[16 * k:16 * k + 16]
        top, total, summed = joined(blocks, own_k)
        own_weight = jnp.exp(own_k - top)
        summed = summed + (
            own_weight.astype(jnp.bfloat16).astype(jnp.float32)
            * new_rows[16 * k:16 * k + 16, :KV_RANK]
        )
        summed = summed / (total + own_weight)
        for b in range(KV_RANK // 128):
            lat[b, pl.ds(16 * k, 16), :] = summed[:, 128 * b:128 * b + 128]

    queries = queries_of(FIRST_PAIR)
    send_latents(LAST, 0)
    for core in range(2):
        latents_left(FIRST_PAIR, core)
    send_latents(LAST, 1)
    attend(FIRST_PAIR, queries)
    for k in (0, 3):
        latents_left(k, 0)
        send_latents(k, 1)

    @pl.when(c == 0)
    def _():
        attend(0)
        attend(3)
        join_first(1)
        attend(2)

    @pl.when(c == 1)
    def _():
        join_first(1)
        attend(0)
        attend(3)
        attend(2)

    for k in (0, 3, 2):
        join_first(k)
    latents_left(LAST, 0)
    for k in (0, 3, 2):
        latents_left(k, 1)
    for k in (1, 0, 3, 2):
        join_last(k)

    loads[1].wait()
    values = []
    for f in range(8):
        rows = jnp.concatenate(
            [lat[b, pl.ds(f, 8, stride=8), :] for b in range(KV_RANK // 128)], axis=1
        ).astype(jnp.bfloat16)
        values.append(jnp.dot(rows, vwv[f], preferred_element_type=jnp.float32))
    packed = jnp.concatenate(
        [jnp.concatenate(values[:4], axis=1), jnp.concatenate(values[4:], axis=1)], axis=0
    )
    hv[p] = packed.astype(jnp.bfloat16)
    for n, (i, j) in enumerate(PRE):
        send(hv.at[p], hv.at[p], s_h.at[n], r_h.at[n], at(x, turn(y, i), z, lax.rem(c + j, 2)))
        later(hv.at[0], s_h.at[n])
    loads[2].wait()
    for n in range(7):
        drain(hv.at[0], r_h.at[n])

    heads = hv[...].astype(jnp.float32).reshape(8, 2, 8, KV_RANK)
    part = jnp.zeros((64, owv.shape[1]), jnp.float32)
    for half in range(2):
        rows = heads[:, half].reshape(64, KV_RANK).astype(jnp.bfloat16)
        rows = jnp.dot(to_slot, rows, preferred_element_type=jnp.float32).astype(jnp.bfloat16)
        part = part + jnp.dot(
            rows, owv[pl.ds(KV_RANK * half, KV_RANK), :], preferred_element_type=jnp.float32
        )
    for s in range(16):
        rss[s] = window(part, s).astype(jnp.bfloat16)
    for n, (i, j) in enumerate(DEC):
        xx, zz = turn(x, i), turn(z, j)
        send(rss.at[4 * xx + zz], rsr.at[n], s_r.at[0], r_r.at[0], at(xx, y, zz, c))
    later(rsr, s_r.at[0])
    drain(rsr, r_r.at[0])
    hidden = resw[d] + rss[d].astype(jnp.float32)
    for n in range(15):
        hidden = hidden + rsr[n].astype(jnp.float32)
    odd = lax.rem(d, 2) == 1
    gains = jnp.broadcast_to(gain[...].astype(jnp.float32).reshape(1, -1), (8, owv.shape[1]))
    scaled = hidden * jnp.where(odd, window(gains, 1), window(gains, 0))
    twice = (
        (lax.broadcasted_iota(jnp.int32, (16, 256), 0) < 8)
        & (lax.broadcasted_iota(jnp.int32, (16, 256), 1) < 128)
        & odd
    )
    squares = jnp.sum(jnp.where(twice, 0.0, hidden * hidden), axis=1, keepdims=True)
    squares = squares + jnp.concatenate([squares[8:], squares[:8]], axis=0)
    first = squares.astype(jnp.bfloat16).astype(jnp.float32)
    second = (squares - first).astype(jnp.bfloat16).astype(jnp.float32)
    third = squares - first - second
    agb[d, :, pl.ds(0, 256)] = scaled.astype(jnp.bfloat16)
    agb[d, :, pl.ds(256, 128)] = jnp.where(
        lane16 == 0, first, jnp.where(lane16 == 1, second, third)
    ).astype(jnp.bfloat16)
    for n, (i, j) in enumerate(DEC):
        send(agb.at[d], agb.at[d], s_a.at[n], r_a.at[n], at(turn(x, i), y, turn(z, j), c))
        later(agb.at[0], s_a.at[n])
    for n in range(15):
        drain(agb.at[0], r_a.at[n])
    gathered = agb[...].astype(jnp.float32).reshape(8, 2, 2, 8, 384)
    squares = sum(
        gathered[:, h, 0, :, 256 + n:257 + n] for h in range(2) for n in range(3)
    )
    sqs[...] = jnp.broadcast_to(squares, (8, 8, 128))
    for n, (i, j) in enumerate(PRE):
        yy, cc = turn(y, i), lax.rem(c + j, 2)
        send(sqs.at[2 * yy + cc], sqr.at[n], s_s.at[0], r_s.at[0], at(x, yy, z, cc))
    later(sqr, s_s.at[0])
    scaled = jnp.concatenate(
        [
            gathered[:, 0, 0, :, 0:256].reshape(64, 256),
            gathered[:, 0, 1, :, 0:256].reshape(64, 256),
            gathered[:, 1, 0, :, 128:256].reshape(64, 128),
            gathered[:, 1, 1, :, 0:256].reshape(64, 256),
        ],
        axis=1,
    ).astype(jnp.bfloat16)

    wide = HALF // CHUNKS

    def join_cores(i):
        lanes = pl.ds(wide * i, wide)
        drain(lr.at[:, :, lanes], r_c.at[i])
        ls[c, :, :, lanes] = (
            ls[c, :, :, lanes].astype(jnp.float32) + lr[:, :, lanes].astype(jnp.float32)
        ).astype(jnp.bfloat16)
        for step in (2, 1, 3):
            yy = turn(y, step)
            send(
                ls.at[c, yy, :, lanes], lb.at[step - 1, :, lanes],
                s_y.at[i], r_y.at[i], at(x, yy, z, c),
            )
        later(lb.at[:, :, lanes], s_y.at[i])

    loads[3].wait()
    for i in range(CHUNKS):
        for half in range(2):
            start = HALF * half + wide * i
            count = min(wide, vocab - start)
            product = lax.dot_general(
                scaled, lmv[pl.ds(start, count), :], (((1,), (1,)), ((), ())),
                preferred_element_type=jnp.float32,
            ).reshape(8, 8, count).astype(jnp.bfloat16)
            for q in range(8):
                ls[q % 2, q // 2, pl.ds(8 * half, 8), pl.ds(wide * i, count)] = product[q]
        lanes = pl.ds(wide * i, wide)
        send(
            ls.at[1 - c, :, :, lanes], lr.at[:, :, lanes],
            s_c.at[i], r_c.at[i], at(x, y, z, 1 - c),
        )
        later(lr.at[:, :, lanes], s_c.at[i])
        if i > 0:
            join_cores(i - 1)
    join_cores(CHUNKS - 1)

    drain(sqr, r_s.at[0])
    norm = sqs[p]
    for n in range(7):
        norm = norm + sqr[n]
    norm = lax.rsqrt(norm[:, 0:1] / D + 1e-06)
    for i in range(CHUNKS):
        drain(lb.at[:, :, pl.ds(wide * i, wide)], r_y.at[i])
    logits = ls[c, y].astype(jnp.float32)
    for n in range(3):
        logits = logits + lb[n].astype(jnp.float32)
    low, high = logits[:8] * norm, logits[8:] * norm

    raws[:, pl.ds(0, HALF)] = low
    raws[:, pl.ds(HALF, vocab - HALF)] = high[:, : vocab - HALF]
    write = pltpu.make_async_copy(raws, out, l_w.at[0])
    write.start()

    column = lax.broadcasted_iota(jnp.int32, (8, HALF), 1)
    high = jnp.where(column < vocab - HALF, high, FILL)
    slot_rows = lax.broadcasted_iota(jnp.int32, (8, 64), 0) + 8 * p
    token = jnp.sum(jnp.where(slots[...] == slot_rows, toks[...], 0), axis=1, keepdims=True)
    token = token - d * vocab
    picked = jnp.sum(jnp.where(column == token, low, 0.0), axis=1, keepdims=True) + jnp.sum(
        jnp.where((column + HALF == token) & (column < vocab - HALF), high, 0.0),
        axis=1, keepdims=True,
    )
    top = jnp.maximum(
        jnp.max(low, axis=1, keepdims=True), jnp.max(high, axis=1, keepdims=True)
    )
    total = jnp.sum(jnp.exp(low - top), axis=1, keepdims=True) + jnp.sum(
        jnp.exp(high - top), axis=1, keepdims=True
    )
    lane8 = lax.broadcasted_iota(jnp.int32, (8, 128), 1)
    mine = jnp.where(lane8 == 0, top, jnp.where(lane8 == 1, total, picked))
    sms[...] = mine
    for n, (i, j) in enumerate(DEC):
        send(sms, smr.at[n], s_m.at[0], r_m.at[0], at(turn(x, i), y, turn(z, j), c))
    later(smr, s_m.at[0])
    drain(smr, r_m.at[0])
    others = smr[...]
    best = jnp.maximum(jnp.max(others[:, :, 0:1], axis=0), top)
    total = total * jnp.exp(top - best) + jnp.sum(
        others[:, :, 1:2] * jnp.exp(others[:, :, 0:1] - best[None]), axis=0
    )
    picked = picked + jnp.sum(others[:, :, 2:3], axis=0)
    normalizer = best + jnp.log(total)
    tail[...] = jnp.where(lane8 == 0, normalizer, picked - normalizer)
    write.wait()
    finish()


def finish_kernel(logits, tail, out, tgt):
    out[...] = logits[...] - tail[:, 0:1]
    square = lax.broadcasted_iota(jnp.int32, (8, 8), 0) == lax.broadcasted_iota(
        jnp.int32, (8, 8), 1
    )
    tgt[...] = jnp.sum(jnp.where(square, tail[:, 1:2], 0.0), axis=0, keepdims=True)


def body(
    latent_cache, query, new_latent, lengths, slot_of, token_ids,
    latent_value_weight, out_weight, residual, norm_gain, lm_weight,
):
    columns, vocab = lm_weight.shape
    bf16, f32 = jnp.bfloat16, jnp.float32
    vmem = pl.BlockSpec(memory_space=pltpu.VMEM)
    anywhere = pl.BlockSpec(memory_space=pl.ANY)
    dma = pltpu.SemaphoreType.DMA
    logits, tail = pl.pallas_call(
        kernel,
        out_shape=(
            jax.ShapeDtypeStruct((8, vocab), f32),
            jax.ShapeDtypeStruct((8, 128), f32),
        ),
        in_specs=[anywhere] * 11,
        out_specs=(anywhere, vmem),
        scratch_shapes=[
            pltpu.SMEM((64,), jnp.int32),
            pltpu.VMEM((64, WIDTH), bf16),
            pltpu.VMEM((1, 64), jnp.int32),
            pltpu.VMEM((1, 64), jnp.int32),
            pltpu.VMEM((64, columns), bf16),
            pltpu.VMEM((columns,), bf16),
            pltpu.VMEM((8, vocab), f32),
            pltpu.VMEM((4, 2, 512, KV_RANK), bf16),
            pltpu.VMEM((64, 64, ROPE), bf16),
            pltpu.VMEM((32, 64, 2 * ROPE), bf16),
            pltpu.VMEM((4, 512, 2 * ROPE), bf16),
            pltpu.VMEM((4, 4, 4, 16, WIDTH), bf16),
            pltpu.VMEM((4, 4, 4, 16, KV_RANK + EXTRA), bf16),
            pltpu.VMEM((4, 4, 16, KV_RANK + EXTRA), bf16),
            pltpu.VMEM((4, 3, 4, 16, KV_RANK + EXTRA), bf16),
            pltpu.VMEM((4, 4, 16, KV_RANK + EXTRA), bf16),
            pltpu.VMEM((8, KV_RANK, VHEAD), bf16),
            pltpu.VMEM((1024, columns), bf16),
            pltpu.VMEM((vocab, columns), bf16),
            pltpu.VMEM((64, WIDTH), bf16),
            pltpu.VMEM((KV_RANK // 128, 64, 128), f32),
            pltpu.VMEM((8, 16, 512), bf16),
            pltpu.VMEM((16, 16, 256), f32),
            pltpu.VMEM((16, 16, 256), bf16),
            pltpu.VMEM((15, 16, 256), bf16),
            pltpu.VMEM((16, 16, 384), bf16),
            pltpu.VMEM((8, 8, 128), f32),
            pltpu.VMEM((7, 8, 128), f32),
            pltpu.VMEM((2, 4, 16, HALF), bf16),
            pltpu.VMEM((4, 16, HALF), bf16),
            pltpu.VMEM((3, 16, HALF), bf16),
            pltpu.VMEM((8, 128), f32),
            pltpu.VMEM((15, 8, 128), f32),
            dma((8,)), dma((4,)), dma((4,)), dma((4,)), dma((4,)), dma((4,)), dma((4,)), dma((4,)),
            dma((4,)), dma((4,)), dma((4,)), dma((4,)),
            dma((11,)),
            dma((7,)), dma((7,)), dma((1,)), dma((1,)), dma((15,)), dma((15,)),
            dma((1,)), dma((1,)), dma((CHUNKS,)), dma((CHUNKS,)), dma((CHUNKS,)),
            dma((CHUNKS,)), dma((1,)), dma((1,)),
        ],
        name="decode_step",
        compiler_params=pltpu.CompilerParams(
            collective_id=0, has_side_effects=True, vmem_limit_bytes=56 << 20
        ),
    )(
        lengths,
        latent_cache,
        query.reshape(-1, WIDTH),
        new_latent,
        slot_of.reshape(1, -1),
        token_ids.reshape(1, -1),
        residual,
        norm_gain,
        latent_value_weight,
        out_weight,
        lm_weight.T,
    )
    logprobs, target = pl.pallas_call(
        finish_kernel,
        out_shape=(
            jax.ShapeDtypeStruct((8, vocab), f32),
            jax.ShapeDtypeStruct((1, 8), f32),
        ),
        name="log_probabilities",
    )(logits, tail)
    return logprobs, target.reshape(8)


def solution(mesh):
    return jax.shard_map(
        body,
        mesh=mesh,
        in_specs=(
            P(None, ("dec", "pre"), None),
            P(None, "dec", None),
            P(),
            P(),
            P(),
            P(),
            P("dec", None, None),
            P("dec", "pre"),
            P(None, "pre"),
            P("pre"),
            P("pre", "dec"),
        ),
        out_specs=(P("pre", "dec"), P("pre")),
        check_vma=False,
    )
```

```python
import functools

import jax
import jax.numpy as jnp
from jax import lax
from jax.experimental import pallas as pl
from jax.experimental.pallas import tpu as pltpu
from jax.sharding import PartitionSpec as P

KV_RANK = 512
ROPE = 64
VHEAD = 128
D = 7168
WIDTH = KV_RANK + ROPE
MESH = pl.DeviceIdType.MESH
FILL = -(2.0**100)
SCALE = (VHEAD + ROPE) ** (-0.5)
EXTRA = 128
HALF = 4096
CHUNKS = 4

PAIRS = ("x", "y", "y", "z")
FIRST_PAIR = 1
LAST = 2
EARLY = ("x", "z", "x", "z")
FIRST = ("z", "x", "z", "x")


def drain(ref, sem):
    pltpu.make_async_copy(ref, ref, sem).wait()


def kernel(
    lens_in, cache, query, newl_in, slots_in, toks_in, resid_in, gain_in, vw, ow, lm,
    out, tail,
    lens, newl, slots, toks, resid, gain, raws, kbuf, raw, rope, krope, qbuf, pout, pjoin, pmid, pin, vwv, owv, lmv, qown, lat, hv, resw, rss, rsr, agb,
    sqs, sqr, ls, lr, lb, sms, smr,
    s_k, r_k, s_o, r_o, s_q, r_q, s_v, r_v, s_p, r_p, s_j, r_j, l_w, s_h, r_h, s_r, r_r, s_a, r_a, s_s, r_s,
    s_c, r_c, s_y, r_y, s_m, r_m,
):
    p, d = lax.axis_index("pre"), lax.axis_index("dec")
    y, c = lax.div(p, 2), lax.rem(p, 2)
    x, z = lax.div(d, 4), lax.rem(d, 4)
    vocab = lm.shape[0]

    def at(xx, yy, zz, cc):
        return (2 * yy + cc, 4 * xx + zz)

    def turn(value, step):
        return lax.rem(value + step, 4)

    def send(src, dst, ssem, rsem, device):
        pltpu.make_async_remote_copy(
            src_ref=src, dst_ref=dst, send_sem=ssem, recv_sem=rsem,
            device_id=device, device_id_type=MESH,
        ).start()

    pending, known = [], set()

    def later(ref, sem):
        pending.append(lambda: drain(ref, sem))

    def once(key, wait):
        if key not in known:
            known.add(key)
            pending.append(wait)

    def finish():
        for wait in pending:
            wait()

    def signal(device):
        pl.semaphore_signal(barrier, inc=1, device_id=device, device_id_type=MESH)

    hops = (0, 1, 2, 1)
    DEC = [(i, j) for i in range(4) for j in range(4) if (i, j) != (0, 0)]
    DEC.sort(key=lambda ij: -hops[ij[0]] - hops[ij[1]])
    PRE = [(i, j) for i in range(4) for j in range(2) if (i, j) != (0, 0)]
    PRE.sort(key=lambda ij: -hops[ij[0]] - ij[1])

    loads = [
        pltpu.make_async_copy(query.at[pl.ds(64 * p, 64)], qown, l_w.at[0]),
        pltpu.make_async_copy(vw, vwv, l_w.at[1]),
        pltpu.make_async_copy(ow, owv, l_w.at[2]),
        pltpu.make_async_copy(lm, lmv, l_w.at[3]),
        pltpu.make_async_copy(cache.at[:, :, pl.ds(KV_RANK, ROPE)], raw, l_w.at[4]),
    ]
    barrier = pltpu.get_barrier_semaphore()
    for i in (2, 1, 3):
        signal(at(y, turn(y, i), z, c))
        signal(at(x, turn(y, i), y, c))

    @pl.when(x != y)
    def _():
        signal(at(y, y, z, c))

    @pl.when(z != y)
    def _():
        signal(at(x, y, y, c))

    for i, j in DEC:
        signal(at(turn(x, i), y, turn(z, j), c))
    for i, j in PRE:
        signal(at(x, turn(y, i), z, lax.rem(c + j, 2)))
    for i in (2, 1, 3):
        signal(at(turn(x, i), y, z, 1 - c))
        signal(at(x, y, turn(z, i), 1 - c))
    small = [
        pltpu.make_async_copy(src, dst, l_w.at[5 + n])
        for n, (src, dst) in enumerate([
            (newl_in, newl), (slots_in, slots), (toks_in, toks), (resid_in, resid),
            (gain_in, gain), (lens_in, lens),
        ])
    ]
    loads[4].start()
    loads[0].start()
    for load in small:
        load.start()
    loads[1].start()
    loads[2].start()

    pl.semaphore_wait(
        barrier,
        15 + 7 + 6 + 6 + (x != y).astype(jnp.int32) + (z != y).astype(jnp.int32),
    )

    def group_of(axis, xx, yy, zz, cc):
        return 2 * {"x": xx, "y": yy, "z": zz}[axis] + cc

    def send_cache(k, source, target, ssem, rsem):
        axis = PAIRS[k]
        mine = group_of(axis, x, y, z, c)
        for i, j in PRE:
            xx = turn(x, i) if axis == "x" else x
            yy = turn(y, i) if axis == "y" else y
            zz = turn(z, i) if axis == "z" else z
            cc = lax.rem(c + j, 2)
            send(
                source(group_of(axis, xx, yy, zz, cc)), target(mine),
                ssem.at[k], rsem.at[k], at(xx, yy, zz, cc),
            )
        pltpu.make_async_copy(source(mine), target(mine), rsem.at[k]).start()

    def send_latents(k, core):
        axis = PAIRS[k]
        target = kbuf.at[k, :, pl.ds(64 * group_of(axis, x, y, z, c), 64), :]

        def source(xx, yy, zz, cc):
            first = 8 * group_of(axis, xx, yy, zz, cc) + 2 * k
            return cache.at[pl.ds(first, 2), :, pl.ds(0, KV_RANK)]

        for i in (2, 1, 3):
            xx = turn(x, i) if axis == "x" else x
            yy = turn(y, i) if axis == "y" else y
            zz = turn(z, i) if axis == "z" else z
            send(
                source(xx, yy, zz, core), target, s_k.at[k + 4 * core], r_k.at[k],
                at(xx, yy, zz, core),
            )
        if core == 0:
            send(source(x, y, z, 1 - c), target, s_k.at[k], r_k.at[k], at(x, y, z, 1 - c))
            pltpu.make_async_copy(source(x, y, z, c), target, r_k.at[k]).start()

    def latents_left(k, core):
        drain(kbuf.at[k, :, pl.ds(0, 192 if core else 256), :], s_k.at[k + 4 * core])

    def send_ropes(k):
        send_cache(
            k,
            lambda group: rope.at[4 * group + k],
            lambda mine: krope.at[k, pl.ds(64 * mine, 64), :],
            s_o, r_o,
        )
        later(krope.at[k, pl.ds(0, 448), :], s_o.at[k])

    def along(axis, step):
        return (turn(x, step), z) if axis == "x" else (x, turn(z, step))

    def coordinate(axis):
        return x if axis == "x" else z

    def send_query(k):
        axis = PAIRS[k]
        met = qbuf.at[k, coordinate(FIRST[k])]
        rows = query.at[pl.ds(64 * group_of(axis, x, y, z, c) + 16 * k, 16)]
        for i in (2, 1, 3):
            xx, zz = along(EARLY[k], i)
            send(
                query.at[pl.ds(64 * group_of(axis, xx, y, zz, c) + 16 * k, 16)], met.at[4 - i],
                s_q.at[k], r_q.at[k], at(xx, y, zz, c),
            )
        for i in (2, 1, 3):
            xx, zz = along(FIRST[k], i)
            send(rows, met.at[0], s_v.at[k], r_v.at[k], at(xx, y, zz, c))
        pltpu.make_async_copy(rows, met.at[0], r_q.at[k]).start()
        later(qbuf.at[k, 0, pl.ds(0, 3)], s_q.at[k])

    def pass_query(k):
        met = qbuf.at[k, coordinate(FIRST[k])]
        drain(met, r_q.at[k])
        for i in (2, 1, 3):
            xx, zz = along(FIRST[k], i)
            send(
                met.at[pl.ds(1, 3)], met.at[pl.ds(1, 3)], s_v.at[k], r_v.at[k],
                at(xx, y, zz, c),
            )
        later(qbuf.at[k, pl.ds(0, 3)], s_v.at[k])

    for k in (1, 0, 3, 2):
        send_query(k)
    for core in range(2):
        send_latents(FIRST_PAIR, core)
    def half(j):
        down = lax.broadcasted_iota(jnp.int32, (ROPE, 2 * ROPE), 0) + ROPE * j
        right = lax.broadcasted_iota(jnp.int32, (ROPE, 2 * ROPE), 1)
        return (down == right).astype(jnp.float32).astype(jnp.bfloat16)

    halves = [half(0), half(1)]
    loads[4].wait()
    for n in range(4):
        keys = raw[pl.ds(16 * n, 16)].reshape(8, 2, 64, ROPE)
        both = sum(
            jnp.dot(
                keys[:, j].reshape(512, ROPE), halves[j], preferred_element_type=jnp.float32
            )
            for j in range(2)
        )
        rope[pl.ds(8 * n, 8)] = both.astype(jnp.bfloat16).reshape(8, 64, 2 * ROPE)
    for k in (1, 0, 3, 2):
        send_ropes(k)
    loads[3].start()

    for k in (1, 0, 3, 2):
        pass_query(k)
    for k in (0, 3):
        send_latents(k, 0)

    def window(rows, n):
        left = 384 * (n % 2)
        block = rows[8 * (n // 2):8 * (n // 2) + 8]
        return jnp.concatenate([block[:, left:left + 256], block[:, left + 256:left + 512]], axis=0)

    loads[0].wait()
    for load in small:
        load.wait()
    row = lax.broadcasted_iota(jnp.int32, (64, 64), 0)
    col = lax.broadcasted_iota(jnp.int32, (64, 64), 1)
    pick = (col == 8 * p + (row >> 3)).astype(jnp.float32).astype(jnp.bfloat16)
    new_rows = jnp.dot(pick, newl[...], preferred_element_type=jnp.float32)
    own = jnp.sum(qown[...].astype(jnp.float32) * new_rows, axis=1, keepdims=True) * SCALE
    to_slot = (slots[...] == row).astype(jnp.float32).astype(jnp.bfloat16)
    resid_slot = jnp.dot(to_slot, resid[...], preferred_element_type=jnp.float32)
    for n in range(16):
        resw[n] = window(resid_slot, n)
    ls[:, :, :, pl.ds(HALF - 128, 128)] = jnp.zeros((2, 4, 16, 128), jnp.bfloat16)

    spot = lax.broadcasted_iota(jnp.int32, (1, 512), 1)
    lane = lax.broadcasted_iota(jnp.int32, (128, EXTRA), 1)
    lane16 = lax.broadcasted_iota(jnp.int32, (16, EXTRA), 1)

    def position(axis):
        slot, core, inner = spot >> 7, (spot >> 6) & 1, spot & 63
        xx = slot if axis == "x" else x
        yy = slot if axis == "y" else y
        zz = slot if axis == "z" else z
        return 64 * ((4 * xx + zz) * 8 + 2 * yy + core) + inner

    def queries_of(k):
        drain(qbuf.at[k, pl.ds(0, 3)], r_v.at[k])
        both = qbuf[k].astype(jnp.float32).reshape(16, 2, 8, WIDTH)
        queries = []
        for j in range(2):
            rows = both[:, j].reshape(128, WIDTH)
            turned = jnp.dot(
                rows[:, KV_RANK:].astype(jnp.bfloat16), halves[j],
                preferred_element_type=jnp.float32,
            )
            queries.append((rows[:, :KV_RANK].astype(jnp.bfloat16), turned.astype(jnp.bfloat16)))
        return queries

    def attend(k, queries=None):
        queries = queries or queries_of(k)
        axis = PAIRS[k]
        spots = position(axis)
        group = group_of(axis, x, y, z, c)
        drain(krope.at[k], r_o.at[k])
        drain(kbuf.at[k], r_k.at[k])
        sums, extras = [], []
        for j in range(2):
            keys = kbuf[k, j]
            scores = (
                lax.dot_general(
                    queries[j][0], keys, (((1,), (1,)), ((), ())),
                    preferred_element_type=jnp.float32,
                )
                + lax.dot_general(
                    queries[j][1], krope[k], (((1,), (1,)), ((), ())),
                    preferred_element_type=jnp.float32,
                )
            ) * SCALE
            scores = jnp.where(spots < lens[8 * group + 2 * k + j], scores, FILL)
            top = jnp.max(scores, axis=1, keepdims=True)
            top = top.astype(jnp.bfloat16).astype(jnp.float32)
            weights = jnp.exp(scores - top)
            total = jnp.sum(weights, axis=1, keepdims=True)
            sums.append(
                jnp.dot(
                    weights.astype(jnp.bfloat16), keys,
                    preferred_element_type=jnp.float32,
                ).reshape(16, 8, KV_RANK)
            )
            high = total.astype(jnp.bfloat16).astype(jnp.float32)
            extra = jnp.where(lane == 0, top, jnp.where(lane == 1, high, total - high))
            extras.append(extra.reshape(16, 8, EXTRA))
        sums = jnp.concatenate(sums, axis=1).astype(jnp.bfloat16).reshape(4, 4, 16, KV_RANK)
        extras = jnp.concatenate(extras, axis=1).astype(jnp.bfloat16).reshape(4, 4, 16, EXTRA)
        for n in range(4):
            pout[k, n, :, :, pl.ds(0, KV_RANK)] = sums[n]
            pout[k, n, :, :, pl.ds(KV_RANK, EXTRA)] = extras[n]
        for i in (2, 1, 3):
            xx, zz = along(FIRST[k], i)
            send(
                pout.at[k, xx if FIRST[k] == "x" else zz], pmid.at[k, i - 1],
                s_p.at[k], r_p.at[k], at(xx, y, zz, c),
            )
        once((0, k), lambda: drain(pmid.at[k], s_p.at[k]))

    def joined(blocks, own=None):
        extra = [block[..., KV_RANK:].astype(jnp.float32) for block in blocks]
        tops = [part[..., 0:1] for part in extra]
        top = functools.reduce(jnp.maximum, tops)
        if own is not None:
            top = jnp.maximum(top, own)
        shrink = [jnp.exp(part - top) for part in tops]
        total = sum((part[..., 1:2] + part[..., 2:3]) * by for part, by in zip(extra, shrink))
        summed = sum(
            block[..., :KV_RANK].astype(jnp.float32) * by for block, by in zip(blocks, shrink)
        )
        return top, total, summed

    def join_first(k):
        axis, first = PAIRS[k], FIRST[k]
        drain(pmid.at[k], r_p.at[k])
        for n in range(4):
            blocks = [pout[k, coordinate(first), n]] + [pmid[k, i, n] for i in range(3)]
            top, total, summed = joined(blocks)
            high = total.astype(jnp.bfloat16).astype(jnp.float32)
            extra = jnp.where(lane16 == 0, top, jnp.where(lane16 == 1, high, total - high))
            pjoin[k, n, :, pl.ds(0, KV_RANK)] = summed.astype(jnp.bfloat16)
            pjoin[k, n, :, pl.ds(KV_RANK, EXTRA)] = extra.astype(jnp.bfloat16)
        yy = {"x": x, "y": y, "z": z}[axis]
        place = y if axis != "y" else (z if first == "x" else x)
        here = z if first == "x" else x
        for i in (2, 1, 3):
            other = turn(here, i)
            xx, zz = (x, other) if first == "x" else (other, z)
            send(
                pjoin.at[k, i], pin.at[k, place],
                s_j.at[k], r_j.at[k], at(xx, yy, zz, c),
            )
        once((1, k), lambda: drain(pin.at[k, pl.ds(0, 3)], s_j.at[k]))

        def keep():
            pltpu.make_async_copy(pjoin.at[k, 0], pin.at[k, place], r_j.at[k]).start()

        if axis == "y":
            keep()
        else:
            pl.when(yy == y)(keep)

            @pl.when(yy != y)
            def _():
                send(
                    pjoin.at[k, 0], pin.at[k, place],
                    s_j.at[k], r_j.at[k], at(x, yy, z, c),
                )

            def left():
                pl.when(yy != y)(lambda: drain(pin.at[k, 0], s_j.at[k]))

            once((2, k), left)

    def join_last(k):
        drain(pin.at[k], r_j.at[k])
        blocks = [pin[k, n] for n in range(4)]
        own_k = own[16 * k:16 * k + 16]
        top, total, summed = joined(blocks, own_k)
        own_weight = jnp.exp(own_k - top)
        summed = summed + (
            own_weight.astype(jnp.bfloat16).astype(jnp.float32)
            * new_rows[16 * k:16 * k + 16, :KV_RANK]
        )
        summed = summed / (total + own_weight)
        for b in range(KV_RANK // 128):
            lat[b, pl.ds(16 * k, 16), :] = summed[:, 128 * b:128 * b + 128]

    queries = queries_of(FIRST_PAIR)
    send_latents(LAST, 0)
    for core in range(2):
        latents_left(FIRST_PAIR, core)
    send_latents(LAST, 1)
    attend(FIRST_PAIR, queries)
    for k in (0, 3):
        latents_left(k, 0)
        send_latents(k, 1)

    @pl.when(c == 0)
    def _():
        attend(0)
        attend(3)
        join_first(1)
        attend(2)

    @pl.when(c == 1)
    def _():
        join_first(1)
        attend(0)
        attend(3)
        attend(2)

    for k in (0, 3, 2):
        join_first(k)
    latents_left(LAST, 0)
    for k in (0, 3, 2):
        latents_left(k, 1)
    for k in (1, 0, 3, 2):
        join_last(k)

    loads[1].wait()
    values = []
    for f in range(8):
        rows = jnp.concatenate(
            [lat[b, pl.ds(f, 8, stride=8), :] for b in range(KV_RANK // 128)], axis=1
        ).astype(jnp.bfloat16)
        values.append(jnp.dot(rows, vwv[f], preferred_element_type=jnp.float32))
    packed = jnp.concatenate(
        [jnp.concatenate(values[:4], axis=1), jnp.concatenate(values[4:], axis=1)], axis=0
    )
    hv[p] = packed.astype(jnp.bfloat16)
    for i, j in PRE:
        send(hv.at[p], hv.at[p], s_h.at[0], r_h.at[0], at(x, turn(y, i), z, lax.rem(c + j, 2)))
    later(hv.at[pl.ds(0, 7)], s_h.at[0])
    loads[2].wait()
    drain(hv.at[pl.ds(0, 7)], r_h.at[0])

    heads = hv[...].astype(jnp.float32).reshape(8, 2, 8, KV_RANK)
    part = jnp.zeros((64, owv.shape[1]), jnp.float32)
    for half in range(2):
        rows = heads[:, half].reshape(64, KV_RANK).astype(jnp.bfloat16)
        rows = jnp.dot(to_slot, rows, preferred_element_type=jnp.float32).astype(jnp.bfloat16)
        part = part + jnp.dot(
            rows, owv[pl.ds(KV_RANK * half, KV_RANK), :], preferred_element_type=jnp.float32
        )
    for s in range(16):
        rss[s] = window(part, s).astype(jnp.bfloat16)
    for n, (i, j) in enumerate(DEC):
        xx, zz = turn(x, i), turn(z, j)
        send(rss.at[4 * xx + zz], rsr.at[n], s_r.at[0], r_r.at[0], at(xx, y, zz, c))
    later(rsr, s_r.at[0])
    drain(rsr, r_r.at[0])
    hidden = resw[d] + rss[d].astype(jnp.float32)
    for n in range(15):
        hidden = hidden + rsr[n].astype(jnp.float32)
    odd = lax.rem(d, 2) == 1
    gains = jnp.broadcast_to(gain[...].astype(jnp.float32).reshape(1, -1), (8, owv.shape[1]))
    scaled = hidden * jnp.where(odd, window(gains, 1), window(gains, 0))
    twice = (
        (lax.broadcasted_iota(jnp.int32, (16, 256), 0) < 8)
        & (lax.broadcasted_iota(jnp.int32, (16, 256), 1) < 128)
        & odd
    )
    squares = jnp.sum(jnp.where(twice, 0.0, hidden * hidden), axis=1, keepdims=True)
    squares = squares + jnp.concatenate([squares[8:], squares[:8]], axis=0)
    first = squares.astype(jnp.bfloat16).astype(jnp.float32)
    second = (squares - first).astype(jnp.bfloat16).astype(jnp.float32)
    third = squares - first - second
    agb[d, :, pl.ds(0, 256)] = scaled.astype(jnp.bfloat16)
    agb[d, :, pl.ds(256, 128)] = jnp.where(
        lane16 == 0, first, jnp.where(lane16 == 1, second, third)
    ).astype(jnp.bfloat16)
    for i, j in DEC:
        send(agb.at[d], agb.at[d], s_a.at[0], r_a.at[0], at(turn(x, i), y, turn(z, j), c))
    later(agb.at[pl.ds(0, 15)], s_a.at[0])
    drain(agb.at[pl.ds(0, 15)], r_a.at[0])
    gathered = agb[...].astype(jnp.float32).reshape(8, 2, 2, 8, 384)
    squares = sum(
        gathered[:, h, 0, :, 256 + n:257 + n] for h in range(2) for n in range(3)
    )
    sqs[...] = jnp.broadcast_to(squares, (8, 8, 128))
    for n, (i, j) in enumerate(PRE):
        yy, cc = turn(y, i), lax.rem(c + j, 2)
        send(sqs.at[2 * yy + cc], sqr.at[n], s_s.at[0], r_s.at[0], at(x, yy, z, cc))
    later(sqr, s_s.at[0])
    scaled = jnp.concatenate(
        [
            gathered[:, 0, 0, :, 0:256].reshape(64, 256),
            gathered[:, 0, 1, :, 0:256].reshape(64, 256),
            gathered[:, 1, 0, :, 128:256].reshape(64, 128),
            gathered[:, 1, 1, :, 0:256].reshape(64, 256),
        ],
        axis=1,
    ).astype(jnp.bfloat16)

    wide = HALF // CHUNKS

    def join_cores(i):
        lanes = pl.ds(wide * i, wide)
        drain(lr.at[:, :, lanes], r_c.at[i])
        ls[c, :, :, lanes] = (
            ls[c, :, :, lanes].astype(jnp.float32) + lr[:, :, lanes].astype(jnp.float32)
        ).astype(jnp.bfloat16)
        for step in (2, 1, 3):
            yy = turn(y, step)
            send(
                ls.at[c, yy, :, lanes], lb.at[step - 1, :, lanes],
                s_y.at[i], r_y.at[i], at(x, yy, z, c),
            )
        later(lb.at[:, :, lanes], s_y.at[i])

    loads[3].wait()
    for i in range(CHUNKS):
        for half in range(2):
            start = HALF * half + wide * i
            count = min(wide, vocab - start)
            product = lax.dot_general(
                scaled, lmv[pl.ds(start, count), :], (((1,), (1,)), ((), ())),
                preferred_element_type=jnp.float32,
            ).reshape(8, 8, count).astype(jnp.bfloat16)
            for q in range(8):
                ls[q % 2, q // 2, pl.ds(8 * half, 8), pl.ds(wide * i, count)] = product[q]
        lanes = pl.ds(wide * i, wide)
        send(
            ls.at[1 - c, :, :, lanes], lr.at[:, :, lanes],
            s_c.at[i], r_c.at[i], at(x, y, z, 1 - c),
        )
        later(lr.at[:, :, lanes], s_c.at[i])
        if i > 0:
            join_cores(i - 1)
    join_cores(CHUNKS - 1)

    drain(sqr, r_s.at[0])
    norm = sqs[p]
    for n in range(7):
        norm = norm + sqr[n]
    norm = lax.rsqrt(norm[:, 0:1] / D + 1e-06)
    for i in range(CHUNKS):
        drain(lb.at[:, :, pl.ds(wide * i, wide)], r_y.at[i])
    logits = ls[c, y].astype(jnp.float32)
    for n in range(3):
        logits = logits + lb[n].astype(jnp.float32)
    low, high = logits[:8] * norm, logits[8:] * norm

    raws[:, pl.ds(0, HALF)] = low
    raws[:, pl.ds(HALF, vocab - HALF)] = high[:, : vocab - HALF]
    write = pltpu.make_async_copy(raws, out, l_w.at[0])
    write.start()

    column = lax.broadcasted_iota(jnp.int32, (8, HALF), 1)
    high = jnp.where(column < vocab - HALF, high, FILL)
    slot_rows = lax.broadcasted_iota(jnp.int32, (8, 64), 0) + 8 * p
    token = jnp.sum(jnp.where(slots[...] == slot_rows, toks[...], 0), axis=1, keepdims=True)
    token = token - d * vocab
    picked = jnp.sum(jnp.where(column == token, low, 0.0), axis=1, keepdims=True) + jnp.sum(
        jnp.where((column + HALF == token) & (column < vocab - HALF), high, 0.0),
        axis=1, keepdims=True,
    )
    top = jnp.maximum(
        jnp.max(low, axis=1, keepdims=True), jnp.max(high, axis=1, keepdims=True)
    )
    total = jnp.sum(jnp.exp(low - top), axis=1, keepdims=True) + jnp.sum(
        jnp.exp(high - top), axis=1, keepdims=True
    )
    lane8 = lax.broadcasted_iota(jnp.int32, (8, 128), 1)
    mine = jnp.where(lane8 == 0, top, jnp.where(lane8 == 1, total, picked))
    sms[...] = mine
    for n, (i, j) in enumerate(DEC):
        send(sms, smr.at[n], s_m.at[0], r_m.at[0], at(turn(x, i), y, turn(z, j), c))
    finish()
    drain(smr, r_m.at[0])
    others = smr[...]
    best = jnp.maximum(jnp.max(others[:, :, 0:1], axis=0), top)
    total = total * jnp.exp(top - best) + jnp.sum(
        others[:, :, 1:2] * jnp.exp(others[:, :, 0:1] - best[None]), axis=0
    )
    picked = picked + jnp.sum(others[:, :, 2:3], axis=0)
    normalizer = best + jnp.log(total)
    tail[...] = jnp.where(lane8 == 0, normalizer, picked - normalizer)
    write.wait()
    drain(smr, s_m.at[0])


def finish_kernel(logits, tail, out, tgt):
    out[...] = logits[...] - tail[:, 0:1]
    square = lax.broadcasted_iota(jnp.int32, (8, 8), 0) == lax.broadcasted_iota(
        jnp.int32, (8, 8), 1
    )
    tgt[...] = jnp.sum(jnp.where(square, tail[:, 1:2], 0.0), axis=0, keepdims=True)


def body(
    latent_cache, query, new_latent, lengths, slot_of, token_ids,
    latent_value_weight, out_weight, residual, norm_gain, lm_weight,
):
    columns, vocab = lm_weight.shape
    bf16, f32 = jnp.bfloat16, jnp.float32
    vmem = pl.BlockSpec(memory_space=pltpu.VMEM)
    anywhere = pl.BlockSpec(memory_space=pl.ANY)
    dma = pltpu.SemaphoreType.DMA
    logits, tail = pl.pallas_call(
        kernel,
        out_shape=(
            jax.ShapeDtypeStruct((8, vocab), f32),
            jax.ShapeDtypeStruct((8, 128), f32),
        ),
        in_specs=[anywhere] * 11,
        out_specs=(anywhere, vmem),
        scratch_shapes=[
            pltpu.SMEM((64,), jnp.int32),
            pltpu.VMEM((64, WIDTH), bf16),
            pltpu.VMEM((1, 64), jnp.int32),
            pltpu.VMEM((1, 64), jnp.int32),
            pltpu.VMEM((64, columns), bf16),
            pltpu.VMEM((columns,), bf16),
            pltpu.VMEM((8, vocab), f32),
            pltpu.VMEM((4, 2, 512, KV_RANK), bf16),
            pltpu.VMEM((64, 64, ROPE), bf16),
            pltpu.VMEM((32, 64, 2 * ROPE), bf16),
            pltpu.VMEM((4, 512, 2 * ROPE), bf16),
            pltpu.VMEM((4, 4, 4, 16, WIDTH), bf16),
            pltpu.VMEM((4, 4, 4, 16, KV_RANK + EXTRA), bf16),
            pltpu.VMEM((4, 4, 16, KV_RANK + EXTRA), bf16),
            pltpu.VMEM((4, 3, 4, 16, KV_RANK + EXTRA), bf16),
            pltpu.VMEM((4, 4, 16, KV_RANK + EXTRA), bf16),
            pltpu.VMEM((8, KV_RANK, VHEAD), bf16),
            pltpu.VMEM((1024, columns), bf16),
            pltpu.VMEM((vocab, columns), bf16),
            pltpu.VMEM((64, WIDTH), bf16),
            pltpu.VMEM((KV_RANK // 128, 64, 128), f32),
            pltpu.VMEM((8, 16, 512), bf16),
            pltpu.VMEM((16, 16, 256), f32),
            pltpu.VMEM((16, 16, 256), bf16),
            pltpu.VMEM((15, 16, 256), bf16),
            pltpu.VMEM((16, 16, 384), bf16),
            pltpu.VMEM((8, 8, 128), f32),
            pltpu.VMEM((7, 8, 128), f32),
            pltpu.VMEM((2, 4, 16, HALF), bf16),
            pltpu.VMEM((4, 16, HALF), bf16),
            pltpu.VMEM((3, 16, HALF), bf16),
            pltpu.VMEM((8, 128), f32),
            pltpu.VMEM((15, 8, 128), f32),
            dma((8,)), dma((4,)), dma((4,)), dma((4,)), dma((4,)), dma((4,)), dma((4,)), dma((4,)),
            dma((4,)), dma((4,)), dma((4,)), dma((4,)),
            dma((11,)),
            dma((1,)), dma((1,)), dma((1,)), dma((1,)), dma((1,)), dma((1,)),
            dma((1,)), dma((1,)), dma((CHUNKS,)), dma((CHUNKS,)), dma((CHUNKS,)),
            dma((CHUNKS,)), dma((1,)), dma((1,)),
        ],
        name="decode_step",
        compiler_params=pltpu.CompilerParams(
            collective_id=0, has_side_effects=True, vmem_limit_bytes=56 << 20
        ),
    )(
        lengths,
        latent_cache,
        query.reshape(-1, WIDTH),
        new_latent,
        slot_of.reshape(1, -1),
        token_ids.reshape(1, -1),
        residual,
        norm_gain,
        latent_value_weight,
        out_weight,
        lm_weight.T,
    )
    logprobs, target = pl.pallas_call(
        finish_kernel,
        out_shape=(
            jax.ShapeDtypeStruct((8, vocab), f32),
            jax.ShapeDtypeStruct((1, 8), f32),
        ),
        name="log_probabilities",
    )(logits, tail)
    return logprobs, target.reshape(8)


def solution(mesh):
    return jax.shard_map(
        body,
        mesh=mesh,
        in_specs=(
            P(None, ("dec", "pre"), None),
            P(None, "dec", None),
            P(),
            P(),
            P(),
            P(),
            P("dec", None, None),
            P("dec", "pre"),
            P(None, "pre"),
            P("pre"),
            P("pre", "dec"),
        ),
        out_specs=(P("pre", "dec"), P("pre")),
        check_vma=False,
    )
```

```python
import functools

import jax
import jax.numpy as jnp
from jax import lax
from jax.experimental import pallas as pl
from jax.experimental.pallas import tpu as pltpu
from jax.sharding import PartitionSpec as P

KV_RANK = 512
ROPE = 64
VHEAD = 128
D = 7168
WIDTH = KV_RANK + ROPE
MESH = pl.DeviceIdType.MESH
FILL = -(2.0**100)
SCALE = (VHEAD + ROPE) ** (-0.5)
EXTRA = 128
HALF = 4096
CHUNKS = 4

PAIRS = ("x", "y", "y", "z")
FIRST_PAIR = 1
LAST = 2
EARLY = ("x", "z", "x", "z")
FIRST = ("z", "x", "z", "x")


def drain(ref, sem):
    pltpu.make_async_copy(ref, ref, sem).wait()


def kernel(
    lens_in, cache, query, newl_in, slots_in, toks_in, resid_in, gain_in, vw, ow, lm,
    out, tail,
    lens, newl, slots, toks, resid, gain, raws, kbuf, raw, rope, krope, qbuf, pout, pjoin, pmid, pin, vwv, owv, lmv, qown, lat, hv, resw, rss, rsr, agb,
    sqs, sqr, ls, lr, lb, sms, smr,
    s_k, r_k, s_o, r_o, s_q, r_q, s_v, r_v, s_p, r_p, s_j, r_j, l_w, s_h, r_h, s_r, r_r, s_a, r_a, s_s, r_s,
    s_c, r_c, s_y, r_y, s_m, r_m,
):
    p, d = lax.axis_index("pre"), lax.axis_index("dec")
    y, c = lax.div(p, 2), lax.rem(p, 2)
    x, z = lax.div(d, 4), lax.rem(d, 4)
    vocab = lm.shape[0]

    def at(xx, yy, zz, cc):
        return (2 * yy + cc, 4 * xx + zz)

    def turn(value, step):
        return lax.rem(value + step, 4)

    def send(src, dst, ssem, rsem, device):
        pltpu.make_async_remote_copy(
            src_ref=src, dst_ref=dst, send_sem=ssem, recv_sem=rsem,
            device_id=device, device_id_type=MESH,
        ).start()

    pending, known = [], set()

    def later(ref, sem):
        pending.append(lambda: drain(ref, sem))

    def once(key, wait):
        if key not in known:
            known.add(key)
            pending.append(wait)

    def finish():
        for wait in pending:
            wait()

    def signal(device):
        pl.semaphore_signal(barrier, inc=1, device_id=device, device_id_type=MESH)

    hops = (0, 1, 2, 1)
    DEC = [(i, j) for i in range(4) for j in range(4) if (i, j) != (0, 0)]
    DEC.sort(key=lambda ij: -hops[ij[0]] - hops[ij[1]])
    PRE = [(i, j) for i in range(4) for j in range(2) if (i, j) != (0, 0)]
    PRE.sort(key=lambda ij: -hops[ij[0]] - ij[1])

    loads = [
        pltpu.make_async_copy(query.at[pl.ds(64 * p, 64)], qown, l_w.at[0]),
        pltpu.make_async_copy(vw, vwv, l_w.at[1]),
        pltpu.make_async_copy(ow, owv, l_w.at[2]),
        pltpu.make_async_copy(lm, lmv, l_w.at[3]),
        pltpu.make_async_copy(cache.at[:, :, pl.ds(KV_RANK, ROPE)], raw, l_w.at[4]),
    ]
    barrier = pltpu.get_barrier_semaphore()
    for i in (2, 1, 3):
        signal(at(y, turn(y, i), z, c))
        signal(at(x, turn(y, i), y, c))

    @pl.when(x != y)
    def _():
        signal(at(y, y, z, c))

    @pl.when(z != y)
    def _():
        signal(at(x, y, y, c))

    for i, j in DEC:
        signal(at(turn(x, i), y, turn(z, j), c))
    for i, j in PRE:
        signal(at(x, turn(y, i), z, lax.rem(c + j, 2)))
    for i in (2, 1, 3):
        signal(at(turn(x, i), y, z, 1 - c))
        signal(at(x, y, turn(z, i), 1 - c))
    small = [
        pltpu.make_async_copy(src, dst, l_w.at[5 + n])
        for n, (src, dst) in enumerate([
            (newl_in, newl), (slots_in, slots), (toks_in, toks), (resid_in, resid),
            (gain_in, gain), (lens_in, lens),
        ])
    ]
    loads[4].start()
    loads[0].start()
    for load in small:
        load.start()
    loads[1].start()
    loads[2].start()

    pl.semaphore_wait(
        barrier,
        15 + 7 + 6 + 6 + (x != y).astype(jnp.int32) + (z != y).astype(jnp.int32),
    )

    def group_of(axis, xx, yy, zz, cc):
        return 2 * {"x": xx, "y": yy, "z": zz}[axis] + cc

    def send_cache(k, source, target, ssem, rsem):
        axis = PAIRS[k]
        mine = group_of(axis, x, y, z, c)
        for i, j in PRE:
            xx = turn(x, i) if axis == "x" else x
            yy = turn(y, i) if axis == "y" else y
            zz = turn(z, i) if axis == "z" else z
            cc = lax.rem(c + j, 2)
            send(
                source(group_of(axis, xx, yy, zz, cc)), target(mine),
                ssem.at[k], rsem.at[k], at(xx, yy, zz, cc),
            )
        pltpu.make_async_copy(source(mine), target(mine), rsem.at[k]).start()

    def send_latents(k, core):
        axis = PAIRS[k]
        target = kbuf.at[k, :, pl.ds(64 * group_of(axis, x, y, z, c), 64), :]

        def source(xx, yy, zz, cc):
            first = 8 * group_of(axis, xx, yy, zz, cc) + 2 * k
            return cache.at[pl.ds(first, 2), :, pl.ds(0, KV_RANK)]

        for i in (2, 1, 3):
            xx = turn(x, i) if axis == "x" else x
            yy = turn(y, i) if axis == "y" else y
            zz = turn(z, i) if axis == "z" else z
            send(
                source(xx, yy, zz, core), target, s_k.at[k + 4 * core], r_k.at[k],
                at(xx, yy, zz, core),
            )
        if core == 0:
            send(source(x, y, z, 1 - c), target, s_k.at[k], r_k.at[k], at(x, y, z, 1 - c))
            pltpu.make_async_copy(source(x, y, z, c), target, r_k.at[k]).start()

    def latents_left(k, core):
        drain(kbuf.at[k, :, pl.ds(0, 192 if core else 256), :], s_k.at[k + 4 * core])

    def send_ropes(k):
        send_cache(
            k,
            lambda group: rope.at[4 * group + k],
            lambda mine: krope.at[k, pl.ds(64 * mine, 64), :],
            s_o, r_o,
        )
        later(krope.at[k, pl.ds(0, 448), :], s_o.at[k])

    def along(axis, step):
        return (turn(x, step), z) if axis == "x" else (x, turn(z, step))

    def coordinate(axis):
        return x if axis == "x" else z

    def send_query(k):
        axis = PAIRS[k]
        met = qbuf.at[k, coordinate(FIRST[k])]
        rows = query.at[pl.ds(64 * group_of(axis, x, y, z, c) + 16 * k, 16)]
        for i in (2, 1, 3):
            xx, zz = along(EARLY[k], i)
            send(
                query.at[pl.ds(64 * group_of(axis, xx, y, zz, c) + 16 * k, 16)], met.at[4 - i],
                s_q.at[k], r_q.at[k], at(xx, y, zz, c),
            )
        for i in (2, 1, 3):
            xx, zz = along(FIRST[k], i)
            send(rows, met.at[0], s_v.at[k], r_v.at[k], at(xx, y, zz, c))
        pltpu.make_async_copy(rows, met.at[0], r_q.at[k]).start()
        later(qbuf.at[k, 0, pl.ds(0, 3)], s_q.at[k])

    def pass_query(k):
        met = qbuf.at[k, coordinate(FIRST[k])]
        drain(met, r_q.at[k])
        for i in (2, 1, 3):
            xx, zz = along(FIRST[k], i)
            send(
                met.at[pl.ds(1, 3)], met.at[pl.ds(1, 3)], s_v.at[k], r_v.at[k],
                at(xx, y, zz, c),
            )
        later(qbuf.at[k, pl.ds(0, 3)], s_v.at[k])

    for k in (1, 0, 3, 2):
        send_query(k)
    for core in range(2):
        send_latents(FIRST_PAIR, core)
    def half(j):
        down = lax.broadcasted_iota(jnp.int32, (ROPE, 2 * ROPE), 0) + ROPE * j
        right = lax.broadcasted_iota(jnp.int32, (ROPE, 2 * ROPE), 1)
        return (down == right).astype(jnp.float32).astype(jnp.bfloat16)

    halves = [half(0), half(1)]
    loads[4].wait()
    for n in range(4):
        keys = raw[pl.ds(16 * n, 16)].reshape(8, 2, 64, ROPE)
        both = sum(
            jnp.dot(
                keys[:, j].reshape(512, ROPE), halves[j], preferred_element_type=jnp.float32
            )
            for j in range(2)
        )
        rope[pl.ds(8 * n, 8)] = both.astype(jnp.bfloat16).reshape(8, 64, 2 * ROPE)
    for k in (1, 0, 3, 2):
        send_ropes(k)
    loads[3].start()

    for k in (1, 0, 3, 2):
        pass_query(k)
    for k in (0, 3):
        send_latents(k, 0)

    def window(rows, n):
        left = 384 * (n % 2)
        block = rows[8 * (n // 2):8 * (n // 2) + 8]
        return jnp.concatenate([block[:, left:left + 256], block[:, left + 256:left + 512]], axis=0)

    loads[0].wait()
    for load in small:
        load.wait()
    row = lax.broadcasted_iota(jnp.int32, (64, 64), 0)
    col = lax.broadcasted_iota(jnp.int32, (64, 64), 1)
    pick = (col == 8 * p + (row >> 3)).astype(jnp.float32).astype(jnp.bfloat16)
    new_rows = jnp.dot(pick, newl[...], preferred_element_type=jnp.float32)
    own = jnp.sum(qown[...].astype(jnp.float32) * new_rows, axis=1, keepdims=True) * SCALE
    to_slot = (slots[...] == row).astype(jnp.float32).astype(jnp.bfloat16)
    resid_slot = jnp.dot(to_slot, resid[...], preferred_element_type=jnp.float32)
    for n in range(16):
        resw[n] = window(resid_slot, n)
    ls[:, :, :, pl.ds(HALF - 128, 128)] = jnp.zeros((2, 4, 16, 128), jnp.bfloat16)

    spot = lax.broadcasted_iota(jnp.int32, (1, 512), 1)
    lane = lax.broadcasted_iota(jnp.int32, (128, EXTRA), 1)
    lane16 = lax.broadcasted_iota(jnp.int32, (16, EXTRA), 1)

    def position(axis):
        slot, core, inner = spot >> 7, (spot >> 6) & 1, spot & 63
        xx = slot if axis == "x" else x
        yy = slot if axis == "y" else y
        zz = slot if axis == "z" else z
        return 64 * ((4 * xx + zz) * 8 + 2 * yy + core) + inner

    def queries_of(k):
        drain(qbuf.at[k, pl.ds(0, 3)], r_v.at[k])
        both = qbuf[k].astype(jnp.float32).reshape(16, 2, 8, WIDTH)
        queries = []
        for j in range(2):
            rows = both[:, j].reshape(128, WIDTH)
            turned = jnp.dot(
                rows[:, KV_RANK:].astype(jnp.bfloat16), halves[j],
                preferred_element_type=jnp.float32,
            )
            queries.append((rows[:, :KV_RANK].astype(jnp.bfloat16), turned.astype(jnp.bfloat16)))
        return queries

    def attend(k, queries=None):
        queries = queries or queries_of(k)
        axis = PAIRS[k]
        spots = position(axis)
        group = group_of(axis, x, y, z, c)
        drain(krope.at[k], r_o.at[k])
        drain(kbuf.at[k], r_k.at[k])
        sums, extras = [], []
        for j in range(2):
            keys = kbuf[k, j]
            scores = (
                lax.dot_general(
                    queries[j][0], keys, (((1,), (1,)), ((), ())),
                    preferred_element_type=jnp.float32,
                )
                + lax.dot_general(
                    queries[j][1], krope[k], (((1,), (1,)), ((), ())),
                    preferred_element_type=jnp.float32,
                )
            ) * SCALE
            scores = jnp.where(spots < lens[8 * group + 2 * k + j], scores, FILL)
            top = jnp.max(scores, axis=1, keepdims=True)
            top = top.astype(jnp.bfloat16).astype(jnp.float32)
            weights = jnp.exp(scores - top)
            total = jnp.sum(weights, axis=1, keepdims=True)
            sums.append(
                jnp.dot(
                    weights.astype(jnp.bfloat16), keys,
                    preferred_element_type=jnp.float32,
                ).reshape(16, 8, KV_RANK)
            )
            high = total.astype(jnp.bfloat16).astype(jnp.float32)
            extra = jnp.where(lane == 0, top, jnp.where(lane == 1, high, total - high))
            extras.append(extra.reshape(16, 8, EXTRA))
        sums = jnp.concatenate(sums, axis=1).astype(jnp.bfloat16).reshape(4, 4, 16, KV_RANK)
        extras = jnp.concatenate(extras, axis=1).astype(jnp.bfloat16).reshape(4, 4, 16, EXTRA)
        for n in range(4):
            pout[k, n, :, :, pl.ds(0, KV_RANK)] = sums[n]
            pout[k, n, :, :, pl.ds(KV_RANK, EXTRA)] = extras[n]
        for i in (2, 1, 3):
            xx, zz = along(FIRST[k], i)
            send(
                pout.at[k, xx if FIRST[k] == "x" else zz], pmid.at[k, i - 1],
                s_p.at[k], r_p.at[k], at(xx, y, zz, c),
            )
        once((0, k), lambda: drain(pmid.at[k], s_p.at[k]))

    def joined(blocks, own=None):
        extra = [block[..., KV_RANK:].astype(jnp.float32) for block in blocks]
        tops = [part[..., 0:1] for part in extra]
        top = functools.reduce(jnp.maximum, tops)
        if own is not None:
            top = jnp.maximum(top, own)
        shrink = [jnp.exp(part - top) for part in tops]
        total = sum((part[..., 1:2] + part[..., 2:3]) * by for part, by in zip(extra, shrink))
        summed = sum(
            block[..., :KV_RANK].astype(jnp.float32) * by for block, by in zip(blocks, shrink)
        )
        return top, total, summed

    def join_first(k):
        axis, first = PAIRS[k], FIRST[k]
        drain(pmid.at[k], r_p.at[k])
        for n in range(4):
            blocks = [pout[k, coordinate(first), n]] + [pmid[k, i, n] for i in range(3)]
            top, total, summed = joined(blocks)
            high = total.astype(jnp.bfloat16).astype(jnp.float32)
            extra = jnp.where(lane16 == 0, top, jnp.where(lane16 == 1, high, total - high))
            pjoin[k, n, :, pl.ds(0, KV_RANK)] = summed.astype(jnp.bfloat16)
            pjoin[k, n, :, pl.ds(KV_RANK, EXTRA)] = extra.astype(jnp.bfloat16)
        yy = {"x": x, "y": y, "z": z}[axis]
        place = y if axis != "y" else (z if first == "x" else x)
        here = z if first == "x" else x
        for i in (2, 1, 3):
            other = turn(here, i)
            xx, zz = (x, other) if first == "x" else (other, z)
            send(
                pjoin.at[k, i], pin.at[k, place],
                s_j.at[k], r_j.at[k], at(xx, yy, zz, c),
            )
        once((1, k), lambda: drain(pin.at[k, pl.ds(0, 3)], s_j.at[k]))

        def keep():
            pltpu.make_async_copy(pjoin.at[k, 0], pin.at[k, place], r_j.at[k]).start()

        if axis == "y":
            keep()
        else:
            pl.when(yy == y)(keep)

            @pl.when(yy != y)
            def _():
                send(
                    pjoin.at[k, 0], pin.at[k, place],
                    s_j.at[k], r_j.at[k], at(x, yy, z, c),
                )

            def left():
                pl.when(yy != y)(lambda: drain(pin.at[k, 0], s_j.at[k]))

            once((2, k), left)

    def join_last(k):
        drain(pin.at[k], r_j.at[k])
        blocks = [pin[k, n] for n in range(4)]
        own_k = own[16 * k:16 * k + 16]
        top, total, summed = joined(blocks, own_k)
        own_weight = jnp.exp(own_k - top)
        summed = summed + (
            own_weight.astype(jnp.bfloat16).astype(jnp.float32)
            * new_rows[16 * k:16 * k + 16, :KV_RANK]
        )
        summed = summed / (total + own_weight)
        for b in range(KV_RANK // 128):
            lat[b, pl.ds(16 * k, 16), :] = summed[:, 128 * b:128 * b + 128]

    queries = queries_of(FIRST_PAIR)
    send_latents(LAST, 0)
    for core in range(2):
        latents_left(FIRST_PAIR, core)
    send_latents(LAST, 1)
    attend(FIRST_PAIR, queries)
    for k in (0, 3):
        latents_left(k, 0)
        send_latents(k, 1)

    @pl.when(c == 0)
    def _():
        attend(0)
        attend(3)
        join_first(1)
        attend(2)

    @pl.when(c == 1)
    def _():
        join_first(1)
        attend(0)
        attend(3)
        attend(2)

    for k in (0, 3, 2):
        join_first(k)
    latents_left(LAST, 0)
    for k in (0, 3, 2):
        latents_left(k, 1)
    for k in (1, 0, 3, 2):
        join_last(k)

    loads[1].wait()
    values = []
    for f in range(8):
        rows = jnp.concatenate(
            [lat[b, pl.ds(f, 8, stride=8), :] for b in range(KV_RANK // 128)], axis=1
        ).astype(jnp.bfloat16)
        values.append(jnp.dot(rows, vwv[f], preferred_element_type=jnp.float32))
    packed = jnp.concatenate(
        [jnp.concatenate(values[:4], axis=1), jnp.concatenate(values[4:], axis=1)], axis=0
    )
    hv[p] = packed.astype(jnp.bfloat16)
    for i, j in PRE:
        send(hv.at[p], hv.at[p], s_h.at[0], r_h.at[0], at(x, turn(y, i), z, lax.rem(c + j, 2)))
    later(hv.at[pl.ds(0, 7)], s_h.at[0])
    loads[2].wait()
    drain(hv.at[pl.ds(0, 7)], r_h.at[0])

    heads = hv[...].astype(jnp.float32).reshape(8, 2, 8, KV_RANK)
    part = jnp.zeros((64, owv.shape[1]), jnp.float32)
    for half in range(2):
        rows = heads[:, half].reshape(64, KV_RANK).astype(jnp.bfloat16)
        rows = jnp.dot(to_slot, rows, preferred_element_type=jnp.float32).astype(jnp.bfloat16)
        part = part + jnp.dot(
            rows, owv[pl.ds(KV_RANK * half, KV_RANK), :], preferred_element_type=jnp.float32
        )
    for s in range(16):
        rss[s] = window(part, s).astype(jnp.bfloat16)
    for n, (i, j) in enumerate(DEC):
        xx, zz = turn(x, i), turn(z, j)
        send(rss.at[4 * xx + zz], rsr.at[n], s_r.at[0], r_r.at[0], at(xx, y, zz, c))
    later(rsr, s_r.at[0])
    drain(rsr, r_r.at[0])
    hidden = resw[d] + rss[d].astype(jnp.float32)
    for n in range(15):
        hidden = hidden + rsr[n].astype(jnp.float32)
    odd = lax.rem(d, 2) == 1
    gains = jnp.broadcast_to(gain[...].astype(jnp.float32).reshape(1, -1), (8, owv.shape[1]))
    scaled = hidden * jnp.where(odd, window(gains, 1), window(gains, 0))
    twice = (
        (lax.broadcasted_iota(jnp.int32, (16, 256), 0) < 8)
        & (lax.broadcasted_iota(jnp.int32, (16, 256), 1) < 128)
        & odd
    )
    squares = jnp.sum(jnp.where(twice, 0.0, hidden * hidden), axis=1, keepdims=True)
    squares = squares + jnp.concatenate([squares[8:], squares[:8]], axis=0)
    first = squares.astype(jnp.bfloat16).astype(jnp.float32)
    second = (squares - first).astype(jnp.bfloat16).astype(jnp.float32)
    third = squares - first - second
    agb[d, :, pl.ds(0, 256)] = scaled.astype(jnp.bfloat16)
    agb[d, :, pl.ds(256, 128)] = jnp.where(
        lane16 == 0, first, jnp.where(lane16 == 1, second, third)
    ).astype(jnp.bfloat16)
    for i, j in DEC:
        send(agb.at[d], agb.at[d], s_a.at[0], r_a.at[0], at(turn(x, i), y, turn(z, j), c))
    later(agb.at[pl.ds(0, 15)], s_a.at[0])
    drain(agb.at[pl.ds(0, 15)], r_a.at[0])
    gathered = agb[...].astype(jnp.float32).reshape(8, 2, 2, 8, 384)
    squares = sum(
        gathered[:, h, 0, :, 256 + n:257 + n] for h in range(2) for n in range(3)
    )
    sqs[...] = jnp.broadcast_to(squares, (8, 8, 128))
    scaled = jnp.concatenate(
        [
            gathered[:, 0, 0, :, 0:256].reshape(64, 256),
            gathered[:, 0, 1, :, 0:256].reshape(64, 256),
            gathered[:, 1, 0, :, 128:256].reshape(64, 128),
            gathered[:, 1, 1, :, 0:256].reshape(64, 256),
        ],
        axis=1,
    ).astype(jnp.bfloat16)

    wide = HALF // CHUNKS

    def join_cores(i):
        lanes = pl.ds(wide * i, wide)
        drain(lr.at[:, :, lanes], r_c.at[i])
        ls[c, :, :, lanes] = (
            ls[c, :, :, lanes].astype(jnp.float32) + lr[:, :, lanes].astype(jnp.float32)
        ).astype(jnp.bfloat16)
        for step in (2, 1, 3):
            yy = turn(y, step)
            send(
                ls.at[c, yy, :, lanes], lb.at[step - 1, :, lanes],
                s_y.at[i], r_y.at[i], at(x, yy, z, c),
            )
        later(lb.at[:, :, lanes], s_y.at[i])

    loads[3].wait()
    for i in range(CHUNKS):
        for half in range(2):
            start = HALF * half + wide * i
            count = min(wide, vocab - start)
            product = lax.dot_general(
                scaled, lmv[pl.ds(start, count), :], (((1,), (1,)), ((), ())),
                preferred_element_type=jnp.float32,
            ).reshape(8, 8, count).astype(jnp.bfloat16)
            for q in range(8):
                ls[q % 2, q // 2, pl.ds(8 * half, 8), pl.ds(wide * i, count)] = product[q]
        lanes = pl.ds(wide * i, wide)
        send(
            ls.at[1 - c, :, :, lanes], lr.at[:, :, lanes],
            s_c.at[i], r_c.at[i], at(x, y, z, 1 - c),
        )
        later(lr.at[:, :, lanes], s_c.at[i])
        if i == 0:
            for n, (up, over) in enumerate(PRE):
                yy, cc = turn(y, up), lax.rem(c + over, 2)
                send(sqs.at[2 * yy + cc], sqr.at[n], s_s.at[0], r_s.at[0], at(x, yy, z, cc))
            later(sqr, s_s.at[0])
        else:
            join_cores(i - 1)
    join_cores(CHUNKS - 1)

    drain(sqr, r_s.at[0])
    norm = sqs[p]
    for n in range(7):
        norm = norm + sqr[n]
    norm = lax.rsqrt(norm[:, 0:1] / D + 1e-06)
    for i in range(CHUNKS):
        drain(lb.at[:, :, pl.ds(wide * i, wide)], r_y.at[i])
    logits = ls[c, y].astype(jnp.float32)
    for n in range(3):
        logits = logits + lb[n].astype(jnp.float32)
    low, high = logits[:8] * norm, logits[8:] * norm

    column = lax.broadcasted_iota(jnp.int32, (8, HALF), 1)
    high = jnp.where(column < vocab - HALF, high, FILL)
    slot_rows = lax.broadcasted_iota(jnp.int32, (8, 64), 0) + 8 * p
    token = jnp.sum(jnp.where(slots[...] == slot_rows, toks[...], 0), axis=1, keepdims=True)
    token = token - d * vocab
    picked = jnp.sum(jnp.where(column == token, low, 0.0), axis=1, keepdims=True) + jnp.sum(
        jnp.where((column + HALF == token) & (column < vocab - HALF), high, 0.0),
        axis=1, keepdims=True,
    )
    top = jnp.maximum(
        jnp.max(low, axis=1, keepdims=True), jnp.max(high, axis=1, keepdims=True)
    )
    total = jnp.sum(jnp.exp(low - top), axis=1, keepdims=True) + jnp.sum(
        jnp.exp(high - top), axis=1, keepdims=True
    )
    lane8 = lax.broadcasted_iota(jnp.int32, (8, 128), 1)
    mine = jnp.where(lane8 == 0, top, jnp.where(lane8 == 1, total, picked))
    sms[...] = mine
    for n, (i, j) in enumerate(DEC):
        send(sms, smr.at[n], s_m.at[0], r_m.at[0], at(turn(x, i), y, turn(z, j), c))
    raws[:, pl.ds(0, HALF)] = low
    raws[:, pl.ds(HALF, vocab - HALF)] = high[:, : vocab - HALF]
    write = pltpu.make_async_copy(raws, out, l_w.at[0])
    write.start()
    finish()
    drain(smr, r_m.at[0])
    others = smr[...]
    best = jnp.maximum(jnp.max(others[:, :, 0:1], axis=0), top)
    total = total * jnp.exp(top - best) + jnp.sum(
        others[:, :, 1:2] * jnp.exp(others[:, :, 0:1] - best[None]), axis=0
    )
    picked = picked + jnp.sum(others[:, :, 2:3], axis=0)
    normalizer = best + jnp.log(total)
    tail[...] = jnp.where(lane8 == 0, normalizer, picked - normalizer)
    write.wait()
    drain(smr, s_m.at[0])


def finish_kernel(logits, tail, out, tgt):
    out[...] = logits[...] - tail[:, 0:1]
    square = lax.broadcasted_iota(jnp.int32, (8, 8), 0) == lax.broadcasted_iota(
        jnp.int32, (8, 8), 1
    )
    tgt[...] = jnp.sum(jnp.where(square, tail[:, 1:2], 0.0), axis=0, keepdims=True)


def body(
    latent_cache, query, new_latent, lengths, slot_of, token_ids,
    latent_value_weight, out_weight, residual, norm_gain, lm_weight,
):
    columns, vocab = lm_weight.shape
    bf16, f32 = jnp.bfloat16, jnp.float32
    vmem = pl.BlockSpec(memory_space=pltpu.VMEM)
    anywhere = pl.BlockSpec(memory_space=pl.ANY)
    dma = pltpu.SemaphoreType.DMA
    logits, tail = pl.pallas_call(
        kernel,
        out_shape=(
            jax.ShapeDtypeStruct((8, vocab), f32),
            jax.ShapeDtypeStruct((8, 128), f32),
        ),
        in_specs=[anywhere] * 11,
        out_specs=(anywhere, vmem),
        scratch_shapes=[
            pltpu.SMEM((64,), jnp.int32),
            pltpu.VMEM((64, WIDTH), bf16),
            pltpu.VMEM((1, 64), jnp.int32),
            pltpu.VMEM((1, 64), jnp.int32),
            pltpu.VMEM((64, columns), bf16),
            pltpu.VMEM((columns,), bf16),
            pltpu.VMEM((8, vocab), f32),
            pltpu.VMEM((4, 2, 512, KV_RANK), bf16),
            pltpu.VMEM((64, 64, ROPE), bf16),
            pltpu.VMEM((32, 64, 2 * ROPE), bf16),
            pltpu.VMEM((4, 512, 2 * ROPE), bf16),
            pltpu.VMEM((4, 4, 4, 16, WIDTH), bf16),
            pltpu.VMEM((4, 4, 4, 16, KV_RANK + EXTRA), bf16),
            pltpu.VMEM((4, 4, 16, KV_RANK + EXTRA), bf16),
            pltpu.VMEM((4, 3, 4, 16, KV_RANK + EXTRA), bf16),
            pltpu.VMEM((4, 4, 16, KV_RANK + EXTRA), bf16),
            pltpu.VMEM((8, KV_RANK, VHEAD), bf16),
            pltpu.VMEM((1024, columns), bf16),
            pltpu.VMEM((vocab, columns), bf16),
            pltpu.VMEM((64, WIDTH), bf16),
            pltpu.VMEM((KV_RANK // 128, 64, 128), f32),
            pltpu.VMEM((8, 16, 512), bf16),
            pltpu.VMEM((16, 16, 256), f32),
            pltpu.VMEM((16, 16, 256), bf16),
            pltpu.VMEM((15, 16, 256), bf16),
            pltpu.VMEM((16, 16, 384), bf16),
            pltpu.VMEM((8, 8, 128), f32),
            pltpu.VMEM((7, 8, 128), f32),
            pltpu.VMEM((2, 4, 16, HALF), bf16),
            pltpu.VMEM((4, 16, HALF), bf16),
            pltpu.VMEM((3, 16, HALF), bf16),
            pltpu.VMEM((8, 128), f32),
            pltpu.VMEM((15, 8, 128), f32),
            dma((8,)), dma((4,)), dma((4,)), dma((4,)), dma((4,)), dma((4,)), dma((4,)), dma((4,)),
            dma((4,)), dma((4,)), dma((4,)), dma((4,)),
            dma((11,)),
            dma((1,)), dma((1,)), dma((1,)), dma((1,)), dma((1,)), dma((1,)),
            dma((1,)), dma((1,)), dma((CHUNKS,)), dma((CHUNKS,)), dma((CHUNKS,)),
            dma((CHUNKS,)), dma((1,)), dma((1,)),
        ],
        name="decode_step",
        compiler_params=pltpu.CompilerParams(
            collective_id=0, has_side_effects=True, vmem_limit_bytes=56 << 20
        ),
    )(
        lengths,
        latent_cache,
        query.reshape(-1, WIDTH),
        new_latent,
        slot_of.reshape(1, -1),
        token_ids.reshape(1, -1),
        residual,
        norm_gain,
        latent_value_weight,
        out_weight,
        lm_weight.T,
    )
    logprobs, target = pl.pallas_call(
        finish_kernel,
        out_shape=(
            jax.ShapeDtypeStruct((8, vocab), f32),
            jax.ShapeDtypeStruct((1, 8), f32),
        ),
        name="log_probabilities",
    )(logits, tail)
    return logprobs, target.reshape(8)


def solution(mesh):
    return jax.shard_map(
        body,
        mesh=mesh,
        in_specs=(
            P(None, ("dec", "pre"), None),
            P(None, "dec", None),
            P(),
            P(),
            P(),
            P(),
            P("dec", None, None),
            P("dec", "pre"),
            P(None, "pre"),
            P("pre"),
            P("pre", "dec"),
        ),
        out_specs=(P("pre", "dec"), P("pre")),
        check_vma=False,
    )
```
